32 devices in a mesh: tp: 4 (over y, x), ep: 8 (over z, core).
Axes of the slice: x: 2, y: 2, z: 4, core: 2. Of those that a mesh axis runs over, the one named last changes fastest.
Arguments:
- tokens: bfloat16 [25088, 768], P('ep'), may hold values from -6 to 6
- cotangent: bfloat16 [25088, 768], P('ep'), may hold values from -6 to 6
- picks: int32 [25088, 2], P('ep'), may hold values from 0 to 7, all different within a row
- priority: int32 [8, 3136], P('ep'), may hold values from 0 to 3135, each once within a row
- router_noise: float32 [25088, 8], P('ep'), may hold values from -3 to 3
- dense_norm_gain: float32 [768], replicated, may hold values from 0.5 to 1.5
- dense_norm_bias: float32 [768], replicated, may hold values from -1.25 to 1.25
- dense_attend_in: bfloat16 [768, 3, 768], P(None, None, 'tp'), may hold values from -0.21875 to 0.21875
- dense_attend_bias: float32 [2, 768], P(None, 'tp'), may hold values from -1.25 to 1.25
- dense_attend_out: bfloat16 [768, 768], P('tp'), may hold values from -1.75 to 1.75
- dense_attend_out_bias: float32 [768], replicated, may hold values from -1.25 to 1.25
- feed_norm_gain: float32 [768], replicated, may hold values from 0.5 to 1.5
- feed_norm_bias: float32 [768], replicated, may hold values from -1.25 to 1.25
- feed_in: bfloat16 [768, 3072], P(None, 'tp'), may hold values from -0.21875 to 0.21875
- feed_in_bias: float32 [3072], P('tp'), may hold values from -1.25 to 1.25
- feed_out: bfloat16 [3072, 768], P('tp'), may hold values from -0.109375 to 0.109375
- feed_out_bias: float32 [768], replicated, may hold values from -1.25 to 1.25
- sparse_norm_gain: float32 [768], replicated, may hold values from 0.5 to 1.5
- sparse_norm_bias: float32 [768], replicated, may hold values from -1.25 to 1.25
- sparse_attend_in: bfloat16 [768, 3, 768], P(None, None, 'tp'), may hold values from -0.21875 to 0.21875
- sparse_attend_bias: float32 [2, 768], P(None, 'tp'), may hold values from -1.25 to 1.25
- sparse_attend_out: bfloat16 [768, 768], P('tp'), may hold values from -1.75 to 1.75
- sparse_attend_out_bias: float32 [768], replicated, may hold values from -1.25 to 1.25
- route_norm_gain: float32 [768], replicated, may hold values from 0.5 to 1.5
- route_norm_bias: float32 [768], replicated, may hold values from -1.25 to 1.25
- router: bfloat16 [768, 8], replicated, may hold values from -0.109375 to 0.109375
- expert_in: bfloat16 [8, 768, 3072], P('ep', None, 'tp'), may hold values from -0.21875 to 0.21875
- expert_in_bias: float32 [8, 3072], P('ep', 'tp'), may hold values from -0.625 to 0.625
- expert_out: bfloat16 [8, 3072, 768], P('ep', 'tp'), may hold values from -0.4375 to 0.4375
- expert_out_bias: float32 [8, 768], P('ep'), may hold values from -3 to 3
Outputs:
- activations: bfloat16 [25088, 768], P('ep')
- input_grad: float32 [25088, 768], P('ep')
- grad_dense_norm_gain: float32 [768], replicated
- grad_dense_norm_bias: float32 [768], replicated
- grad_dense_attend_in: float32 [768, 3, 768], P(None, None, 'tp')
- grad_dense_attend_bias: float32 [2, 768], P(None, 'tp')
- grad_dense_attend_out: float32 [768, 768], P('tp')
- grad_dense_attend_out_bias: float32 [768], replicated
- grad_feed_norm_gain: float32 [768], replicated
- grad_feed_norm_bias: float32 [768], replicated
- grad_feed_in: float32 [768, 3072], P(None, 'tp')
- grad_feed_in_bias: float32 [3072], P('tp')
- grad_feed_out: float32 [3072, 768], P('tp')
- grad_feed_out_bias: float32 [768], replicated
- grad_sparse_norm_gain: float32 [768], replicated
- grad_sparse_norm_bias: float32 [768], replicated
- grad_sparse_attend_in: float32 [768, 3, 768], P(None, None, 'tp')
- grad_sparse_attend_bias: float32 [2, 768], P(None, 'tp')
- grad_sparse_attend_out: float32 [768, 768], P('tp')
- grad_sparse_attend_out_bias: float32 [768], replicated
- grad_route_norm_gain: float32 [768], replicated
- grad_route_norm_bias: float32 [768], replicated
- grad_router: float32 [768, 8], replicated
- grad_expert_in: float32 [8, 768, 3072], P('ep', None, 'tp')
- grad_expert_in_bias: float32 [8, 3072], P('ep', 'tp')
- grad_expert_out: float32 [8, 3072, 768], P('ep', 'tp')
- grad_expert_out_bias: float32 [8, 768], P('ep')
The draws below stay inside these ranges and needn't reach their ends.
Inputs may be any that keep to these rules, and one draw needn't show every extreme that they name: `picks`: each row names two different experts; every expert is named by some row. `priority`: each row holds every number of 0 to 3135 once.
All inputs are finite; a program needn't handle non-finite values.
Results may differ from the reference program's by a relative error of at most 0.02.
Values may be sent and summed in bfloat16 or wider, within the bound.
A program may use at most 384 MiB of HBM per device.

```python
import jax
import jax.numpy as jnp
from jax import lax

D = 768
HEADS = 12
HEAD = 64
FF = 3072
LEN = 196
IMG_DEV = 16
TOK_DEV = 3136
EXPERTS = 8
TOKENS = 25088
N_EP = 8


def shard_levels(stream_key, shape, cuts, smallest, top_value):
    loudness = 1.0
    for dim, shards_of in cuts:
        heights = jax.random.uniform(jax.random.fold_in(jax.random.fold_in(stream_key, 6), dim), (shards_of,), jnp.float32, smallest / len(cuts), top_value / len(cuts))
        loudness = loudness * jnp.repeat(jnp.exp(heights), shape[dim] // shards_of).reshape((-1,) + (1,) * (len(shape) - 1 - dim))
    return loudness


def choose_distinct(stream_key, rows, count, top, lift):
    order = jax.random.permutation(jax.random.fold_in(stream_key, 1), count)
    pull = order
    for power in range(3):
        pull = pull * pull // count
    pull = pull * lift // count
    tickets = jax.random.randint(jax.random.fold_in(stream_key, 2), (rows, count), 0, 4096) + pull
    holders = jax.random.permutation(jax.random.fold_in(stream_key, 3), rows)[jnp.arange(count) % rows]
    tickets = jnp.where(jnp.arange(rows)[:, None] == holders[None, :], 1 << 14, tickets)
    merit = tickets * count + jnp.arange(count)
    return lax.top_k(merit.astype(jnp.int32), top)[1].astype(jnp.int32)


def gaussian(stream_key, extent, width, most, split=(), kind=jnp.bfloat16):
    drawn = width * jax.random.normal(stream_key, extent, jnp.float32)
    if split:
        drawn = drawn * shard_levels(stream_key, extent, split, -0.22, 0.18)
    return jnp.clip(drawn, -most, most).astype(kind)


def setup_inputs(seed: int = 0) -> dict:
    arg_keys = jax.random.split(jax.random.key(seed), 31)
    tokens = gaussian(arg_keys[0], (TOKENS, D), 1.0, 6.0, ((0, 8),))
    cotangent = gaussian(arg_keys[1], (TOKENS, D), 1.0, 6.0, ((0, 8),))
    picks = choose_distinct(arg_keys[2], TOKENS, EXPERTS, 2, 2048)
    priority = jax.vmap(lambda own: jax.random.permutation(own, TOK_DEV))(jax.random.split(arg_keys[3], (TOKENS // TOK_DEV))).reshape((TOKENS // TOK_DEV, TOK_DEV)).astype(jnp.int32)
    router_noise = gaussian(arg_keys[4], (TOKENS, EXPERTS), 0.5, 3.0, ((0, 8),), jnp.float32)
    dense_norm_gain = jnp.clip(1.0 + 0.1 * jax.random.normal(arg_keys[5], (D,), jnp.float32), 0.5, 1.5)
    dense_norm_bias = gaussian(arg_keys[6], (D,), 0.2, 1.25, (), jnp.float32)
    dense_attend_in = gaussian(arg_keys[7], (D, 3, D), D ** -0.5, 0.21875, ((2, 4),))
    dense_attend_bias = gaussian(arg_keys[8], (2, D), 0.2, 1.25, ((1, 4),), jnp.float32)
    dense_attend_out = gaussian(arg_keys[9], (D, D), (max(1, D // 64)) ** -0.5, 1.75, ((0, 4),))
    dense_attend_out_bias = gaussian(arg_keys[10], (D,), 0.2, 1.25, (), jnp.float32)
    feed_norm_gain = jnp.clip(1.0 + 0.1 * jax.random.normal(arg_keys[11], (D,), jnp.float32), 0.5, 1.5)
    feed_norm_bias = gaussian(arg_keys[12], (D,), 0.2, 1.25, (), jnp.float32)
    feed_in = gaussian(arg_keys[13], (D, FF), D ** -0.5, 0.21875, ((1, 4),))
    feed_in_bias = gaussian(arg_keys[14], (FF,), 0.2, 1.25, ((0, 4),), jnp.float32)
    feed_out = gaussian(arg_keys[15], (FF, D), FF ** -0.5, 0.109375, ((0, 4),))
    feed_out_bias = gaussian(arg_keys[16], (D,), 0.2, 1.25, (), jnp.float32)
    sparse_norm_gain = jnp.clip(1.0 + 0.1 * jax.random.normal(arg_keys[17], (D,), jnp.float32), 0.5, 1.5)
    sparse_norm_bias = gaussian(arg_keys[18], (D,), 0.2, 1.25, (), jnp.float32)
    sparse_attend_in = gaussian(arg_keys[19], (D, 3, D), D ** -0.5, 0.21875, ((2, 4),))
    sparse_attend_bias = gaussian(arg_keys[20], (2, D), 0.2, 1.25, ((1, 4),), jnp.float32)
    sparse_attend_out = gaussian(arg_keys[21], (D, D), (max(1, D // 64)) ** -0.5, 1.75, ((0, 4),))
    sparse_attend_out_bias = gaussian(arg_keys[22], (D,), 0.2, 1.25, (), jnp.float32)
    route_norm_gain = jnp.clip(1.0 + 0.1 * jax.random.normal(arg_keys[23], (D,), jnp.float32), 0.5, 1.5)
    route_norm_bias = gaussian(arg_keys[24], (D,), 0.2, 1.25, (), jnp.float32)
    router = gaussian(arg_keys[25], (D, EXPERTS), (4 * D) ** -0.5, 0.109375)
    expert_in = gaussian(arg_keys[26], (EXPERTS, D, FF), D ** -0.5, 0.21875, ((0, 8), (2, 4)))
    expert_in_bias = gaussian(arg_keys[27], (EXPERTS, FF), 0.1, 0.625, ((0, 8), (1, 4)), jnp.float32)
    expert_out = gaussian(arg_keys[28], (EXPERTS, FF, D), (max(1, 4 * FF // (EXPERTS * EXPERTS))) ** -0.5, 0.4375, ((0, 8), (1, 4)))
    expert_out_bias = gaussian(arg_keys[29], (EXPERTS, D), 0.5, 3.0, ((0, 8),), jnp.float32)
    return dict(tokens=tokens, cotangent=cotangent, picks=picks, priority=priority, router_noise=router_noise, dense_norm_gain=dense_norm_gain, dense_norm_bias=dense_norm_bias, dense_attend_in=dense_attend_in, dense_attend_bias=dense_attend_bias, dense_attend_out=dense_attend_out, dense_attend_out_bias=dense_attend_out_bias, feed_norm_gain=feed_norm_gain, feed_norm_bias=feed_norm_bias, feed_in=feed_in, feed_in_bias=feed_in_bias, feed_out=feed_out, feed_out_bias=feed_out_bias, sparse_norm_gain=sparse_norm_gain, sparse_norm_bias=sparse_norm_bias, sparse_attend_in=sparse_attend_in, sparse_attend_bias=sparse_attend_bias, sparse_attend_out=sparse_attend_out, sparse_attend_out_bias=sparse_attend_out_bias, route_norm_gain=route_norm_gain, route_norm_bias=route_norm_bias, router=router, expert_in=expert_in, expert_in_bias=expert_in_bias, expert_out=expert_out, expert_out_bias=expert_out_bias)


EPSILON = 1e-06
HIGH = lax.Precision.HIGHEST

@jax.custom_vjp
def low(v):
    return lax.optimization_barrier(v.astype(jnp.bfloat16)).astype(jnp.float32)

@jax.custom_vjp
def low_back(v):
    return v

def low_keep(v):
    return (low(v), None)

def low_pass(kept, grad):
    return (grad,)

def back_keep(v):
    return (v, None)

def back_low(kept, grad):
    return (low(grad),)
low.defvjp(low_keep, low_pass)
low_back.defvjp(back_keep, back_low)

def layer_norm(residual, norm_gain, norm_bias):
    average = lax.optimization_barrier(jnp.mean(residual, axis=-1, keepdims=True))
    centred = residual - average
    variance = lax.optimization_barrier(jnp.mean(centred * centred, axis=-1, keepdims=True))
    return centred * lax.rsqrt(variance + EPSILON) * norm_gain + norm_bias

def gelu_exact(value_in):
    return jax.nn.gelu(value_in, approximate=False)

def by_image(tensor):
    return tensor.reshape(N_EP, IMG_DEV, LEN, HEADS, HEAD)

def attend_group(bundle):
    queries, keys_in, values = bundle
    scores = low_back(jnp.einsum('bqhc,bkhc->bhqk', queries, keys_in, precision=HIGH) * HEAD ** (-0.5))
    weights = low(jax.nn.softmax(scores, axis=-1))
    return jnp.einsum('bhqk,bkhc->bqhc', weights, values, precision=HIGH)

def attention(residual, norm_gain, norm_bias, proj_in, proj_bias, proj_out, out_bias):
    normed = low(layer_norm(residual, norm_gain, norm_bias))
    projected = jnp.einsum('td,dkc->tkc', normed, proj_in, precision=HIGH)
    queries = low_back(low(projected[:, 0] + proj_bias[0]))
    keys_in = low_back(low(projected[:, 1]))
    values = low_back(low(projected[:, 2] + proj_bias[1]))
    context = lax.map(jax.checkpoint(attend_group), (by_image(queries), by_image(keys_in), by_image(values)))
    context = low_back(low(context.reshape(TOKENS, D)))
    return low_back(jnp.dot(context, proj_out, precision=HIGH) + out_bias)

def feed_forward(residual, norm_gain, norm_bias, weight_in, bias_in, weight_out, bias_out):
    normed = low(layer_norm(residual, norm_gain, norm_bias))
    hidden_pre = low_back(jnp.dot(normed, weight_in, precision=HIGH) + bias_in)
    hidden = low(gelu_exact(hidden_pre))
    return low_back(jnp.dot(hidden, weight_out, precision=HIGH) + bias_out)

def route(device_picks, device_order, capacity, experts):
    rows_dev = device_picks.shape[0]
    ranked = device_picks[device_order]
    sequence = jnp.concatenate([ranked[:, 0], ranked[:, 1]])
    onehot = (sequence[:, None] == jnp.arange(experts, dtype=jnp.int32)[None, :]).astype(jnp.int32)
    earlier = (jnp.cumsum(onehot, axis=0) - onehot).astype(jnp.int32)
    position = lax.optimization_barrier(jnp.sum(earlier * onehot, axis=1)).astype(jnp.int32)
    slot_index = jnp.zeros((rows_dev, 2), jnp.int32).at[device_order].set(position.reshape(2, rows_dev).T)
    kept_mask = slot_index < capacity
    target = jnp.where(kept_mask, device_picks * capacity + slot_index, experts * capacity).astype(jnp.int32)
    pair_ids = jnp.arange(2, dtype=jnp.int32)[None, :] * rows_dev + jnp.arange(rows_dev, dtype=jnp.int32)[:, None]
    slot_table = jnp.full((experts * capacity + 1,), 2 * rows_dev, jnp.int32)
    slot_table = slot_table.at[target.reshape(-1)].set(pair_ids.reshape(-1))
    return (kept_mask, target, slot_table[:experts * capacity])

def pick_rows(rows_in, chosen_rows):
    return rows_in[chosen_rows]

def mixture(residual, norm_gain, norm_bias, router, expert_in, expert_in_bias, expert_out, expert_out_bias, router_noise, picks, priority):
    experts = N_EP
    capacity = TOK_DEV // N_EP
    normed = low(layer_norm(residual, norm_gain, norm_bias))
    logits = low_back(jnp.dot(normed, router, precision=HIGH) + router_noise)
    gate_probs = jax.nn.softmax(logits, axis=-1)
    device_picks = picks.reshape(N_EP, TOK_DEV, 2)
    kept_mask, target, slot_table = jax.vmap(lambda chosen, ordering: route(chosen, ordering, capacity, experts))(device_picks, priority)
    filled = slot_table < 2 * TOK_DEV
    token_of = slot_table % TOK_DEV
    gathered = jax.vmap(pick_rows)(normed.reshape(N_EP, TOK_DEV, D), token_of)
    dispatched = jnp.where(filled[:, :, None], gathered, 0.0)
    dispatched = dispatched.reshape(N_EP, experts, capacity, D).transpose(1, 0, 2, 3).reshape(experts, N_EP * capacity, D)
    dispatched = low_back(dispatched)
    hidden_pre = low_back(jnp.einsum('esd,edf->esf', dispatched, expert_in, precision=HIGH) + expert_in_bias[:, None, :])
    hidden = low(gelu_exact(hidden_pre))
    returned = low_back(low(jnp.einsum('esf,efd->esd', hidden, expert_out, precision=HIGH) + expert_out_bias[:, None, :]))
    returned = returned.reshape(experts, N_EP, capacity, D).transpose(1, 0, 2, 3).reshape(N_EP, experts * capacity, D)
    picked_gate = jnp.take_along_axis(gate_probs, picks, axis=1).reshape(N_EP, TOK_DEV, 2)
    pair_weight = jnp.where(kept_mask, picked_gate, 0.0)
    row_index = jnp.minimum(target, experts * capacity - 1)
    first_rows = jax.vmap(pick_rows)(returned, row_index[:, :, 0])
    second_rows = jax.vmap(pick_rows)(returned, row_index[:, :, 1])
    combined = pair_weight[:, :, 0:1] * first_rows + pair_weight[:, :, 1:2] * second_rows
    return combined.reshape(TOKENS, D)

def forward(tokens, dense_norm_gain, dense_norm_bias, dense_attend_in, dense_attend_bias, dense_attend_out, dense_attend_out_bias, feed_norm_gain, feed_norm_bias, feed_in, feed_in_bias, feed_out, feed_out_bias, sparse_norm_gain, sparse_norm_bias, sparse_attend_in, sparse_attend_bias, sparse_attend_out, sparse_attend_out_bias, route_norm_gain, route_norm_bias, router, expert_in, expert_in_bias, expert_out, expert_out_bias, router_noise, picks, priority):
    residual = tokens
    residual = residual + attention(residual, dense_norm_gain, dense_norm_bias, dense_attend_in, dense_attend_bias, dense_attend_out, dense_attend_out_bias)
    residual = residual + feed_forward(residual, feed_norm_gain, feed_norm_bias, feed_in, feed_in_bias, feed_out, feed_out_bias)
    residual = residual + attention(residual, sparse_norm_gain, sparse_norm_bias, sparse_attend_in, sparse_attend_bias, sparse_attend_out, sparse_attend_out_bias)
    residual = residual + mixture(residual, route_norm_gain, route_norm_bias, router, expert_in, expert_in_bias, expert_out, expert_out_bias, router_noise, picks, priority)
    return residual

def reference(tokens, cotangent, picks, priority, router_noise, dense_norm_gain, dense_norm_bias, dense_attend_in, dense_attend_bias, dense_attend_out, dense_attend_out_bias, feed_norm_gain, feed_norm_bias, feed_in, feed_in_bias, feed_out, feed_out_bias, sparse_norm_gain, sparse_norm_bias, sparse_attend_in, sparse_attend_bias, sparse_attend_out, sparse_attend_out_bias, route_norm_gain, route_norm_bias, router, expert_in, expert_in_bias, expert_out, expert_out_bias):
    floats = (tokens, dense_norm_gain, dense_norm_bias, dense_attend_in, dense_attend_bias, dense_attend_out, dense_attend_out_bias, feed_norm_gain, feed_norm_bias, feed_in, feed_in_bias, feed_out, feed_out_bias, sparse_norm_gain, sparse_norm_bias, sparse_attend_in, sparse_attend_bias, sparse_attend_out, sparse_attend_out_bias, route_norm_gain, route_norm_bias, router, expert_in, expert_in_bias, expert_out, expert_out_bias)
    floats = tuple((array_in.astype(jnp.float32) for array_in in floats))
    noise_f = router_noise.astype(jnp.float32)

    def whole_net(*params):
        return forward(*params, noise_f, picks, priority)
    final, pullback = jax.vjp(whole_net, *floats)
    grads = pullback(cotangent.astype(jnp.float32))
    return (final.astype(jnp.bfloat16), grads[0], grads[1], grads[2], grads[3], grads[4], grads[5], grads[6], grads[7], grads[8], grads[9], grads[10], grads[11], grads[12], grads[13], grads[14], grads[15], grads[16], grads[17], grads[18], grads[19], grads[20], grads[21], grads[22], grads[23], grads[24], grads[25])
```

```python
import jax
import jax.numpy as jnp
from jax import lax
from jax.experimental import pallas as pl
from jax.experimental.pallas import tpu as pltpu
from jax.sharding import PartitionSpec as P

HEAD = 64
LEN = 196
PAD = 208
EPSILON = 1e-06
BF = jnp.bfloat16
F32 = jnp.float32
NN = ((1,), (0,))
NT = ((1,), (1,))
TN = ((0,), (0,))
SQRT_HALF = 0.7071067811865476
VMEM_LIMIT = 60 * 1024 * 1024


def dot(a, b, dims):
    return lax.dot_general(a, b, (dims, ((), ())), preferred_element_type=F32)


def norm_parts(x):
    average = jnp.mean(x, axis=-1, keepdims=True)
    centred = x - average
    variance = jnp.mean(centred * centred, axis=-1, keepdims=True)
    scale = lax.rsqrt(variance + EPSILON)
    return centred * scale, scale


def norm_back(hat, scale, gain, grad):
    inner = grad * gain
    first = jnp.mean(inner, axis=-1, keepdims=True)
    second = jnp.mean(inner * hat, axis=-1, keepdims=True)
    return scale * (inner - first - hat * second)


def gelu_parts(u):
    z = jnp.abs(u) * SQRT_HALF
    t = 1.0 / (1.0 + 0.3275911 * z)
    bell = jnp.exp(-(z * z))
    poly = t * (
        0.254829592
        + t * (-0.284496736 + t * (1.421413741 + t * (-1.453152027 + t * 1.061405429)))
    )
    tail = 0.5 * poly * bell
    cdf = jnp.where(u >= 0.0, 1.0 - tail, tail)
    return u * cdf, cdf + u * (bell * 0.3989422804014327)


def whole():
    return pl.BlockSpec(memory_space=pltpu.VMEM)


def params(semantics=1):
    return pltpu.CompilerParams(
        dimension_semantics=("arbitrary",) * semantics, vmem_limit_bytes=VMEM_LIMIT
    )


def key_mask():
    rows = lax.broadcasted_iota(jnp.int32, (PAD, 1), 0)
    return jnp.where(rows < LEN, 0.0, -1e30)


def attend_backward_kernel(
    g_ref,
    h_ref,
    gain_ref,
    bias_ref,
    w_ref,
    qkv_ref,
    lse_ref,
    ctx_ref,
    gout_ref,
    dw_ref,
    small_ref,
    acc_ref,
    dqkv_ref,
    dc_ref,
    db_ref,
):
    step = pl.program_id(0)
    mine = lax.axis_index("tp")
    shards = w_ref.shape[0]
    width = w_ref.shape[1] // 4
    heads = width // HEAD

    @pl.when(step == 0)
    def _():
        acc_ref[...] = jnp.zeros_like(acc_ref)
        db_ref[...] = jnp.zeros_like(db_ref)
        small_ref[...] = jnp.zeros_like(small_ref)

    grad = g_ref[...]
    hat, scale = norm_parts(h_ref[...])
    a = (hat * gain_ref[...] + bias_ref[...]).astype(BF)
    gr = grad.astype(BF)
    mask = key_mask()
    da = jnp.zeros(grad.shape, F32)
    factor = HEAD**-0.5
    for r in range(shards):
        dc_ref[...] = dot(w_ref[r, 3 * width :, :], gr, NT).astype(BF)
        acc_ref[r, 3 * width :, :] += dot(ctx_ref[0, r], gr, NN)
        for h in range(heads):
            lo = HEAD * h
            q = qkv_ref[0, r, lo : lo + HEAD, :]
            k = qkv_ref[0, r, width + lo : width + lo + HEAD, :]
            v = qkv_ref[0, r, 2 * width + lo : 2 * width + lo + HEAD, :]
            dc = dc_ref[lo : lo + HEAD, :]
            s = dot(k, q, TN) * factor + mask
            p = jnp.exp(s - lse_ref[0, r, h : h + 1, :])
            pb = p.astype(BF)
            dp = dot(v, dc, TN)
            dv = dot(dc, pb, NT)
            pdp = p * dp
            delta = jnp.sum(pdp, axis=0, keepdims=True)
            ds = (pdp - p * delta).astype(BF)
            dq = dot(k, ds, NN) * factor
            dk = dot(q, ds, NT) * factor
            dqkv_ref[lo : lo + HEAD, :] = dq.astype(BF)
            dqkv_ref[width + lo : width + lo + HEAD, :] = dk.astype(BF)
            dqkv_ref[2 * width + lo : 2 * width + lo + HEAD, :] = dv.astype(BF)
        dqkv = dqkv_ref[...]
        acc_ref[r, : 3 * width, :] += dot(dqkv, a, NN)
        db_ref[r] += jnp.sum(dqkv.astype(F32), axis=1, keepdims=True)
        da += dot(dqkv, w_ref[r, : 3 * width, :], TN)
    gout_ref[...] = grad + norm_back(hat, scale, gain_ref[...], da)
    small_ref[0:1, :] += jnp.sum(da * hat, axis=0, keepdims=True)
    small_ref[1:2, :] += jnp.sum(da, axis=0, keepdims=True)
    small_ref[2:3, :] += jnp.sum(gr.astype(F32), axis=0, keepdims=True)

    @pl.when(step == pl.num_programs(0) - 1)
    def _():
        dw_ref[...] = acc_ref[...].astype(BF)
        for r in range(shards):
            line = jnp.transpose(jnp.broadcast_to(db_ref[r], (3 * width, 128)))[0:1, :]
            line = jnp.concatenate([line, jnp.zeros((1, width), F32)], axis=1)
            small_ref[pl.ds(3 + (mine ^ r), 1), :] = line


def attend_backward(grad, h, gain, bias, w, kept):
    qkv, lse, ctx = kept
    rows, depth = h.shape
    images = rows // PAD
    shards, four, _ = w.shape
    width = four // 4
    heads = width // HEAD
    row_block = pl.BlockSpec((PAD, depth), lambda i: (i, 0))
    flops = 2 * rows * depth * depth * 4 + 4 * rows * PAD * depth
    return pl.pallas_call(
        attend_backward_kernel,
        grid=(images,),
        in_specs=[
            row_block,
            row_block,
            whole(),
            whole(),
            whole(),
            pl.BlockSpec((1, shards, 3 * width, PAD), lambda i: (i, 0, 0, 0)),
            pl.BlockSpec((1, shards, heads, PAD), lambda i: (i, 0, 0, 0)),
            pl.BlockSpec((1, shards, width, PAD), lambda i: (i, 0, 0, 0)),
        ],
        out_specs=[row_block, whole(), whole()],
        out_shape=[
            jax.ShapeDtypeStruct((rows, depth), F32),
            jax.ShapeDtypeStruct((shards, four, depth), BF),
            jax.ShapeDtypeStruct((8, depth), F32),
        ],
        scratch_shapes=[
            pltpu.VMEM((shards, four, depth), F32),
            pltpu.VMEM((3 * width, PAD), BF),
            pltpu.VMEM((width, PAD), BF),
            pltpu.VMEM((shards, 3 * width, 1), F32),
        ],
        compiler_params=params(),
        cost_estimate=pl.CostEstimate(
            flops=flops * 6, bytes_accessed=30_000_000, transcendentals=rows * PAD * 12
        ),
        name="attend_backward",
    )(grad, h, gain, bias, w, qkv, lse, ctx)


def feed_backward_kernel(
    g_ref,
    h_ref,
    gain_ref,
    bias_ref,
    w_ref,
    hid_ref,
    slope_ref,
    gout_ref,
    dw_ref,
    small_ref,
    m_ref,
    gr_ref,
    dm_ref,
):
    step = pl.program_id(0)
    depth = h_ref.shape[1]
    mine = lax.axis_index("tp")

    @pl.when(step == 0)
    def _():
        hat, _ = norm_parts(h_ref[...])
        m_ref[...] = (hat * gain_ref[...] + bias_ref[...]).astype(BF)
        gr_ref[...] = g_ref[...].astype(BF)
        dm_ref[...] = jnp.zeros_like(dm_ref)

    gr = gr_ref[...]
    dw_ref[0, depth:, :] = dot(hid_ref[0], gr, TN).astype(BF)
    dr = dot(gr, w_ref[0, depth:, :], NT)
    du = (slope_ref[0].astype(F32) * dr).astype(BF)
    small_ref[pl.ds(3 + (mine ^ step), 1), :] = jnp.sum(du.astype(F32), axis=0, keepdims=True)
    dw_ref[0, :depth, :] = dot(m_ref[...], du, TN).astype(BF)
    dm_ref[...] += dot(du, w_ref[0, :depth, :], NT)

    @pl.when(step == pl.num_programs(0) - 1)
    def _():
        hat, scale = norm_parts(h_ref[...])
        dm = dm_ref[...]
        gout_ref[...] = g_ref[...] + norm_back(hat, scale, gain_ref[...], dm)
        small_ref[0:1, :] = jnp.sum(dm * hat, axis=0, keepdims=True)
        small_ref[1:2, :] = jnp.sum(dm, axis=0, keepdims=True)
        small_ref[2:3, :] = jnp.sum(gr_ref[...].astype(F32), axis=0, keepdims=True)
        small_ref[7:8, :] = jnp.zeros((1, depth), F32)


def feed_backward(grad, h, gain, bias, w, kept):
    hid, slope = kept
    rows, depth = h.shape
    shards, double, hidden = w.shape
    shard = lambda i: (i, 0, 0)
    return pl.pallas_call(
        feed_backward_kernel,
        grid=(shards,),
        in_specs=[
            whole(),
            whole(),
            whole(),
            whole(),
            pl.BlockSpec((1, double, hidden), shard),
            pl.BlockSpec((1, rows, hidden), shard),
            pl.BlockSpec((1, rows, hidden), shard),
        ],
        out_specs=[
            whole(),
            pl.BlockSpec((1, double, hidden), shard),
            whole(),
        ],
        out_shape=[
            jax.ShapeDtypeStruct((rows, depth), F32),
            jax.ShapeDtypeStruct((shards, double, hidden), BF),
            jax.ShapeDtypeStruct((8, depth), F32),
        ],
        scratch_shapes=[
            pltpu.VMEM((rows, depth), BF),
            pltpu.VMEM((rows, depth), BF),
            pltpu.VMEM((rows, depth), F32),
        ],
        compiler_params=params(),
        cost_estimate=pl.CostEstimate(
            flops=8 * rows * depth * hidden * shards * 2,
            bytes_accessed=35_000_000,
            transcendentals=0,
        ),
        name="feed_backward",
    )(grad, h, gain, bias, w, hid, slope)


def expert_pair(mine_ref, other_ref):
    first = lax.rem(lax.axis_index("ep"), 2) == 0
    mine, other = mine_ref[0], other_ref[0]
    return jnp.where(first, mine, other), jnp.where(first, other, mine)


def expert_forward_kernel(x_ref, mine_ref, other_ref, b1_ref, b2_ref, y_ref, hid_ref, slope_ref, acc_ref):
    r = pl.program_id(0)

    @pl.when(r == 0)
    def _():
        acc_ref[...] = jnp.zeros_like(acc_ref)

    w_in, w_out = expert_pair(mine_ref, other_ref)
    u = dot(x_ref[...], w_in, NN) + b1_ref[0]
    value, slope = gelu_parts(u)
    value = value.astype(BF)
    hid_ref[0] = value
    slope_ref[0] = slope.astype(BF)
    acc_ref[...] += dot(value, w_out, NN)

    @pl.when(r == pl.num_programs(0) - 1)
    def _():
        y_ref[...] = (acc_ref[...] + b2_ref[...]).astype(BF)


def expert_forward(x, mine, other, b1, b2):
    rows, depth = x.shape
    shards, _, hidden = mine.shape
    shard = lambda r: (r, 0, 0)
    wide = pl.BlockSpec((1, rows, hidden), shard)
    weight = pl.BlockSpec((1, depth, hidden), shard)
    return pl.pallas_call(
        expert_forward_kernel,
        grid=(shards,),
        in_specs=[whole(), weight, weight, pl.BlockSpec((1, 1, hidden), shard), whole()],
        out_specs=[whole(), wide, wide],
        out_shape=[
            jax.ShapeDtypeStruct((rows, depth), BF),
            jax.ShapeDtypeStruct((shards, rows, hidden), BF),
            jax.ShapeDtypeStruct((shards, rows, hidden), BF),
        ],
        scratch_shapes=[pltpu.VMEM((rows, depth), F32)],
        compiler_params=params(),
        cost_estimate=pl.CostEstimate(
            flops=4 * rows * depth * hidden * shards * 2,
            bytes_accessed=25_000_000,
            transcendentals=rows * hidden * shards,
        ),
        name="expert_forward",
    )(x, mine, other, b1, b2)


def expert_input_kernel(
    y_ref,
    cot_ref,
    gate_ref,
    mine_ref,
    other_ref,
    slope_ref,
    wy_ref,
    dy_ref,
    dx_ref,
    dgate_ref,
    du_ref,
    small_ref,
    acc_ref,
):
    r = pl.program_id(0)
    mine = lax.axis_index("tp")

    @pl.when(r == 0)
    def _():
        y = y_ref[...].astype(F32)
        cot = cot_ref[...].astype(F32)
        gate = gate_ref[...]
        dgate_ref[...] = jnp.sum(cot * y, axis=1, keepdims=True)
        wy_ref[...] = (gate * y).astype(BF)
        dy = (gate * cot).astype(BF)
        dy_ref[...] = dy
        small_ref[4:5, :] = jnp.sum(dy.astype(F32), axis=0, keepdims=True)
        small_ref[5:8, :] = jnp.zeros((3, dy.shape[1]), F32)
        acc_ref[...] = jnp.zeros_like(acc_ref)

    w_in, w_out = expert_pair(mine_ref, other_ref)
    dr = dot(dy_ref[...], w_out, NT)
    du = (slope_ref[0].astype(F32) * dr).astype(BF)
    du_ref[0] = du
    small_ref[pl.ds(mine ^ r, 1), :] = jnp.sum(du.astype(F32), axis=0, keepdims=True)
    acc_ref[...] += dot(du, w_in, NT)

    @pl.when(r == pl.num_programs(0) - 1)
    def _():
        dx_ref[...] = acc_ref[...].astype(BF)


def expert_input(y, cot, gate, mine, other, slope):
    rows, depth = y.shape
    shards, _, hidden = mine.shape
    shard = lambda r: (r, 0, 0)
    wide = pl.BlockSpec((1, rows, hidden), shard)
    weight = pl.BlockSpec((1, depth, hidden), shard)
    return pl.pallas_call(
        expert_input_kernel,
        grid=(shards,),
        in_specs=[whole(), whole(), whole(), weight, weight, wide],
        out_specs=[
            whole(),
            whole(),
            whole(),
            whole(),
            wide,
            whole(),
        ],
        out_shape=[
            jax.ShapeDtypeStruct((rows, depth), BF),
            jax.ShapeDtypeStruct((rows, depth), BF),
            jax.ShapeDtypeStruct((rows, depth), BF),
            jax.ShapeDtypeStruct((rows, 1), F32),
            jax.ShapeDtypeStruct((shards, rows, hidden), BF),
            jax.ShapeDtypeStruct((8, depth), F32),
        ],
        scratch_shapes=[pltpu.VMEM((rows, depth), F32)],
        compiler_params=params(),
        cost_estimate=pl.CostEstimate(
            flops=4 * rows * depth * hidden * shards * 2,
            bytes_accessed=25_000_000,
            transcendentals=0,
        ),
        name="expert_input",
    )(y, cot, gate, mine, other, slope)


def expert_weight_kernel(x_ref, dy_ref, hid_ref, du_ref, dw_ref):
    depth = x_ref.shape[1]
    dw_ref[0, depth:, :] = dot(hid_ref[0], dy_ref[...], TN).astype(BF)
    dw_ref[0, :depth, :] = dot(x_ref[...], du_ref[0], TN).astype(BF)


def expert_weight(x, dy, hid, du):
    rows, depth = x.shape
    shards, _, hidden = hid.shape
    shard = lambda r: (r, 0, 0)
    wide = pl.BlockSpec((1, rows, hidden), shard)
    return pl.pallas_call(
        expert_weight_kernel,
        grid=(shards,),
        in_specs=[whole(), whole(), wide, wide],
        out_specs=pl.BlockSpec((1, 2 * depth, hidden), shard),
        out_shape=jax.ShapeDtypeStruct((shards, 2 * depth, hidden), BF),
        compiler_params=params(),
        cost_estimate=pl.CostEstimate(
            flops=4 * rows * depth * hidden * shards * 2,
            bytes_accessed=25_000_000,
            transcendentals=0,
        ),
        name="expert_weight",
    )(x, dy, hid, du)


ROUTES = 6


def attend_image(x, gain, bias, w_ref, biases_ref, bias_row, bout, qkv_ref, lse_ref, ctx_ref):
    shards = w_ref.shape[0]
    width = w_ref.shape[1] // 4
    heads = width // HEAD
    hat, _ = norm_parts(x)
    a = (hat * gain + bias).astype(BF)
    mask = key_mask()
    branch = jnp.zeros(x.shape, F32)
    for r in range(shards):
        column = jnp.transpose(biases_ref[r])[: 3 * width, bias_row : bias_row + 1]
        qkv = (dot(w_ref[r, : 3 * width, :], a, NT) + column).astype(BF)
        qkv_ref[0, r] = qkv
        for h in range(heads):
            q = qkv[HEAD * h : HEAD * (h + 1)]
            k = qkv[width + HEAD * h : width + HEAD * (h + 1)]
            v = qkv[2 * width + HEAD * h : 2 * width + HEAD * (h + 1)]
            s = dot(k, q, TN) * (HEAD**-0.5) + mask
            peak = jnp.max(s, axis=0, keepdims=True)
            e = jnp.exp(s - peak)
            total = jnp.sum(e, axis=0, keepdims=True)
            lse_ref[0, r, h : h + 1, :] = peak + jnp.log(total)
            c = dot(v, e.astype(BF), NN) * (1.0 / total)
            ctx_ref[0, r, HEAD * h : HEAD * (h + 1), :] = c.astype(BF)
        branch += dot(ctx_ref[0, r], w_ref[r, 3 * width :, :], TN)
    return x + branch + bout


def forward_kernel(
    x_ref,
    vec_ref,
    bias_ref,
    one_ref,
    feed_ref,
    two_ref,
    h1_ref,
    h2_ref,
    h3_ref,
    qkv1_ref,
    lse1_ref,
    ctx1_ref,
    hid_ref,
    slope_ref,
    qkv2_ref,
    lse2_ref,
    ctx2_ref,
    w1_out,
    wf_out,
    w2_out,
    normed_out,
    biases_out,
    h_ref,
    w1_ref,
    wf_ref,
    w2_ref,
    b_ref,
    n_ref,
    send_sem,
    recv_sem,
    n_send,
    n_recv,
    small_send,
    small_recv,
    local_sem,
):
    step = pl.program_id(0)
    images = 4
    mine = lax.axis_index("tp")
    place = lax.axis_index("ep")
    core = lax.rem(place, 2)
    side = lax.rem(mine, 2)
    to_x = {"tp": mine ^ 1}
    to_y = {"tp": mine ^ 2}
    to_far = {"tp": mine ^ 3}
    to_core = {"ep": place ^ 1}
    depth = x_ref.shape[1]

    def remote(src, dst, sends, recvs, index, peer):
        return pltpu.make_async_remote_copy(
            src_ref=src,
            dst_ref=dst,
            send_sem=sends.at[index],
            recv_sem=recvs.at[index],
            device_id=peer,
            device_id_type=pl.DeviceIdType.MESH,
        )

    def copies(group, own, full):
        rows = own.shape[0] // 2
        start = pl.multiple_of(core * rows, rows)
        quarter = rows // 2
        middle = pl.multiple_of(start + quarter, quarter)
        half = pl.ds(start, rows)
        low = pl.ds(start, quarter)
        high = pl.ds(middle, quarter)

        def make(k, src, dst, peer):
            return remote(src, dst, send_sem, recv_sem, (group, k), peer)

        return [
            make(0, own.at[half], full.at[1, half], to_x),
            make(1, own.at[half], full.at[2, half], to_y),
            make(2, full.at[1, low], full.at[3, low], to_y),
            make(3, full.at[2, high], full.at[3, high], to_x),
            make(4, full.at[pl.ds(1, 2), half], full.at[pl.ds(1, 2), half], to_core),
            make(5, full.at[3, half], full.at[3, half], to_core),
        ]

    one = copies(0, one_ref, w1_ref)
    feed = copies(1, feed_ref, wf_ref)
    two = copies(2, two_ref, w2_ref)

    small = [
        remote(bias_ref, b_ref.at[r], small_send, small_recv, r - 1, peer)
        for r, peer in ((1, to_x), (2, to_y), (3, to_far))
    ]
    own_local = [
        pltpu.make_async_copy(one_ref, w1_ref.at[0], local_sem.at[0]),
        pltpu.make_async_copy(feed_ref, wf_ref.at[0], local_sem.at[1]),
        pltpu.make_async_copy(two_ref, w2_ref.at[0], local_sem.at[2]),
    ]
    saves = [
        pltpu.make_async_copy(w1_ref, w1_out, local_sem.at[4]),
        pltpu.make_async_copy(wf_ref, wf_out, local_sem.at[5]),
        pltpu.make_async_copy(w2_ref, w2_out, local_sem.at[6]),
    ]

    def rows_copy(i):
        rows = pl.ds(PAD * i, PAD)
        low, high = pl.ds(PAD * i, 96), pl.ds(PAD * i + 96, PAD - 96)
        return [
            remote(n_ref.at[i], normed_out.at[1, rows], n_send, n_recv, (0, i), to_x),
            remote(n_ref.at[i], normed_out.at[2, rows], n_send, n_recv, (1, i), to_y),
            remote(normed_out.at[1, low], normed_out.at[3, low], n_send, n_recv, (2, i), to_y),
            remote(normed_out.at[2, high], normed_out.at[3, high], n_send, n_recv, (3, i), to_x),
            pltpu.make_async_copy(n_ref.at[i], normed_out.at[0, rows], local_sem.at[8 + i]),
        ]

    def vec(k):
        return vec_ref[k : k + 1, :]

    @pl.when(step == 0)
    def _():
        barrier = pltpu.get_barrier_semaphore()
        for peer in (to_x, to_y, to_far, to_core):
            pl.semaphore_signal(barrier, inc=1, device_id=peer, device_id_type=pl.DeviceIdType.MESH)
        pl.semaphore_wait(barrier, 4)
        one[0].start()
        one[1].start()
        own_local[0].start()
        for copy in small:
            copy.start()
        b_ref[0] = bias_ref[...]
        one[0].wait_recv()
        one[1].wait_recv()
        one[2].start()
        one[3].start()
        one[4].start()
        one[2].wait_recv()
        one[3].wait_recv()
        one[5].start()
        feed[0].start()
        feed[1].start()
        own_local[1].start()
        own_local[2].start()
        own_local[0].wait()
        for copy in small:
            copy.wait_recv()
        one[4].wait_recv()
        one[5].wait_recv()

    @pl.when(step == 2)
    def _():
        saves[0].start()
        feed[0].wait_recv()
        feed[1].wait_recv()
        feed[2].start()
        feed[3].start()
        feed[4].start()

    @pl.when(step == 4)
    def _():
        feed[2].wait_recv()
        feed[3].wait_recv()
        feed[5].start()
        two[0].start()
        two[1].start()
        own_local[1].wait()
        feed[4].wait_recv()
        feed[5].wait_recv()

    @pl.when(step == 6)
    def _():
        saves[1].start()
        two[0].wait_recv()
        two[1].wait_recv()
        two[2].start()
        two[3].start()
        two[4].start()

    @pl.when(step == 7)
    def _():
        two[2].wait_recv()
        two[3].wait_recv()
        two[5].start()

    @pl.when(step == 8)
    def _():
        own_local[2].wait()
        two[4].wait_recv()
        two[5].wait_recv()

    @pl.when(step == 10)
    def _():
        saves[2].start()

    @pl.when(step < images)
    def _():
        x = x_ref[pl.ds(pl.multiple_of(step * PAD, PAD), PAD), :].astype(F32)
        h = attend_image(
            x, vec(0), vec(1), w1_ref, b_ref, 0, vec(2), qkv1_ref, lse1_ref, ctx1_ref
        )
        h_ref[step] = h
        h1_ref[...] = h

    @pl.when((step >= images) & (step < 2 * images))
    def _():
        tile = step - images
        x = h_ref[tile]
        hat, _ = norm_parts(x)
        m = (hat * vec(3) + vec(4)).astype(BF)
        acc = x + vec(5)
        for r in range(wf_ref.shape[0]):
            u = dot(m, wf_ref[r, :depth, :], NN) + b_ref[r, 2:3, :]
            value, slope = gelu_parts(u)
            value = value.astype(BF)
            hid_ref[r] = value
            slope_ref[r] = slope.astype(BF)
            acc += dot(value, wf_ref[r, depth:, :], NN)
        h_ref[tile] = acc
        h2_ref[...] = acc

    @pl.when(step >= 2 * images)
    def _():
        image = step - 2 * images
        h = attend_image(
            h_ref[image], vec(6), vec(7), w2_ref, b_ref, 1, vec(8), qkv2_ref, lse2_ref, ctx2_ref
        )
        h3_ref[...] = h
        hat, _ = norm_parts(h)
        n_ref[image] = (hat * vec(9) + vec(10)).astype(BF)

    for i in range(images):

        @pl.when(step == 2 * images + i)
        def _(i=i):
            to_send = rows_copy(i)
            to_send[0].start()
            to_send[1].start()
            to_send[4].start()
            if i > 0:
                before = rows_copy(i - 1)
                before[0].wait_recv()
                before[1].wait_recv()
                before[2].start()
                before[3].start()

    @pl.when(step == 3 * images - 1)
    def _():
        last = rows_copy(images - 1)
        last[0].wait_recv()
        last[1].wait_recv()
        last[2].start()
        last[3].start()
        pltpu.make_async_copy(b_ref, biases_out, local_sem.at[7]).start()
        for i in range(images):
            moved = rows_copy(i)
            moved[2].wait_recv()
            moved[3].wait_recv()
            for k in range(4):
                moved[k].wait_send()
            moved[4].wait()
        for group in (one, feed, two):
            for copy in group:
                copy.wait_send()
        for copy in small:
            copy.wait_send()
        for copy in saves:
            copy.wait()
        pltpu.make_async_copy(b_ref, biases_out, local_sem.at[7]).wait()


def dense_forward(x, vectors, bias, pack_one, pack_feed, pack_two):
    rows, depth = x.shape
    images = rows // PAD
    shards = 4
    four = pack_one.shape[0]
    width = four // 4
    heads = width // HEAD
    double, hidden = pack_feed.shape
    any_spec = pl.BlockSpec(memory_space=pl.ANY)

    def part(number):
        return lambda s: jnp.clip(s - images * number, 0, images - 1)

    def row_spec(number):
        at = part(number)
        return pl.BlockSpec((PAD, depth), lambda s: (at(s), 0))

    def attend_specs(number):
        at = part(number)
        return [
            pl.BlockSpec((1, shards, 3 * width, PAD), lambda s: (at(s), 0, 0, 0)),
            pl.BlockSpec((1, shards, heads, PAD), lambda s: (at(s), 0, 0, 0)),
            pl.BlockSpec((1, shards, width, PAD), lambda s: (at(s), 0, 0, 0)),
        ]

    tile_at = part(1)
    hid_spec = pl.BlockSpec((shards, PAD, hidden), lambda s: (0, tile_at(s), 0))
    shape = jax.ShapeDtypeStruct
    attend_shapes = [
        shape((images, shards, 3 * width, PAD), BF),
        shape((images, shards, heads, PAD), F32),
        shape((images, shards, width, PAD), BF),
    ]
    out = pl.pallas_call(
        forward_kernel,
        grid=(3 * images,),
        in_specs=[whole(), whole(), whole()] + [any_spec] * 3,
        out_specs=[row_spec(0), row_spec(1), row_spec(2)]
        + attend_specs(0)
        + [hid_spec, hid_spec]
        + attend_specs(2)
        + [any_spec] * 5,
        out_shape=[shape((rows, depth), F32)] * 3
        + attend_shapes
        + [shape((shards, rows, hidden), BF)] * 2
        + attend_shapes
        + [
            shape((shards, four, depth), BF),
            shape((shards, double, hidden), BF),
            shape((shards, four, depth), BF),
            shape((shards, rows, depth), BF),
            shape((shards, 8, depth), F32),
        ],
        scratch_shapes=[
            pltpu.VMEM((images, PAD, depth), F32),
            pltpu.VMEM((shards, four, depth), BF),
            pltpu.VMEM((shards, double, hidden), BF),
            pltpu.VMEM((shards, four, depth), BF),
            pltpu.VMEM((shards, 8, depth), F32),
            pltpu.VMEM((images, PAD, depth), BF),
            pltpu.SemaphoreType.DMA((3, ROUTES)),
            pltpu.SemaphoreType.DMA((3, ROUTES)),
            pltpu.SemaphoreType.DMA((4, 4)),
            pltpu.SemaphoreType.DMA((4, 4)),
            pltpu.SemaphoreType.DMA((3,)),
            pltpu.SemaphoreType.DMA((3,)),
            pltpu.SemaphoreType.DMA((12,)),
        ],
        compiler_params=pltpu.CompilerParams(
            dimension_semantics=("arbitrary",),
            vmem_limit_bytes=VMEM_LIMIT,
            collective_id=0,
            has_side_effects=True,
        ),
        cost_estimate=pl.CostEstimate(
            flops=60_000_000_000, bytes_accessed=60_000_000, transcendentals=10_000_000
        ),
        name="dense_forward",
    )(x, vectors, bias, pack_one, pack_feed, pack_two)
    (h1, h2, h3, q1, l1, c1, hid, slope, q2, l2, c2, w1, wf, w2, normed, biases) = out
    return (h1, h2, h3), (q1, l1, c1), (hid, slope), (q2, l2, c2), (w1, wf, w2), normed, biases


TAIL_ORDER = (0, 1, 2, 3, 0, 1, 0, 2, 0, 1, 3, 0, 1, 2, 4, 0, 3, 1, 2, 0, 3, 1, 2, 4, 0, 3, 1, 2, 4)


def add_rows(dst, src, rows):
    tile = 48

    def body(i, carry):
        at = pl.ds(pl.multiple_of(i * tile, 16), tile)
        dst[at] = (dst[at].astype(F32) + src[at].astype(F32)).astype(BF)
        return carry

    lax.fori_loop(0, rows // tile, body, 0)


def plane_bits(size):
    return [1 << k for k in range(1, size.bit_length() - 1)]


def halvings(rows, bits):
    count = 0
    while count < len(bits) and rows % 32 == 0:
        rows //= 2
        count += 1
    return count


def tail_kernel(size, rows_list, *refs):
    groups = len(rows_list)
    bits = plane_bits(size)
    take = iter(refs)
    sources = [next(take) for _ in range(groups)]
    ig_ref, small_ref = next(take), next(take)
    outs = [next(take) for _ in range(groups)]
    ig_out, total_ref, pair_ref = next(take), next(take), next(take)
    keeps = [next(take) for _ in range(groups)]
    cores = [next(take) for _ in range(groups)]
    firsts = [next(take) for _ in range(groups)]
    seconds = [next(take) for _ in range(groups)]
    planes = [next(take) for _ in range(groups)]
    halves = [next(take) for _ in range(groups)]
    landed = next(take)
    send_sem, recv_sem, local_sem, ig_send, ig_recv, small_send, small_recv = take

    mine = lax.axis_index("tp")
    place = lax.axis_index("ep")
    core = lax.rem(place, 2)
    to_x = {"tp": mine ^ 1}
    to_y = {"tp": mine ^ 2}
    to_core = {"ep": place ^ 1}
    to_plane = [{"ep": place ^ bit} for bit in bits]

    barrier = pltpu.get_barrier_semaphore()
    for peer in [to_x, to_y, to_core] + to_plane:
        pl.semaphore_signal(barrier, inc=1, device_id=peer, device_id_type=pl.DeviceIdType.MESH)
    pl.semaphore_wait(barrier, 3 + len(bits))

    def remote(src, dst, sends, recvs, index, peer):
        return pltpu.make_async_remote_copy(
            src_ref=src,
            dst_ref=dst,
            send_sem=sends.at[index],
            recv_sem=recvs.at[index],
            device_id=peer,
            device_id_type=pl.DeviceIdType.MESH,
        )

    def group_steps(g):
        rows = rows_list[g]
        half, quarter = rows // 2, rows // 4
        source, keep, came, first, second = sources[g], keeps[g], cores[g], firsts[g], seconds[g]
        plane, out, whole_half = planes[g], outs[g], halves[g]
        own_half = pl.ds(pl.multiple_of(core * half, half), half)
        other_half = pl.ds(pl.multiple_of((1 - core) * half, half), half)
        number = iter(range(100))
        sent = []

        def send(src, dst, peer):
            copy = remote(src, dst, send_sem, recv_sem, (g, next(number)), peer)
            copy.start()
            sent.append(copy)
            return copy

        every = pl.ds(0, keep.shape[0])
        local = pltpu.make_async_copy(source.at[every, own_half], keep, local_sem.at[g])
        local.start()
        swap = send(source.at[every, other_half], came, to_core)
        yield
        local.wait()
        swap.wait_recv()
        for r in range(keep.shape[0]):
            add_rows(keep.at[r], came.at[r], half)
        low, high = pl.ds(0, quarter), pl.ds(quarter, quarter)
        waits = [
            send(keep.at[1, low], first.at[0], to_x),
            send(keep.at[3, low], first.at[1], to_x),
            send(keep.at[pl.ds(2, 2), high], first.at[pl.ds(2, 2)], to_y),
        ]
        yield
        for copy in waits:
            copy.wait_recv()
        add_rows(keep.at[2, low], first.at[1], quarter)
        add_rows(keep.at[1, high], first.at[3], quarter)
        waits = [
            send(keep.at[2, low], second.at[0], to_y),
            send(keep.at[1, high], second.at[1], to_x),
        ]
        add_rows(keep.at[0, low], first.at[0], quarter)
        add_rows(keep.at[0, high], first.at[2], quarter)
        yield
        for copy in waits:
            copy.wait_recv()
        add_rows(keep.at[0, low], second.at[0], quarter)
        add_rows(keep.at[0, high], second.at[1], quarter)
        start, length, done = 0, half, []
        offset = 0
        for k, bit in enumerate(bits):
            if k < halvings(half, bits):
                length //= 2
                side = lax.rem(place // bit, 2)
                mine_at = pl.ds(pl.multiple_of(start + side * length, 16), length)
                give_at = pl.ds(pl.multiple_of(start + (1 - side) * length, 16), length)
                land = plane.at[pl.ds(offset, length)]
                copy = send(keep.at[0, give_at], land, to_plane[k])
                done.append((mine_at, k))
                start = start + side * length
            else:
                mine_at = pl.ds(pl.multiple_of(start + 0 * place, 16), length)
                land = plane.at[pl.ds(offset, length)]
                copy = send(keep.at[0, mine_at], land, to_plane[k])
            yield
            copy.wait_recv()
            if k >= halvings(half, bits):
                copy.wait_send()
                sent.pop()
            add_rows(keep.at[0, mine_at], land, length)
            offset += length
        at = done[-1][0]
        whole_half[at] = keep[0, at, :]
        for at, k in done[::-1]:
            copy = send(whole_half.at[at], whole_half.at[at], to_plane[k])
            yield
            copy.wait_recv()
        copy = send(whole_half, out.at[own_half], to_core)
        local = pltpu.make_async_copy(whole_half, out.at[own_half], local_sem.at[groups + g])
        local.start()
        yield
        copy.wait_recv()
        local.wait()
        for copy in sent:
            copy.wait_send()

    def ig_steps():
        half = ig_ref.shape[0] // 32 * 16
        low, high = pl.ds(0, half), pl.ds(half, ig_ref.shape[0] - half)
        near = [
            remote(ig_ref, ig_out.at[mine], ig_send, ig_recv, 0, to_x),
            remote(ig_ref, ig_out.at[mine], ig_send, ig_recv, 1, to_y),
        ]
        local = pltpu.make_async_copy(ig_ref, ig_out.at[mine], local_sem.at[2 * groups])
        local.start()
        for copy in near:
            copy.start()
        yield
        for copy in near:
            copy.wait_recv()
        relay = [
            remote(ig_out.at[mine ^ 1, low], ig_out.at[mine ^ 1, low], ig_send, ig_recv, 2, to_y),
            remote(ig_out.at[mine ^ 2, high], ig_out.at[mine ^ 2, high], ig_send, ig_recv, 3, to_x),
        ]
        for copy in relay:
            copy.start()
        yield
        for copy in relay:
            copy.wait_recv()
        for copy in near + relay:
            copy.wait_send()
        local.wait()

    def small_steps():
        total_ref[...] = small_ref[...]
        peers = [to_x, to_y, to_core] + to_plane
        for k, peer in enumerate(peers):
            copy = remote(total_ref, landed.at[k], small_send, small_recv, k, peer)
            copy.start()
            yield
            copy.wait()
            total_ref[...] += landed[k]
            if k == 2:
                pair_ref[...] = total_ref[...]

    running = [group_steps(g) for g in range(groups)] + [small_steps(), ig_steps()]
    ended = set()

    def advance(which):
        if which not in ended:
            try:
                next(running[which])
            except StopIteration:
                ended.add(which)

    for which in TAIL_ORDER:
        advance(which)
    while len(ended) < len(running):
        for which in range(len(running)):
            advance(which)


def tail(grads, ig, small, size):
    shards, _, depth = grads[0].shape
    rows_list = [g.shape[1] for g in grads]
    groups = len(grads)
    bits = plane_bits(size)
    any_spec = pl.BlockSpec(memory_space=pl.ANY)
    shape = jax.ShapeDtypeStruct

    def plane_rows(rows):
        half, total = rows // 2, 0
        for k in range(len(bits)):
            if k < halvings(rows // 2, bits):
                half //= 2
            total += half
        return total

    copies = 4 + 2 + 2 * len(bits) + 1
    return pl.pallas_call(
        lambda *refs: tail_kernel(size, rows_list, *refs),
        in_specs=[any_spec] * (groups + 1) + [whole()],
        out_specs=[any_spec] * (groups + 1) + [whole(), whole()],
        out_shape=[shape((rows, depth), BF) for rows in rows_list]
        + [shape((shards,) + ig.shape, BF), shape(small.shape, F32), shape(small.shape, F32)],
        scratch_shapes=[pltpu.VMEM((shards, rows // 2, depth), BF) for rows in rows_list]
        + [pltpu.VMEM((shards, rows // 2, depth), BF) for rows in rows_list]
        + [pltpu.VMEM((4, rows // 4, depth), BF) for rows in rows_list]
        + [pltpu.VMEM((2, rows // 4, depth), BF) for rows in rows_list]
        + [pltpu.VMEM((plane_rows(rows), depth), BF) for rows in rows_list]
        + [pltpu.VMEM((rows // 2, depth), BF) for rows in rows_list]
        + [
            pltpu.VMEM((3 + len(bits),) + small.shape, F32),
            pltpu.SemaphoreType.DMA((groups, copies)),
            pltpu.SemaphoreType.DMA((groups, copies)),
            pltpu.SemaphoreType.DMA((2 * groups + 1,)),
            pltpu.SemaphoreType.DMA((4,)),
            pltpu.SemaphoreType.DMA((4,)),
            pltpu.SemaphoreType.DMA((3 + len(bits),)),
            pltpu.SemaphoreType.DMA((3 + len(bits),)),
        ],
        compiler_params=pltpu.CompilerParams(
            vmem_limit_bytes=VMEM_LIMIT, collective_id=1, has_side_effects=True
        ),
        cost_estimate=pl.CostEstimate(flops=30_000_000, bytes_accessed=60_000_000, transcendentals=0),
        name="tail",
    )(*grads, ig, small)


def hop(value, axis, bit):
    size = lax.axis_size(axis)
    return lax.ppermute(value, axis, [(i, i ^ bit) for i in range(size)])


def after(value, *deps):
    return lax.optimization_barrier((value, deps))[0]


def near(value):
    return hop(value, "tp", 1), hop(value, "tp", 2)


def far(from_x, from_y):
    half = from_x.shape[0] // 2
    low = hop(from_x[:half], "tp", 2)
    high = hop(from_y[half:], "tp", 1)
    return jnp.concatenate([low, high])


def gather_tp_small(value):
    return jnp.stack([value, hop(value, "tp", 1), hop(value, "tp", 2), hop(value, "tp", 3)])


def take_half(value, which, axis=0):
    half = value.shape[axis] // 2
    return lax.dynamic_slice_in_dim(value, which * half, half, axis=axis)


def join_halves(value, other, which, axis=0):
    half = value.shape[axis]
    three = jnp.concatenate([value, other, value], axis=axis)
    return lax.dynamic_slice_in_dim(three, which * half, 2 * half, axis=axis)


def plus(a, b):
    return (a.astype(F32) + b.astype(F32)).astype(BF)


def core_sum(value):
    core = lax.axis_index("ep") % 2
    return plus(take_half(value, core, 1), hop(take_half(value, 1 - core, 1), "ep", 1))


def swap_ep(value):
    return lax.all_to_all(value, "ep", split_axis=0, concat_axis=0, tiled=True)


def route_kernel(order_ref, index_ref, hot_ref, out_ref, rank_ref):
    rows = order_ref.shape[1]
    tile = rows // 7
    half = hot_ref.shape[1] // 2
    for i in range(7):
        ids = lax.broadcasted_iota(jnp.int32, (tile, 1), 0) + tile * i
        match = jnp.where(order_ref[...] == ids, 1.0, 0.0).astype(BF)
        rank_ref[tile * i : tile * (i + 1), :] = dot(match, index_ref[...], NN)
    parts = rank_ref[...]
    rank = parts[:, 0:1] * 64.0 + parts[:, 1:2]
    rank_row = jnp.transpose(jnp.broadcast_to(rank, parts.shape))[0:1, :]
    hot = hot_ref[...]
    total = jnp.sum(hot.astype(F32), axis=0, keepdims=True)
    lanes = lax.broadcasted_iota(jnp.int32, (1, 2 * half), 1)
    firsts = jnp.where(lanes < half, total, 0.0)
    firsts = jnp.concatenate([jnp.zeros((1, half), F32), firsts[:, :half]], axis=1)
    for i in range(7):
        at = slice(tile * i, tile * (i + 1))
        earlier = jnp.where(rank_row < rank[at], 1.0, 0.0).astype(BF)
        count = dot(earlier, hot, NN) + firsts
        picked = count * hot[at].astype(F32)
        first = jnp.sum(jnp.where(lanes < half, picked, 0.0), axis=1, keepdims=True)
        second = jnp.sum(jnp.where(lanes < half, 0.0, picked), axis=1, keepdims=True)
        out_ref[at, :] = jnp.where(lanes == 0, first, second)


def route(picks, order):
    rows = picks.shape[0]
    half = 64
    ids = jnp.arange(half, dtype=jnp.int32)[None, :]
    hot = jnp.concatenate([picks[:, 0:1] == ids, picks[:, 1:2] == ids], axis=1).astype(BF)
    line = jnp.arange(rows, dtype=jnp.int32)[:, None]
    column = jnp.arange(2 * half, dtype=jnp.int32)[None, :]
    index = jnp.where(column == 0, line // 64, jnp.where(column == 1, line % 64, 0)).astype(BF)
    out = pl.pallas_call(
        route_kernel,
        in_specs=[whole(), whole(), whole()],
        out_specs=whole(),
        out_shape=jax.ShapeDtypeStruct((rows, 2 * half), F32),
        scratch_shapes=[pltpu.VMEM((rows, 2 * half), F32)],
        compiler_params=pltpu.CompilerParams(vmem_limit_bytes=VMEM_LIMIT),
        cost_estimate=pl.CostEstimate(
            flops=4 * rows * rows * 128, bytes_accessed=4_000_000, transcendentals=0
        ),
        name="route",
    )(order.reshape(1, rows), index, hot)
    return out[:, :2].astype(jnp.int32)


def body(
    tokens,
    cotangent,
    picks,
    priority,
    router_noise,
    dense_norm_gain,
    dense_norm_bias,
    dense_attend_in,
    dense_attend_bias,
    dense_attend_out,
    dense_attend_out_bias,
    feed_norm_gain,
    feed_norm_bias,
    feed_in,
    feed_in_bias,
    feed_out,
    feed_out_bias,
    sparse_norm_gain,
    sparse_norm_bias,
    sparse_attend_in,
    sparse_attend_bias,
    sparse_attend_out,
    sparse_attend_out_bias,
    route_norm_gain,
    route_norm_bias,
    router,
    expert_in,
    expert_in_bias,
    expert_out,
    expert_out_bias,
):
    shards = lax.axis_size("tp")
    experts = lax.axis_size("ep")
    mine = lax.axis_index("tp")
    rows_dev, depth = tokens.shape
    own = rows_dev // shards
    images = own // LEN
    own_pad = images * PAD
    capacity = rows_dev // experts
    part = -(-capacity // (8 * shards)) * 8
    width = dense_attend_bias.shape[1]
    hidden = feed_in_bias.shape[0]

    def pad_images(value):
        blocks = value.reshape(-1, LEN, value.shape[-1])
        return jnp.pad(blocks, ((0, 0), (0, PAD - LEN), (0, 0))).reshape(-1, value.shape[-1])

    def drop_pad(value):
        return value.reshape(images, PAD, depth)[:, :LEN].reshape(own, depth)

    def own_rows(value):
        return lax.dynamic_slice_in_dim(value, mine * own, own, axis=0)

    def by_index(value):
        return jnp.stack(
            [
                lax.dynamic_index_in_dim(value, mine ^ r, axis=0, keepdims=False)
                for r in range(shards)
            ]
        )

    def row(value):
        return value.reshape(1, -1)

    def attend_pack(proj_in, proj_out):
        return jnp.concatenate([proj_in.transpose(1, 2, 0).reshape(3 * width, depth), proj_out])

    pair_side = lax.axis_index("ep") % 2
    chip_side = mine % 2
    same = pair_side == chip_side
    keep_exp = jnp.where(pair_side == 0, expert_in[0], expert_out[0])
    give_exp = jnp.where(pair_side == 0, expert_out[0], expert_in[0])
    vectors = jnp.stack(
        [
            dense_norm_gain,
            dense_norm_bias,
            dense_attend_out_bias,
            feed_norm_gain,
            feed_norm_bias,
            feed_out_bias,
            sparse_norm_gain,
            sparse_norm_bias,
            sparse_attend_out_bias,
            route_norm_gain,
            route_norm_bias,
        ]
    )
    vectors = jnp.pad(vectors, ((0, 5), (0, 0)))

    def bias_line(value):
        gap = jnp.zeros((width,), F32)
        return jnp.concatenate([value[0], gap, value[1], jnp.zeros((depth - 3 * width,), F32)])

    own_biases = jnp.stack(
        [
            bias_line(dense_attend_bias),
            bias_line(sparse_attend_bias),
            feed_in_bias,
            expert_in_bias[0],
            expert_out_bias[0],
        ]
    )
    own_biases = jnp.pad(own_biases, ((0, 3), (0, 0)))
    position = route(picks, priority[0])
    targets = jnp.where(position < capacity, picks * (part * shards) + position, -1).T
    slots = jnp.arange(experts * part, dtype=jnp.int32)

    def slots_of(index):
        block, inside = slots // part, slots % part
        expert = 2 * (block // 2) + index % 2
        quarter = 2 * (index // 2) + block % 2
        return expert * (part * shards) + quarter * part + inside

    slot_ids = slots_of(mine)
    pad_targets = jnp.pad(
        targets.reshape(2, -1, LEN), ((0, 0), (0, 0), (0, PAD - LEN)), constant_values=-1
    ).reshape(2, -1)
    near_targets = jnp.concatenate(
        [
            lax.dynamic_slice_in_dim(pad_targets, (mine ^ r) * own_pad, own_pad, axis=1)
            for r in range(shards)
        ],
        axis=1,
    )
    noise_pad = pad_images(router_noise)
    all_slots = jnp.concatenate([slots_of(mine ^ r) for r in range(shards)])
    own_targets = near_targets[:, :own_pad].T
    back_hot = (own_targets[:, 0:1] == all_slots[None, :]) | (
        own_targets[:, 1:2] == all_slots[None, :]
    )
    back_hot_bf = back_hot.astype(BF)

    swapped = hop(give_exp, "ep", 1)
    home_exp = jnp.where(same, keep_exp, swapped)
    away_exp = jnp.where(same, swapped, keep_exp)
    level_zero = after(pad_images(own_rows(tokens)), home_exp, away_exp)
    (level_one, level_two, level_three), kept_one, kept_feed, kept_two, gathered, normed, biases = (
        dense_forward(
            level_zero,
            vectors,
            own_biases,
            attend_pack(dense_attend_in, dense_attend_out),
            jnp.concatenate([feed_in, feed_out]),
            attend_pack(sparse_attend_in, sparse_attend_out),
        )
    )
    w_one, w_feed, w_two = gathered
    level_zero = level_zero.astype(F32)
    exp_small = biases[:, 3:5]
    exp_small = jnp.where(same, exp_small, hop(exp_small, "ep", 1))
    b_exp = exp_small[:, 0:1]
    b_exp_out = exp_small[0, 1:2]

    home_exp = after(home_exp, normed)
    away_exp = after(away_exp, normed)
    exp_x = hop(away_exp, "tp", 1)
    exp_far = hop(away_exp, "tp", 3)
    exp_y = hop(home_exp, "tp", 2)
    other_home = hop(home_exp, "ep", 1)

    all_normed = normed.reshape(shards * own_pad, depth)
    route_normed = normed[0]
    noise = jnp.concatenate(
        [
            lax.dynamic_slice_in_dim(noise_pad, (mine ^ r) * own_pad, own_pad, axis=0)
            for r in range(shards)
        ]
    )
    logits = dot(all_normed, router, NN) + noise
    gates = jax.nn.softmax(logits, axis=-1)
    own_hot = (slot_ids[:, None] == near_targets[0][None, :]) | (
        slot_ids[:, None] == near_targets[1][None, :]
    )
    side_gates = lax.dynamic_index_in_dim(
        gates.T.reshape(experts // 2, 2, -1), chip_side, axis=1, keepdims=False
    )
    hot_gates = own_hot.reshape(experts // 2, 2 * part, -1).astype(F32) * side_gates[:, None, :]
    slot_gate = jnp.sum(hot_gates, axis=2).reshape(-1, 1)

    def two_parts(value):
        high = lax.reduce_precision(value, 8, 7)
        rest = jnp.zeros((value.shape[0], 126), BF)
        return jnp.concatenate([high.astype(BF), (value - high).astype(BF), rest], axis=1)

    def swap_rows(value):
        wide = value.shape[-1]
        return swap_ep(value.reshape(experts, part, wide)).reshape(experts * part, wide)

    rows = dot(own_hot.astype(BF), all_normed, NN).astype(BF)
    arrived = swap_rows(jnp.concatenate([rows, two_parts(slot_gate)], axis=1))
    cot_hot = (slot_ids[:, None] == targets[0][None, :]) | (slot_ids[:, None] == targets[1][None, :])
    cot_sent = dot(after(cot_hot.astype(BF), rows), cotangent, NN).astype(BF)
    cot_rows = swap_rows(cot_sent)
    exp_mine = jnp.stack([home_exp, exp_x, exp_y, exp_far])
    exp_other = jnp.stack(
        [other_home, hop(exp_x, "ep", 1), hop(exp_y, "ep", 1), hop(exp_far, "ep", 1)]
    )
    inputs = arrived[:, :depth]
    gate_in = arrived[:, depth : depth + 2].astype(F32)
    gate_in = gate_in[:, 0:1] + gate_in[:, 1:2]
    outputs, exp_hidden, exp_slope = expert_forward(inputs, exp_mine, exp_other, b_exp, b_exp_out)
    weighted, grad_outputs, grad_inputs, slot_dot, exp_du, small_exp = (
        expert_input(outputs, cot_rows, gate_in, exp_mine, exp_other, exp_slope)
    )
    returned_sent = jnp.concatenate([grad_inputs, two_parts(slot_dot)], axis=1)
    returned = swap_rows(returned_sent)
    g_exp = expert_weight(after(inputs, returned_sent), grad_outputs, exp_hidden, exp_du)
    part_exp = core_sum(g_exp)
    exp_from_y = hop(part_exp[3], "tp", 2)
    returned = after(returned, g_exp)
    near_grad = near(returned)
    grad_slots = jnp.concatenate([returned, *near_grad, far(*near_grad)])
    dot_slots = grad_slots[:, depth : depth + 2].astype(F32)
    dot_slots = dot_slots[:, 0] + dot_slots[:, 1]
    grad_slots = grad_slots[:, :depth]
    weighted = swap_rows(after(weighted, returned))

    grad_stream = pad_images(own_rows(cotangent)).astype(F32)
    own_gates = gates[:own_pad]
    hot_dots = jnp.where(back_hot, dot_slots[None, :], 0.0).reshape(
        own_pad, 2, 2, experts // 2, 2 * part
    )
    by_side = jnp.sum(hot_dots, axis=(1, 4))
    by_side = jnp.where(chip_side == 0, by_side, by_side[:, ::-1])
    grad_gates = by_side.transpose(0, 2, 1).reshape(own_pad, experts)
    grad_logits = own_gates * (grad_gates - jnp.sum(own_gates * grad_gates, axis=1, keepdims=True))
    grad_logits = grad_logits.astype(BF)
    g_router = dot(grad_logits, route_normed, TN)
    grad_normed = dot(grad_logits, router, NT) + dot(back_hot_bf, grad_slots, NN)
    hat, scale = norm_parts(level_three)
    g_route_gain = jnp.sum(grad_normed * hat, axis=0)
    g_route_bias = jnp.sum(grad_normed, axis=0)
    grad_stream = grad_stream + norm_back(hat, scale, route_norm_gain, grad_normed)

    near_weighted = near(after(weighted, grad_stream))
    grad_stream, g_two, small_two = attend_backward(
        grad_stream, level_two, row(sparse_norm_gain), row(sparse_norm_bias), w_two, kept_two
    )
    near_weighted = after(near_weighted, g_two)
    far_weighted = far(*near_weighted)
    exp_from_y = after(exp_from_y, g_two)
    exp_from_y2 = hop(after(part_exp[2], g_two), "tp", 2)
    exp_give = plus(part_exp[1], exp_from_y)
    exp_away = hop(exp_give, "tp", 1)
    grad_stream, g_feed, small_feed = feed_backward(
        grad_stream, level_one, row(feed_norm_gain), row(feed_norm_bias), w_feed, kept_feed
    )
    far_weighted, exp_from_y2, exp_away = lax.optimization_barrier(
        ((far_weighted, exp_from_y2, exp_away), g_feed)
    )[0]
    exp_keep = plus(part_exp[0], exp_from_y2)
    keep_sum = jnp.where(same, exp_keep, exp_away)
    other_sum = hop(jnp.where(same, exp_away, exp_keep), "ep", 1)
    weighted_slots = jnp.concatenate([weighted, *near_weighted, far_weighted])
    level_four = level_three + dot(back_hot_bf, weighted_slots, NN)
    own_final = drop_pad(level_four.astype(BF))
    near_final = near(own_final)
    grad_stream = after(grad_stream, own_final)
    grad_stream, g_one, small_one = attend_backward(
        grad_stream, level_zero, row(dense_norm_gain), row(dense_norm_bias), w_one, kept_one
    )
    near_final = after(near_final, g_one)
    far_final = far(*near_final)

    blank = jnp.zeros_like(small_exp)
    first = chip_side == 0
    small = jnp.concatenate(
        [
            small_one,
            small_feed,
            small_two,
            jnp.where(first, small_exp, blank),
            jnp.where(first, blank, small_exp),
            g_router,
            jnp.pad(jnp.stack([g_route_gain, g_route_bias]), ((0, 6), (0, 0))),
        ]
    )
    t_two, t_feed, t_one, ig_all, total, pair_total = tail(
        [g_two, g_feed, g_one], drop_pad(grad_stream.astype(BF)), small, experts
    )
    input_grad = ig_all.reshape(rows_dev, depth).astype(F32)
    far_final, other_sum = after((far_final, other_sum), t_one)

    def absolute(blocks, kind):
        out = jnp.zeros((rows_dev, depth), kind)
        for r in range(shards):
            out = lax.dynamic_update_slice_in_dim(
                out, blocks[r].astype(kind), (mine ^ r) * own, axis=0
            )
        return out

    final = absolute([own_final, *near_final, far_final], BF)

    def attend_split(value):
        value = value.astype(F32)
        return (
            value[: 3 * width].reshape(3, width, depth).transpose(2, 0, 1),
            value[3 * width :],
        )

    t_exp_in = jnp.where(pair_side == 0, keep_sum, other_sum).astype(F32)
    t_exp_out = jnp.where(pair_side == 0, other_sum, keep_sum).astype(F32)
    t_in_two, t_out_two = attend_split(t_two)
    t_in_one, t_out_one = attend_split(t_one)
    t_feed = t_feed.astype(F32)

    def own_line(value, start):
        return lax.dynamic_slice_in_dim(value, start + mine, 1, axis=0)[0]

    def two_biases(start):
        line = own_line(total, start)
        return jnp.stack([line[:width], line[2 * width : 3 * width]])

    s_one, s_feed, s_two = total[0:8], total[8:16], total[16:24]
    s_exp = lax.dynamic_slice_in_dim(pair_total, 24 + 8 * pair_side, 8, axis=0)
    s_router = total[40 : 40 + experts].T
    s_route = total[40 + experts :]
    return (
        final,
        input_grad,
        s_one[0],
        s_one[1],
        t_in_one,
        two_biases(3),
        t_out_one,
        s_one[2],
        s_feed[0],
        s_feed[1],
        t_feed[:depth],
        own_line(total, 11),
        t_feed[depth:],
        s_feed[2],
        s_two[0],
        s_two[1],
        t_in_two,
        two_biases(19),
        t_out_two,
        s_two[2],
        s_route[0],
        s_route[1],
        s_router,
        t_exp_in[None],
        own_line(s_exp, 0)[None],
        t_exp_out[None],
        s_exp[4][None],
    )


def solution(mesh):
    in_specs = (
        P("ep", None),
        P("ep", None),
        P("ep", None),
        P("ep", None),
        P("ep", None),
        P(),
        P(),
        P(None, None, "tp"),
        P(None, "tp"),
        P("tp", None),
        P(),
        P(),
        P(),
        P(None, "tp"),
        P("tp"),
        P("tp", None),
        P(),
        P(),
        P(),
        P(None, None, "tp"),
        P(None, "tp"),
        P("tp", None),
        P(),
        P(),
        P(),
        P(),
        P("ep", None, "tp"),
        P("ep", "tp"),
        P("ep", "tp", None),
        P("ep", None),
    )
    out_specs = (
        P("ep", None),
        P("ep", None),
        P(),
        P(),
        P(None, None, "tp"),
        P(None, "tp"),
        P("tp", None),
        P(),
        P(),
        P(),
        P(None, "tp"),
        P("tp"),
        P("tp", None),
        P(),
        P(),
        P(),
        P(None, None, "tp"),
        P(None, "tp"),
        P("tp", None),
        P(),
        P(),
        P(),
        P(),
        P("ep", None, "tp"),
        P("ep", "tp"),
        P("ep", "tp", None),
        P("ep", None),
    )
    return jax.shard_map(body, mesh=mesh, in_specs=in_specs, out_specs=out_specs, check_vma=False)
```

```python
import jax
import jax.numpy as jnp
from jax import lax
from jax.experimental import pallas as pl
from jax.experimental.pallas import tpu as pltpu
from jax.sharding import PartitionSpec as P

HEAD = 64
LEN = 196
PAD = 208
EPSILON = 1e-06
BF = jnp.bfloat16
F32 = jnp.float32
NN = ((1,), (0,))
NT = ((1,), (1,))
TN = ((0,), (0,))
SQRT_HALF = 0.7071067811865476
VMEM_LIMIT = 60 * 1024 * 1024


def dot(a, b, dims):
    return lax.dot_general(a, b, (dims, ((), ())), preferred_element_type=F32)


def norm_parts(x):
    average = jnp.mean(x, axis=-1, keepdims=True)
    centred = x - average
    variance = jnp.mean(centred * centred, axis=-1, keepdims=True)
    scale = lax.rsqrt(variance + EPSILON)
    return centred * scale, scale


def norm_back(hat, scale, gain, grad):
    inner = grad * gain
    first = jnp.mean(inner, axis=-1, keepdims=True)
    second = jnp.mean(inner * hat, axis=-1, keepdims=True)
    return scale * (inner - first - hat * second)


def gelu_parts(u):
    z = jnp.abs(u) * SQRT_HALF
    t = 1.0 / (1.0 + 0.3275911 * z)
    bell = jnp.exp(-(z * z))
    poly = t * (
        0.254829592
        + t * (-0.284496736 + t * (1.421413741 + t * (-1.453152027 + t * 1.061405429)))
    )
    tail = 0.5 * poly * bell
    cdf = jnp.where(u >= 0.0, 1.0 - tail, tail)
    return u * cdf, cdf + u * (bell * 0.3989422804014327)


def whole():
    return pl.BlockSpec(memory_space=pltpu.VMEM)


def params(semantics=1):
    return pltpu.CompilerParams(
        dimension_semantics=("arbitrary",) * semantics, vmem_limit_bytes=VMEM_LIMIT
    )


def key_mask():
    rows = lax.broadcasted_iota(jnp.int32, (PAD, 1), 0)
    return jnp.where(rows < LEN, 0.0, -1e30)


def attend_backward_kernel(
    g_ref,
    h_ref,
    gain_ref,
    bias_ref,
    w_ref,
    qkv_ref,
    lse_ref,
    ctx_ref,
    gout_ref,
    dw_ref,
    small_ref,
    acc_ref,
    dqkv_ref,
    dc_ref,
    db_ref,
):
    step = pl.program_id(0)
    mine = lax.axis_index("tp")
    shards = w_ref.shape[0]
    width = w_ref.shape[1] // 4
    heads = width // HEAD

    @pl.when(step == 0)
    def _():
        acc_ref[...] = jnp.zeros_like(acc_ref)
        db_ref[...] = jnp.zeros_like(db_ref)
        small_ref[...] = jnp.zeros_like(small_ref)

    grad = g_ref[...]
    hat, scale = norm_parts(h_ref[...])
    a = (hat * gain_ref[...] + bias_ref[...]).astype(BF)
    gr = grad.astype(BF)
    mask = key_mask()
    da = jnp.zeros(grad.shape, F32)
    factor = HEAD**-0.5
    for r in range(shards):
        dc_ref[...] = dot(w_ref[r, 3 * width :, :], gr, NT).astype(BF)
        acc_ref[r, 3 * width :, :] += dot(ctx_ref[0, r], gr, NN)
        for h in range(heads):
            lo = HEAD * h
            q = qkv_ref[0, r, lo : lo + HEAD, :]
            k = qkv_ref[0, r, width + lo : width + lo + HEAD, :]
            v = qkv_ref[0, r, 2 * width + lo : 2 * width + lo + HEAD, :]
            dc = dc_ref[lo : lo + HEAD, :]
            s = dot(k, q, TN) * factor + mask
            p = jnp.exp(s - lse_ref[0, r, h : h + 1, :])
            pb = p.astype(BF)
            dp = dot(v, dc, TN)
            dv = dot(dc, pb, NT)
            pdp = p * dp
            delta = jnp.sum(pdp, axis=0, keepdims=True)
            ds = (pdp - p * delta).astype(BF)
            dq = dot(k, ds, NN) * factor
            dk = dot(q, ds, NT) * factor
            dqkv_ref[lo : lo + HEAD, :] = dq.astype(BF)
            dqkv_ref[width + lo : width + lo + HEAD, :] = dk.astype(BF)
            dqkv_ref[2 * width + lo : 2 * width + lo + HEAD, :] = dv.astype(BF)
        dqkv = dqkv_ref[...]
        acc_ref[r, : 3 * width, :] += dot(dqkv, a, NN)
        db_ref[r] += jnp.sum(dqkv.astype(F32), axis=1, keepdims=True)
        da += dot(dqkv, w_ref[r, : 3 * width, :], TN)
    gout_ref[...] = grad + norm_back(hat, scale, gain_ref[...], da)
    small_ref[0:1, :] += jnp.sum(da * hat, axis=0, keepdims=True)
    small_ref[1:2, :] += jnp.sum(da, axis=0, keepdims=True)
    small_ref[2:3, :] += jnp.sum(gr.astype(F32), axis=0, keepdims=True)

    @pl.when(step == pl.num_programs(0) - 1)
    def _():
        dw_ref[...] = acc_ref[...].astype(BF)
        for r in range(shards):
            line = jnp.transpose(jnp.broadcast_to(db_ref[r], (3 * width, 128)))[0:1, :]
            line = jnp.concatenate([line, jnp.zeros((1, width), F32)], axis=1)
            small_ref[pl.ds(3 + (mine ^ r), 1), :] = line


def attend_backward(grad, h, gain, bias, w, kept):
    qkv, lse, ctx = kept
    rows, depth = h.shape
    images = rows // PAD
    shards, four, _ = w.shape
    width = four // 4
    heads = width // HEAD
    row_block = pl.BlockSpec((PAD, depth), lambda i: (i, 0))
    flops = 2 * rows * depth * depth * 4 + 4 * rows * PAD * depth
    return pl.pallas_call(
        attend_backward_kernel,
        grid=(images,),
        in_specs=[
            row_block,
            row_block,
            whole(),
            whole(),
            whole(),
            pl.BlockSpec((1, shards, 3 * width, PAD), lambda i: (i, 0, 0, 0)),
            pl.BlockSpec((1, shards, heads, PAD), lambda i: (i, 0, 0, 0)),
            pl.BlockSpec((1, shards, width, PAD), lambda i: (i, 0, 0, 0)),
        ],
        out_specs=[row_block, whole(), whole()],
        out_shape=[
            jax.ShapeDtypeStruct((rows, depth), F32),
            jax.ShapeDtypeStruct((shards, four, depth), BF),
            jax.ShapeDtypeStruct((8, depth), F32),
        ],
        scratch_shapes=[
            pltpu.VMEM((shards, four, depth), F32),
            pltpu.VMEM((3 * width, PAD), BF),
            pltpu.VMEM((width, PAD), BF),
            pltpu.VMEM((shards, 3 * width, 1), F32),
        ],
        compiler_params=params(),
        cost_estimate=pl.CostEstimate(
            flops=flops * 6, bytes_accessed=30_000_000, transcendentals=rows * PAD * 12
        ),
        name="attend_backward",
    )(grad, h, gain, bias, w, qkv, lse, ctx)


def feed_backward_kernel(
    g_ref,
    h_ref,
    gain_ref,
    bias_ref,
    w_ref,
    hid_ref,
    slope_ref,
    gout_ref,
    dw_ref,
    small_ref,
    m_ref,
    gr_ref,
    dm_ref,
):
    step = pl.program_id(0)
    depth = h_ref.shape[1]
    mine = lax.axis_index("tp")

    @pl.when(step == 0)
    def _():
        hat, _ = norm_parts(h_ref[...])
        m_ref[...] = (hat * gain_ref[...] + bias_ref[...]).astype(BF)
        gr_ref[...] = g_ref[...].astype(BF)
        dm_ref[...] = jnp.zeros_like(dm_ref)

    gr = gr_ref[...]
    dw_ref[0, depth:, :] = dot(hid_ref[0], gr, TN).astype(BF)
    dr = dot(gr, w_ref[0, depth:, :], NT)
    du = (slope_ref[0].astype(F32) * dr).astype(BF)
    small_ref[pl.ds(3 + (mine ^ step), 1), :] = jnp.sum(du.astype(F32), axis=0, keepdims=True)
    dw_ref[0, :depth, :] = dot(m_ref[...], du, TN).astype(BF)
    dm_ref[...] += dot(du, w_ref[0, :depth, :], NT)

    @pl.when(step == pl.num_programs(0) - 1)
    def _():
        hat, scale = norm_parts(h_ref[...])
        dm = dm_ref[...]
        gout_ref[...] = g_ref[...] + norm_back(hat, scale, gain_ref[...], dm)
        small_ref[0:1, :] = jnp.sum(dm * hat, axis=0, keepdims=True)
        small_ref[1:2, :] = jnp.sum(dm, axis=0, keepdims=True)
        small_ref[2:3, :] = jnp.sum(gr_ref[...].astype(F32), axis=0, keepdims=True)
        small_ref[7:8, :] = jnp.zeros((1, depth), F32)


def feed_backward(grad, h, gain, bias, w, kept):
    hid, slope = kept
    rows, depth = h.shape
    shards, double, hidden = w.shape
    shard = lambda i: (i, 0, 0)
    return pl.pallas_call(
        feed_backward_kernel,
        grid=(shards,),
        in_specs=[
            whole(),
            whole(),
            whole(),
            whole(),
            pl.BlockSpec((1, double, hidden), shard),
            pl.BlockSpec((1, rows, hidden), shard),
            pl.BlockSpec((1, rows, hidden), shard),
        ],
        out_specs=[
            whole(),
            pl.BlockSpec((1, double, hidden), shard),
            whole(),
        ],
        out_shape=[
            jax.ShapeDtypeStruct((rows, depth), F32),
            jax.ShapeDtypeStruct((shards, double, hidden), BF),
            jax.ShapeDtypeStruct((8, depth), F32),
        ],
        scratch_shapes=[
            pltpu.VMEM((rows, depth), BF),
            pltpu.VMEM((rows, depth), BF),
            pltpu.VMEM((rows, depth), F32),
        ],
        compiler_params=params(),
        cost_estimate=pl.CostEstimate(
            flops=8 * rows * depth * hidden * shards * 2,
            bytes_accessed=35_000_000,
            transcendentals=0,
        ),
        name="feed_backward",
    )(grad, h, gain, bias, w, hid, slope)


def expert_pair(mine_ref, other_ref):
    first = lax.rem(lax.axis_index("ep"), 2) == 0
    mine, other = mine_ref[0], other_ref[0]
    return jnp.where(first, mine, other), jnp.where(first, other, mine)


def expert_forward_kernel(x_ref, mine_ref, other_ref, b1_ref, b2_ref, y_ref, hid_ref, slope_ref, acc_ref):
    r = pl.program_id(0)

    @pl.when(r == 0)
    def _():
        acc_ref[...] = jnp.zeros_like(acc_ref)

    w_in, w_out = expert_pair(mine_ref, other_ref)
    u = dot(x_ref[...], w_in, NN) + b1_ref[0]
    value, slope = gelu_parts(u)
    value = value.astype(BF)
    hid_ref[0] = value
    slope_ref[0] = slope.astype(BF)
    acc_ref[...] += dot(value, w_out, NN)

    @pl.when(r == pl.num_programs(0) - 1)
    def _():
        y_ref[...] = (acc_ref[...] + b2_ref[...]).astype(BF)


def expert_forward(x, mine, other, b1, b2):
    rows, depth = x.shape
    shards, _, hidden = mine.shape
    shard = lambda r: (r, 0, 0)
    wide = pl.BlockSpec((1, rows, hidden), shard)
    weight = pl.BlockSpec((1, depth, hidden), shard)
    return pl.pallas_call(
        expert_forward_kernel,
        grid=(shards,),
        in_specs=[whole(), weight, weight, pl.BlockSpec((1, 1, hidden), shard), whole()],
        out_specs=[whole(), wide, wide],
        out_shape=[
            jax.ShapeDtypeStruct((rows, depth), BF),
            jax.ShapeDtypeStruct((shards, rows, hidden), BF),
            jax.ShapeDtypeStruct((shards, rows, hidden), BF),
        ],
        scratch_shapes=[pltpu.VMEM((rows, depth), F32)],
        compiler_params=params(),
        cost_estimate=pl.CostEstimate(
            flops=4 * rows * depth * hidden * shards * 2,
            bytes_accessed=25_000_000,
            transcendentals=rows * hidden * shards,
        ),
        name="expert_forward",
    )(x, mine, other, b1, b2)


def expert_input_kernel(
    y_ref,
    cot_ref,
    gate_ref,
    mine_ref,
    other_ref,
    slope_ref,
    wy_ref,
    dy_ref,
    dx_ref,
    dgate_ref,
    du_ref,
    small_ref,
    acc_ref,
):
    r = pl.program_id(0)
    mine = lax.axis_index("tp")

    @pl.when(r == 0)
    def _():
        y = y_ref[...].astype(F32)
        cot = cot_ref[...].astype(F32)
        gate = gate_ref[...]
        dgate_ref[...] = jnp.sum(cot * y, axis=1, keepdims=True)
        wy_ref[...] = (gate * y).astype(BF)
        dy = (gate * cot).astype(BF)
        dy_ref[...] = dy
        small_ref[4:5, :] = jnp.sum(dy.astype(F32), axis=0, keepdims=True)
        small_ref[5:8, :] = jnp.zeros((3, dy.shape[1]), F32)
        acc_ref[...] = jnp.zeros_like(acc_ref)

    w_in, w_out = expert_pair(mine_ref, other_ref)
    dr = dot(dy_ref[...], w_out, NT)
    du = (slope_ref[0].astype(F32) * dr).astype(BF)
    du_ref[0] = du
    small_ref[pl.ds(mine ^ r, 1), :] = jnp.sum(du.astype(F32), axis=0, keepdims=True)
    acc_ref[...] += dot(du, w_in, NT)

    @pl.when(r == pl.num_programs(0) - 1)
    def _():
        dx_ref[...] = acc_ref[...].astype(BF)


def expert_input(y, cot, gate, mine, other, slope):
    rows, depth = y.shape
    shards, _, hidden = mine.shape
    shard = lambda r: (r, 0, 0)
    wide = pl.BlockSpec((1, rows, hidden), shard)
    weight = pl.BlockSpec((1, depth, hidden), shard)
    return pl.pallas_call(
        expert_input_kernel,
        grid=(shards,),
        in_specs=[whole(), whole(), whole(), weight, weight, wide],
        out_specs=[
            whole(),
            whole(),
            whole(),
            whole(),
            wide,
            whole(),
        ],
        out_shape=[
            jax.ShapeDtypeStruct((rows, depth), BF),
            jax.ShapeDtypeStruct((rows, depth), BF),
            jax.ShapeDtypeStruct((rows, depth), BF),
            jax.ShapeDtypeStruct((rows, 1), F32),
            jax.ShapeDtypeStruct((shards, rows, hidden), BF),
            jax.ShapeDtypeStruct((8, depth), F32),
        ],
        scratch_shapes=[pltpu.VMEM((rows, depth), F32)],
        compiler_params=params(),
        cost_estimate=pl.CostEstimate(
            flops=4 * rows * depth * hidden * shards * 2,
            bytes_accessed=25_000_000,
            transcendentals=0,
        ),
        name="expert_input",
    )(y, cot, gate, mine, other, slope)


def expert_return_kernel(
    size,
    x_ref,
    dy_ref,
    hid_ref,
    du_ref,
    sent_ref,
    dw_ref,
    out_ref,
    swap_send,
    swap_recv,
    pass_send,
    pass_recv,
    local_sem,
):
    step = pl.program_id(0)
    depth = x_ref.shape[1]
    mine = lax.axis_index("tp")
    place = lax.axis_index("ep")
    to_x = {"tp": mine ^ 1}
    to_y = {"tp": mine ^ 2}

    def remote(src, dst, sends, recvs, index, peer):
        return pltpu.make_async_remote_copy(
            src_ref=src,
            dst_ref=dst,
            send_sem=sends.at[index],
            recv_sem=recvs.at[index],
            device_id=peer,
            device_id_type=pl.DeviceIdType.MESH,
        )

    def exchange(k):
        peer = place ^ k
        return remote(
            sent_ref.at[peer], out_ref.at[0, place], swap_send, swap_recv, k, {"ep": peer}
        )

    def keep():
        return pltpu.make_async_copy(sent_ref.at[place], out_ref.at[0, place], local_sem)

    def along(k, way):
        slab = place ^ k
        return remote(
            out_ref.at[0, slab],
            out_ref.at[1 + way, slab],
            pass_send,
            pass_recv,
            (way, k),
            (to_x, to_y)[way],
        )

    def relay(k):
        slab = place ^ k
        way = k % 2
        return remote(
            out_ref.at[1 + way, slab],
            out_ref.at[3, slab],
            pass_send,
            pass_recv,
            (2, k),
            (to_y, to_x)[way],
        )

    def forward(group):
        for k in range(size // 4 * group, size // 4 * (group + 1)):
            if k == 0:
                keep().wait()
            else:
                exchange(k).wait_recv()
            along(k, 0).start()
            along(k, 1).start()

    @pl.when(step == 0)
    def _():
        barrier = pltpu.get_barrier_semaphore()
        for peer in [to_x, to_y] + [{"ep": place ^ k} for k in range(1, size)]:
            pl.semaphore_signal(barrier, inc=1, device_id=peer, device_id_type=pl.DeviceIdType.MESH)
        pl.semaphore_wait(barrier, size + 1)
        keep().start()
        for k in range(1, size):
            exchange(k).start()

    for group in range(3):

        @pl.when(step == group + 1)
        def _(group=group):
            forward(group)

    dw_ref[0, depth:, :] = dot(hid_ref[0], dy_ref[...], TN).astype(BF)
    dw_ref[0, :depth, :] = dot(x_ref[...], du_ref[0], TN).astype(BF)

    @pl.when(step == 3)
    def _():
        forward(3)
        for k in range(size):
            along(k, k % 2).wait_recv()
            relay(k).start()
        for k in range(size):
            along(k, 1 - k % 2).wait_recv()
            relay(k).wait_recv()
        for k in range(size):
            if k > 0:
                exchange(k).wait_send()
            along(k, 0).wait_send()
            along(k, 1).wait_send()
            relay(k).wait_send()


def expert_return(x, dy, hid, du, sent):
    rows, depth = x.shape
    shards, _, hidden = hid.shape
    size = sent.shape[0]
    shard = lambda r: (r, 0, 0)
    wide = pl.BlockSpec((1, rows, hidden), shard)
    any_spec = pl.BlockSpec(memory_space=pl.ANY)
    return pl.pallas_call(
        lambda *refs: expert_return_kernel(size, *refs),
        grid=(shards,),
        in_specs=[whole(), whole(), wide, wide, any_spec],
        out_specs=[pl.BlockSpec((1, 2 * depth, hidden), shard), any_spec],
        out_shape=[
            jax.ShapeDtypeStruct((shards, 2 * depth, hidden), BF),
            jax.ShapeDtypeStruct((shards,) + sent.shape, BF),
        ],
        scratch_shapes=[
            pltpu.SemaphoreType.DMA((size,)),
            pltpu.SemaphoreType.DMA((size,)),
            pltpu.SemaphoreType.DMA((3, size)),
            pltpu.SemaphoreType.DMA((3, size)),
            pltpu.SemaphoreType.DMA,
        ],
        compiler_params=pltpu.CompilerParams(
            dimension_semantics=("arbitrary",),
            vmem_limit_bytes=VMEM_LIMIT,
            collective_id=2,
            has_side_effects=True,
        ),
        cost_estimate=pl.CostEstimate(
            flops=4 * rows * depth * hidden * shards * 2,
            bytes_accessed=40_000_000,
            transcendentals=0,
        ),
        name="expert_return",
    )(x, dy, hid, du, sent)


ROUTES = 6


def attend_image(x, gain, bias, w_ref, biases_ref, bias_row, bout, qkv_ref, lse_ref, ctx_ref):
    shards = w_ref.shape[0]
    width = w_ref.shape[1] // 4
    heads = width // HEAD
    hat, _ = norm_parts(x)
    a = (hat * gain + bias).astype(BF)
    mask = key_mask()
    branch = jnp.zeros(x.shape, F32)
    for r in range(shards):
        column = jnp.transpose(biases_ref[r])[: 3 * width, bias_row : bias_row + 1]
        qkv = (dot(w_ref[r, : 3 * width, :], a, NT) + column).astype(BF)
        qkv_ref[0, r] = qkv
        for h in range(heads):
            q = qkv[HEAD * h : HEAD * (h + 1)]
            k = qkv[width + HEAD * h : width + HEAD * (h + 1)]
            v = qkv[2 * width + HEAD * h : 2 * width + HEAD * (h + 1)]
            s = dot(k, q, TN) * (HEAD**-0.5) + mask
            peak = jnp.max(s, axis=0, keepdims=True)
            e = jnp.exp(s - peak)
            total = jnp.sum(e, axis=0, keepdims=True)
            lse_ref[0, r, h : h + 1, :] = peak + jnp.log(total)
            c = dot(v, e.astype(BF), NN) * (1.0 / total)
            ctx_ref[0, r, HEAD * h : HEAD * (h + 1), :] = c.astype(BF)
        branch += dot(ctx_ref[0, r], w_ref[r, 3 * width :, :], TN)
    return x + branch + bout


def forward_kernel(
    x_ref,
    vec_ref,
    bias_ref,
    one_ref,
    feed_ref,
    two_ref,
    h1_ref,
    h2_ref,
    h3_ref,
    qkv1_ref,
    lse1_ref,
    ctx1_ref,
    hid_ref,
    slope_ref,
    qkv2_ref,
    lse2_ref,
    ctx2_ref,
    w1_out,
    wf_out,
    w2_out,
    normed_out,
    biases_out,
    h_ref,
    w1_ref,
    wf_ref,
    w2_ref,
    b_ref,
    n_ref,
    send_sem,
    recv_sem,
    n_send,
    n_recv,
    small_send,
    small_recv,
    local_sem,
):
    step = pl.program_id(0)
    images = 4
    mine = lax.axis_index("tp")
    place = lax.axis_index("ep")
    core = lax.rem(place, 2)
    side = lax.rem(mine, 2)
    to_x = {"tp": mine ^ 1}
    to_y = {"tp": mine ^ 2}
    to_far = {"tp": mine ^ 3}
    to_core = {"ep": place ^ 1}
    depth = x_ref.shape[1]

    def remote(src, dst, sends, recvs, index, peer):
        return pltpu.make_async_remote_copy(
            src_ref=src,
            dst_ref=dst,
            send_sem=sends.at[index],
            recv_sem=recvs.at[index],
            device_id=peer,
            device_id_type=pl.DeviceIdType.MESH,
        )

    def copies(group, own, full):
        rows = own.shape[0] // 2
        start = pl.multiple_of(core * rows, rows)
        quarter = rows // 2
        middle = pl.multiple_of(start + quarter, quarter)
        half = pl.ds(start, rows)
        low = pl.ds(start, quarter)
        high = pl.ds(middle, quarter)

        def make(k, src, dst, peer):
            return remote(src, dst, send_sem, recv_sem, (group, k), peer)

        return [
            make(0, own.at[half], full.at[1, half], to_x),
            make(1, own.at[half], full.at[2, half], to_y),
            make(2, full.at[1, low], full.at[3, low], to_y),
            make(3, full.at[2, high], full.at[3, high], to_x),
            make(4, full.at[pl.ds(1, 2), half], full.at[pl.ds(1, 2), half], to_core),
            make(5, full.at[3, half], full.at[3, half], to_core),
        ]

    one = copies(0, one_ref, w1_ref)
    feed = copies(1, feed_ref, wf_ref)
    two = copies(2, two_ref, w2_ref)

    small = [
        remote(bias_ref, b_ref.at[r], small_send, small_recv, r - 1, peer)
        for r, peer in ((1, to_x), (2, to_y), (3, to_far))
    ]
    own_local = [
        pltpu.make_async_copy(one_ref, w1_ref.at[0], local_sem.at[0]),
        pltpu.make_async_copy(feed_ref, wf_ref.at[0], local_sem.at[1]),
        pltpu.make_async_copy(two_ref, w2_ref.at[0], local_sem.at[2]),
    ]
    saves = [
        pltpu.make_async_copy(w1_ref, w1_out, local_sem.at[4]),
        pltpu.make_async_copy(wf_ref, wf_out, local_sem.at[5]),
        pltpu.make_async_copy(w2_ref, w2_out, local_sem.at[6]),
    ]

    def rows_copy(i):
        rows = pl.ds(PAD * i, PAD)
        low, high = pl.ds(PAD * i, 96), pl.ds(PAD * i + 96, PAD - 96)
        return [
            remote(n_ref.at[i], normed_out.at[1, rows], n_send, n_recv, (0, i), to_x),
            remote(n_ref.at[i], normed_out.at[2, rows], n_send, n_recv, (1, i), to_y),
            remote(normed_out.at[1, low], normed_out.at[3, low], n_send, n_recv, (2, i), to_y),
            remote(normed_out.at[2, high], normed_out.at[3, high], n_send, n_recv, (3, i), to_x),
            pltpu.make_async_copy(n_ref.at[i], normed_out.at[0, rows], local_sem.at[8 + i]),
        ]

    def vec(k):
        return vec_ref[k : k + 1, :]

    @pl.when(step == 0)
    def _():
        barrier = pltpu.get_barrier_semaphore()
        for peer in (to_x, to_y, to_far, to_core):
            pl.semaphore_signal(barrier, inc=1, device_id=peer, device_id_type=pl.DeviceIdType.MESH)
        pl.semaphore_wait(barrier, 4)
        one[0].start()
        one[1].start()
        own_local[0].start()
        for copy in small:
            copy.start()
        b_ref[0] = bias_ref[...]
        one[0].wait_recv()
        one[1].wait_recv()
        one[2].start()
        one[3].start()
        one[4].start()
        one[2].wait_recv()
        one[3].wait_recv()
        one[5].start()
        feed[0].start()
        feed[1].start()
        own_local[1].start()
        own_local[2].start()
        own_local[0].wait()
        for copy in small:
            copy.wait_recv()
        one[4].wait_recv()
        one[5].wait_recv()

    @pl.when(step == 2)
    def _():
        saves[0].start()
        feed[0].wait_recv()
        feed[1].wait_recv()
        feed[2].start()
        feed[3].start()
        feed[4].start()

    @pl.when(step == 4)
    def _():
        feed[2].wait_recv()
        feed[3].wait_recv()
        feed[5].start()
        two[0].start()
        two[1].start()
        own_local[1].wait()
        feed[4].wait_recv()
        feed[5].wait_recv()

    @pl.when(step == 6)
    def _():
        saves[1].start()
        two[0].wait_recv()
        two[1].wait_recv()
        two[2].start()
        two[3].start()
        two[4].start()

    @pl.when(step == 7)
    def _():
        two[2].wait_recv()
        two[3].wait_recv()
        two[5].start()

    @pl.when(step == 8)
    def _():
        own_local[2].wait()
        two[4].wait_recv()
        two[5].wait_recv()

    @pl.when(step == 10)
    def _():
        saves[2].start()

    @pl.when(step < images)
    def _():
        x = x_ref[pl.ds(pl.multiple_of(step * PAD, PAD), PAD), :].astype(F32)
        h = attend_image(
            x, vec(0), vec(1), w1_ref, b_ref, 0, vec(2), qkv1_ref, lse1_ref, ctx1_ref
        )
        h_ref[step] = h
        h1_ref[...] = h

    @pl.when((step >= images) & (step < 2 * images))
    def _():
        tile = step - images
        x = h_ref[tile]
        hat, _ = norm_parts(x)
        m = (hat * vec(3) + vec(4)).astype(BF)
        acc = x + vec(5)
        for r in range(wf_ref.shape[0]):
            u = dot(m, wf_ref[r, :depth, :], NN) + b_ref[r, 2:3, :]
            value, slope = gelu_parts(u)
            value = value.astype(BF)
            hid_ref[r] = value
            slope_ref[r] = slope.astype(BF)
            acc += dot(value, wf_ref[r, depth:, :], NN)
        h_ref[tile] = acc
        h2_ref[...] = acc

    @pl.when(step >= 2 * images)
    def _():
        image = step - 2 * images
        h = attend_image(
            h_ref[image], vec(6), vec(7), w2_ref, b_ref, 1, vec(8), qkv2_ref, lse2_ref, ctx2_ref
        )
        h3_ref[...] = h
        hat, _ = norm_parts(h)
        n_ref[image] = (hat * vec(9) + vec(10)).astype(BF)

    for i in range(images):

        @pl.when(step == 2 * images + i)
        def _(i=i):
            to_send = rows_copy(i)
            to_send[0].start()
            to_send[1].start()
            to_send[4].start()
            if i > 0:
                before = rows_copy(i - 1)
                before[0].wait_recv()
                before[1].wait_recv()
                before[2].start()
                before[3].start()

    @pl.when(step == 3 * images - 1)
    def _():
        last = rows_copy(images - 1)
        last[0].wait_recv()
        last[1].wait_recv()
        last[2].start()
        last[3].start()
        pltpu.make_async_copy(b_ref, biases_out, local_sem.at[7]).start()
        for i in range(images):
            moved = rows_copy(i)
            moved[2].wait_recv()
            moved[3].wait_recv()
            for k in range(4):
                moved[k].wait_send()
            moved[4].wait()
        for group in (one, feed, two):
            for copy in group:
                copy.wait_send()
        for copy in small:
            copy.wait_send()
        for copy in saves:
            copy.wait()
        pltpu.make_async_copy(b_ref, biases_out, local_sem.at[7]).wait()


def dense_forward(x, vectors, bias, pack_one, pack_feed, pack_two):
    rows, depth = x.shape
    images = rows // PAD
    shards = 4
    four = pack_one.shape[0]
    width = four // 4
    heads = width // HEAD
    double, hidden = pack_feed.shape
    any_spec = pl.BlockSpec(memory_space=pl.ANY)

    def part(number):
        return lambda s: jnp.clip(s - images * number, 0, images - 1)

    def row_spec(number):
        at = part(number)
        return pl.BlockSpec((PAD, depth), lambda s: (at(s), 0))

    def attend_specs(number):
        at = part(number)
        return [
            pl.BlockSpec((1, shards, 3 * width, PAD), lambda s: (at(s), 0, 0, 0)),
            pl.BlockSpec((1, shards, heads, PAD), lambda s: (at(s), 0, 0, 0)),
            pl.BlockSpec((1, shards, width, PAD), lambda s: (at(s), 0, 0, 0)),
        ]

    tile_at = part(1)
    hid_spec = pl.BlockSpec((shards, PAD, hidden), lambda s: (0, tile_at(s), 0))
    shape = jax.ShapeDtypeStruct
    attend_shapes = [
        shape((images, shards, 3 * width, PAD), BF),
        shape((images, shards, heads, PAD), F32),
        shape((images, shards, width, PAD), BF),
    ]
    out = pl.pallas_call(
        forward_kernel,
        grid=(3 * images,),
        in_specs=[whole(), whole(), whole()] + [any_spec] * 3,
        out_specs=[row_spec(0), row_spec(1), row_spec(2)]
        + attend_specs(0)
        + [hid_spec, hid_spec]
        + attend_specs(2)
        + [any_spec] * 5,
        out_shape=[shape((rows, depth), F32)] * 3
        + attend_shapes
        + [shape((shards, rows, hidden), BF)] * 2
        + attend_shapes
        + [
            shape((shards, four, depth), BF),
            shape((shards, double, hidden), BF),
            shape((shards, four, depth), BF),
            shape((shards, rows, depth), BF),
            shape((shards, 8, depth), F32),
        ],
        scratch_shapes=[
            pltpu.VMEM((images, PAD, depth), F32),
            pltpu.VMEM((shards, four, depth), BF),
            pltpu.VMEM((shards, double, hidden), BF),
            pltpu.VMEM((shards, four, depth), BF),
            pltpu.VMEM((shards, 8, depth), F32),
            pltpu.VMEM((images, PAD, depth), BF),
            pltpu.SemaphoreType.DMA((3, ROUTES)),
            pltpu.SemaphoreType.DMA((3, ROUTES)),
            pltpu.SemaphoreType.DMA((4, 4)),
            pltpu.SemaphoreType.DMA((4, 4)),
            pltpu.SemaphoreType.DMA((3,)),
            pltpu.SemaphoreType.DMA((3,)),
            pltpu.SemaphoreType.DMA((12,)),
        ],
        compiler_params=pltpu.CompilerParams(
            dimension_semantics=("arbitrary",),
            vmem_limit_bytes=VMEM_LIMIT,
            collective_id=0,
            has_side_effects=True,
        ),
        cost_estimate=pl.CostEstimate(
            flops=60_000_000_000, bytes_accessed=60_000_000, transcendentals=10_000_000
        ),
        name="dense_forward",
    )(x, vectors, bias, pack_one, pack_feed, pack_two)
    (h1, h2, h3, q1, l1, c1, hid, slope, q2, l2, c2, w1, wf, w2, normed, biases) = out
    return (h1, h2, h3), (q1, l1, c1), (hid, slope), (q2, l2, c2), (w1, wf, w2), normed, biases


TAIL_ORDER = (0, 1, 2, 3, 0, 1, 0, 2, 0, 1, 3, 0, 1, 2, 4, 0, 3, 1, 2, 0, 3, 1, 2, 4, 0, 3, 1, 2, 4)


def add_rows(dst, src, rows):
    tile = 48

    def body(i, carry):
        at = pl.ds(pl.multiple_of(i * tile, 16), tile)
        dst[at] = (dst[at].astype(F32) + src[at].astype(F32)).astype(BF)
        return carry

    lax.fori_loop(0, rows // tile, body, 0)


def plane_bits(size):
    return [1 << k for k in range(1, size.bit_length() - 1)]


def halvings(rows, bits):
    count = 0
    while count < len(bits) and rows % 32 == 0:
        rows //= 2
        count += 1
    return count


def tail_kernel(size, rows_list, *refs):
    groups = len(rows_list)
    bits = plane_bits(size)
    take = iter(refs)
    sources = [next(take) for _ in range(groups)]
    ig_ref, act_x, act_y, small_ref = [next(take) for _ in range(4)]
    outs = [next(take) for _ in range(groups)]
    ig_out, act_out, total_ref, pair_ref = [next(take) for _ in range(4)]
    keeps = [next(take) for _ in range(groups)]
    cores = [next(take) for _ in range(groups)]
    firsts = [next(take) for _ in range(groups)]
    seconds = [next(take) for _ in range(groups)]
    planes = [next(take) for _ in range(groups)]
    halves = [next(take) for _ in range(groups)]
    landed = next(take)
    send_sem, recv_sem, local_sem, ig_send, ig_recv, small_send, small_recv = take

    mine = lax.axis_index("tp")
    place = lax.axis_index("ep")
    core = lax.rem(place, 2)
    to_x = {"tp": mine ^ 1}
    to_y = {"tp": mine ^ 2}
    to_core = {"ep": place ^ 1}
    to_plane = [{"ep": place ^ bit} for bit in bits]

    barrier = pltpu.get_barrier_semaphore()
    for peer in [to_x, to_y, to_core] + to_plane:
        pl.semaphore_signal(barrier, inc=1, device_id=peer, device_id_type=pl.DeviceIdType.MESH)
    pl.semaphore_wait(barrier, 3 + len(bits))

    def remote(src, dst, sends, recvs, index, peer):
        return pltpu.make_async_remote_copy(
            src_ref=src,
            dst_ref=dst,
            send_sem=sends.at[index],
            recv_sem=recvs.at[index],
            device_id=peer,
            device_id_type=pl.DeviceIdType.MESH,
        )

    def group_steps(g):
        rows = rows_list[g]
        half, quarter = rows // 2, rows // 4
        source, keep, came, first, second = sources[g], keeps[g], cores[g], firsts[g], seconds[g]
        plane, out, whole_half = planes[g], outs[g], halves[g]
        own_half = pl.ds(pl.multiple_of(core * half, half), half)
        other_half = pl.ds(pl.multiple_of((1 - core) * half, half), half)
        number = iter(range(100))
        sent = []

        def send(src, dst, peer):
            copy = remote(src, dst, send_sem, recv_sem, (g, next(number)), peer)
            copy.start()
            sent.append(copy)
            return copy

        every = pl.ds(0, keep.shape[0])
        local = pltpu.make_async_copy(source.at[every, own_half], keep, local_sem.at[g])
        local.start()
        swap = send(source.at[every, other_half], came, to_core)
        yield
        local.wait()
        swap.wait_recv()
        for r in range(keep.shape[0]):
            add_rows(keep.at[r], came.at[r], half)
        low, high = pl.ds(0, quarter), pl.ds(quarter, quarter)
        waits = [
            send(keep.at[1, low], first.at[0], to_x),
            send(keep.at[3, low], first.at[1], to_x),
            send(keep.at[pl.ds(2, 2), high], first.at[pl.ds(2, 2)], to_y),
        ]
        yield
        for copy in waits:
            copy.wait_recv()
        add_rows(keep.at[2, low], first.at[1], quarter)
        add_rows(keep.at[1, high], first.at[3], quarter)
        waits = [
            send(keep.at[2, low], second.at[0], to_y),
            send(keep.at[1, high], second.at[1], to_x),
        ]
        add_rows(keep.at[0, low], first.at[0], quarter)
        add_rows(keep.at[0, high], first.at[2], quarter)
        yield
        for copy in waits:
            copy.wait_recv()
        add_rows(keep.at[0, low], second.at[0], quarter)
        add_rows(keep.at[0, high], second.at[1], quarter)
        start, length, done = 0, half, []
        offset = 0
        for k, bit in enumerate(bits):
            if k < halvings(half, bits):
                length //= 2
                side = lax.rem(place // bit, 2)
                mine_at = pl.ds(pl.multiple_of(start + side * length, 16), length)
                give_at = pl.ds(pl.multiple_of(start + (1 - side) * length, 16), length)
                land = plane.at[pl.ds(offset, length)]
                copy = send(keep.at[0, give_at], land, to_plane[k])
                done.append((mine_at, k))
                start = start + side * length
            else:
                mine_at = pl.ds(pl.multiple_of(start + 0 * place, 16), length)
                land = plane.at[pl.ds(offset, length)]
                copy = send(keep.at[0, mine_at], land, to_plane[k])
            yield
            copy.wait_recv()
            if k >= halvings(half, bits):
                copy.wait_send()
                sent.pop()
            add_rows(keep.at[0, mine_at], land, length)
            offset += length
        at = done[-1][0]
        whole_half[at] = keep[0, at, :]
        for at, k in done[::-1]:
            copy = send(whole_half.at[at], whole_half.at[at], to_plane[k])
            yield
            copy.wait_recv()
        copy = send(whole_half, out.at[own_half], to_core)
        local = pltpu.make_async_copy(whole_half, out.at[own_half], local_sem.at[groups + g])
        local.start()
        yield
        copy.wait_recv()
        local.wait()
        for copy in sent:
            copy.wait_send()

    def ig_steps():
        half = ig_ref.shape[0] // 32 * 16
        low, high = pl.ds(0, half), pl.ds(half, ig_ref.shape[0] - half)
        near = [
            remote(ig_ref, ig_out.at[mine], ig_send, ig_recv, 0, to_x),
            remote(ig_ref, ig_out.at[mine], ig_send, ig_recv, 1, to_y),
        ]
        local = pltpu.make_async_copy(ig_ref, ig_out.at[mine], local_sem.at[2 * groups])
        local.start()
        for copy in near:
            copy.start()
        yield
        passed = [
            remote(act_x.at[low], act_out.at[low], ig_send, ig_recv, 4, to_y),
            remote(act_y.at[high], act_out.at[high], ig_send, ig_recv, 5, to_x),
        ]
        for copy in passed:
            copy.start()
        for copy in near:
            copy.wait_recv()
        relay = [
            remote(ig_out.at[mine ^ 1, low], ig_out.at[mine ^ 1, low], ig_send, ig_recv, 2, to_y),
            remote(ig_out.at[mine ^ 2, high], ig_out.at[mine ^ 2, high], ig_send, ig_recv, 3, to_x),
        ]
        for copy in relay:
            copy.start()
        yield
        for copy in relay:
            copy.wait_recv()
        for copy in passed:
            copy.wait_recv()
        for copy in near + relay + passed:
            copy.wait_send()
        local.wait()

    def small_steps():
        total_ref[...] = small_ref[...]
        peers = [to_x, to_y, to_core] + to_plane
        for k, peer in enumerate(peers):
            copy = remote(total_ref, landed.at[k], small_send, small_recv, k, peer)
            copy.start()
            yield
            copy.wait()
            total_ref[...] += landed[k]
            if k == 2:
                pair_ref[...] = total_ref[...]

    running = [group_steps(g) for g in range(groups)] + [small_steps(), ig_steps()]
    ended = set()

    def advance(which):
        if which not in ended:
            try:
                next(running[which])
            except StopIteration:
                ended.add(which)

    for which in TAIL_ORDER:
        advance(which)
    while len(ended) < len(running):
        for which in range(len(running)):
            advance(which)


def tail(grads, ig, act_x, act_y, small, size):
    shards, _, depth = grads[0].shape
    rows_list = [g.shape[1] for g in grads]
    groups = len(grads)
    bits = plane_bits(size)
    any_spec = pl.BlockSpec(memory_space=pl.ANY)
    shape = jax.ShapeDtypeStruct

    def plane_rows(rows):
        half, total = rows // 2, 0
        for k in range(len(bits)):
            if k < halvings(rows // 2, bits):
                half //= 2
            total += half
        return total

    copies = 4 + 2 + 2 * len(bits) + 1
    return pl.pallas_call(
        lambda *refs: tail_kernel(size, rows_list, *refs),
        in_specs=[any_spec] * (groups + 3) + [whole()],
        out_specs=[any_spec] * (groups + 2) + [whole(), whole()],
        out_shape=[shape((rows, depth), BF) for rows in rows_list]
        + [shape((shards,) + ig.shape, BF), shape(ig.shape, BF), shape(small.shape, F32), shape(small.shape, F32)],
        scratch_shapes=[pltpu.VMEM((shards, rows // 2, depth), BF) for rows in rows_list]
        + [pltpu.VMEM((shards, rows // 2, depth), BF) for rows in rows_list]
        + [pltpu.VMEM((4, rows // 4, depth), BF) for rows in rows_list]
        + [pltpu.VMEM((2, rows // 4, depth), BF) for rows in rows_list]
        + [pltpu.VMEM((plane_rows(rows), depth), BF) for rows in rows_list]
        + [pltpu.VMEM((rows // 2, depth), BF) for rows in rows_list]
        + [
            pltpu.VMEM((3 + len(bits),) + small.shape, F32),
            pltpu.SemaphoreType.DMA((groups, copies)),
            pltpu.SemaphoreType.DMA((groups, copies)),
            pltpu.SemaphoreType.DMA((2 * groups + 1,)),
            pltpu.SemaphoreType.DMA((6,)),
            pltpu.SemaphoreType.DMA((6,)),
            pltpu.SemaphoreType.DMA((3 + len(bits),)),
            pltpu.SemaphoreType.DMA((3 + len(bits),)),
        ],
        compiler_params=pltpu.CompilerParams(
            vmem_limit_bytes=VMEM_LIMIT, collective_id=1, has_side_effects=True
        ),
        cost_estimate=pl.CostEstimate(flops=30_000_000, bytes_accessed=60_000_000, transcendentals=0),
        name="tail",
    )(*grads, ig, act_x, act_y, small)


def hop(value, axis, bit):
    size = lax.axis_size(axis)
    return lax.ppermute(value, axis, [(i, i ^ bit) for i in range(size)])


def after(value, *deps):
    return lax.optimization_barrier((value, deps))[0]


def near(value):
    return hop(value, "tp", 1), hop(value, "tp", 2)


def far(from_x, from_y):
    half = from_x.shape[0] // 2
    low = hop(from_x[:half], "tp", 2)
    high = hop(from_y[half:], "tp", 1)
    return jnp.concatenate([low, high])


def gather_tp_small(value):
    return jnp.stack([value, hop(value, "tp", 1), hop(value, "tp", 2), hop(value, "tp", 3)])


def take_half(value, which, axis=0):
    half = value.shape[axis] // 2
    return lax.dynamic_slice_in_dim(value, which * half, half, axis=axis)


def join_halves(value, other, which, axis=0):
    half = value.shape[axis]
    three = jnp.concatenate([value, other, value], axis=axis)
    return lax.dynamic_slice_in_dim(three, which * half, 2 * half, axis=axis)


def plus(a, b):
    return (a.astype(F32) + b.astype(F32)).astype(BF)


def core_sum(value):
    core = lax.axis_index("ep") % 2
    return plus(take_half(value, core, 1), hop(take_half(value, 1 - core, 1), "ep", 1))


def swap_ep(value):
    return lax.all_to_all(value, "ep", split_axis=0, concat_axis=0, tiled=True)


def route_kernel(order_ref, index_ref, hot_ref, out_ref, rank_ref):
    rows = order_ref.shape[1]
    tile = rows // 7
    half = hot_ref.shape[1] // 2
    for i in range(7):
        ids = lax.broadcasted_iota(jnp.int32, (tile, 1), 0) + tile * i
        match = jnp.where(order_ref[...] == ids, 1.0, 0.0).astype(BF)
        rank_ref[tile * i : tile * (i + 1), :] = dot(match, index_ref[...], NN)
    parts = rank_ref[...]
    rank = parts[:, 0:1] * 64.0 + parts[:, 1:2]
    rank_row = jnp.transpose(jnp.broadcast_to(rank, parts.shape))[0:1, :]
    hot = hot_ref[...]
    total = jnp.sum(hot.astype(F32), axis=0, keepdims=True)
    lanes = lax.broadcasted_iota(jnp.int32, (1, 2 * half), 1)
    firsts = jnp.where(lanes < half, total, 0.0)
    firsts = jnp.concatenate([jnp.zeros((1, half), F32), firsts[:, :half]], axis=1)
    for i in range(7):
        at = slice(tile * i, tile * (i + 1))
        earlier = jnp.where(rank_row < rank[at], 1.0, 0.0).astype(BF)
        count = dot(earlier, hot, NN) + firsts
        picked = count * hot[at].astype(F32)
        first = jnp.sum(jnp.where(lanes < half, picked, 0.0), axis=1, keepdims=True)
        second = jnp.sum(jnp.where(lanes < half, 0.0, picked), axis=1, keepdims=True)
        out_ref[at, :] = jnp.where(lanes == 0, first, second)


def route(picks, order):
    rows = picks.shape[0]
    half = 64
    ids = jnp.arange(half, dtype=jnp.int32)[None, :]
    hot = jnp.concatenate([picks[:, 0:1] == ids, picks[:, 1:2] == ids], axis=1).astype(BF)
    line = jnp.arange(rows, dtype=jnp.int32)[:, None]
    column = jnp.arange(2 * half, dtype=jnp.int32)[None, :]
    index = jnp.where(column == 0, line // 64, jnp.where(column == 1, line % 64, 0)).astype(BF)
    out = pl.pallas_call(
        route_kernel,
        in_specs=[whole(), whole(), whole()],
        out_specs=whole(),
        out_shape=jax.ShapeDtypeStruct((rows, 2 * half), F32),
        scratch_shapes=[pltpu.VMEM((rows, 2 * half), F32)],
        compiler_params=pltpu.CompilerParams(vmem_limit_bytes=VMEM_LIMIT),
        cost_estimate=pl.CostEstimate(
            flops=4 * rows * rows * 128, bytes_accessed=4_000_000, transcendentals=0
        ),
        name="route",
    )(order.reshape(1, rows), index, hot)
    return out[:, :2].astype(jnp.int32)


def body(
    tokens,
    cotangent,
    picks,
    priority,
    router_noise,
    dense_norm_gain,
    dense_norm_bias,
    dense_attend_in,
    dense_attend_bias,
    dense_attend_out,
    dense_attend_out_bias,
    feed_norm_gain,
    feed_norm_bias,
    feed_in,
    feed_in_bias,
    feed_out,
    feed_out_bias,
    sparse_norm_gain,
    sparse_norm_bias,
    sparse_attend_in,
    sparse_attend_bias,
    sparse_attend_out,
    sparse_attend_out_bias,
    route_norm_gain,
    route_norm_bias,
    router,
    expert_in,
    expert_in_bias,
    expert_out,
    expert_out_bias,
):
    shards = lax.axis_size("tp")
    experts = lax.axis_size("ep")
    mine = lax.axis_index("tp")
    rows_dev, depth = tokens.shape
    own = rows_dev // shards
    images = own // LEN
    own_pad = images * PAD
    capacity = rows_dev // experts
    part = -(-capacity // (8 * shards)) * 8
    width = dense_attend_bias.shape[1]
    hidden = feed_in_bias.shape[0]

    def pad_images(value):
        blocks = value.reshape(-1, LEN, value.shape[-1])
        return jnp.pad(blocks, ((0, 0), (0, PAD - LEN), (0, 0))).reshape(-1, value.shape[-1])

    def drop_pad(value):
        return value.reshape(images, PAD, depth)[:, :LEN].reshape(own, depth)

    def own_rows(value):
        return lax.dynamic_slice_in_dim(value, mine * own, own, axis=0)

    def by_index(value):
        return jnp.stack(
            [
                lax.dynamic_index_in_dim(value, mine ^ r, axis=0, keepdims=False)
                for r in range(shards)
            ]
        )

    def row(value):
        return value.reshape(1, -1)

    def attend_pack(proj_in, proj_out):
        return jnp.concatenate([proj_in.transpose(1, 2, 0).reshape(3 * width, depth), proj_out])

    pair_side = lax.axis_index("ep") % 2
    chip_side = mine % 2
    same = pair_side == chip_side
    keep_exp = jnp.where(pair_side == 0, expert_in[0], expert_out[0])
    give_exp = jnp.where(pair_side == 0, expert_out[0], expert_in[0])
    vectors = jnp.stack(
        [
            dense_norm_gain,
            dense_norm_bias,
            dense_attend_out_bias,
            feed_norm_gain,
            feed_norm_bias,
            feed_out_bias,
            sparse_norm_gain,
            sparse_norm_bias,
            sparse_attend_out_bias,
            route_norm_gain,
            route_norm_bias,
        ]
    )
    vectors = jnp.pad(vectors, ((0, 5), (0, 0)))

    def bias_line(value):
        gap = jnp.zeros((width,), F32)
        return jnp.concatenate([value[0], gap, value[1], jnp.zeros((depth - 3 * width,), F32)])

    own_biases = jnp.stack(
        [
            bias_line(dense_attend_bias),
            bias_line(sparse_attend_bias),
            feed_in_bias,
            expert_in_bias[0],
            expert_out_bias[0],
        ]
    )
    own_biases = jnp.pad(own_biases, ((0, 3), (0, 0)))
    swapped = hop(give_exp, "ep", 1)
    home_exp = jnp.where(same, keep_exp, swapped)
    away_exp = jnp.where(same, swapped, keep_exp)
    level_zero = after(pad_images(own_rows(tokens)), home_exp, away_exp)
    (level_one, level_two, level_three), kept_one, kept_feed, kept_two, gathered, normed, biases = (
        dense_forward(
            level_zero,
            vectors,
            own_biases,
            attend_pack(dense_attend_in, dense_attend_out),
            jnp.concatenate([feed_in, feed_out]),
            attend_pack(sparse_attend_in, sparse_attend_out),
        )
    )
    w_one, w_feed, w_two = gathered
    level_zero = level_zero.astype(F32)
    exp_small = biases[:, 3:5]
    exp_small = jnp.where(same, exp_small, hop(exp_small, "ep", 1))
    b_exp = exp_small[:, 0:1]
    b_exp_out = exp_small[0, 1:2]

    home_exp = after(home_exp, normed)
    away_exp = after(away_exp, normed)
    exp_x = hop(away_exp, "tp", 1)
    exp_far = hop(away_exp, "tp", 3)
    exp_y = hop(home_exp, "tp", 2)
    other_home = hop(home_exp, "ep", 1)

    position = route(after(picks, normed), priority[0])
    targets = jnp.where(position < capacity, picks * (part * shards) + position, -1).T
    slots = jnp.arange(experts * part, dtype=jnp.int32)

    def slots_of(index):
        block, inside = slots // part, slots % part
        expert = 2 * (block // 2) + index % 2
        quarter = 2 * (index // 2) + block % 2
        return expert * (part * shards) + quarter * part + inside

    slot_ids = slots_of(mine)
    pad_targets = jnp.pad(
        targets.reshape(2, -1, LEN), ((0, 0), (0, 0), (0, PAD - LEN)), constant_values=-1
    ).reshape(2, -1)
    near_targets = jnp.concatenate(
        [
            lax.dynamic_slice_in_dim(pad_targets, (mine ^ r) * own_pad, own_pad, axis=1)
            for r in range(shards)
        ],
        axis=1,
    )
    noise_pad = pad_images(router_noise)
    all_slots = jnp.concatenate([slots_of(mine ^ r) for r in range(shards)])
    own_targets = near_targets[:, :own_pad].T
    back_hot = (own_targets[:, 0:1] == all_slots[None, :]) | (
        own_targets[:, 1:2] == all_slots[None, :]
    )
    back_hot_bf = back_hot.astype(BF)

    all_normed = normed.reshape(shards * own_pad, depth)
    route_normed = normed[0]
    noise = jnp.concatenate(
        [
            lax.dynamic_slice_in_dim(noise_pad, (mine ^ r) * own_pad, own_pad, axis=0)
            for r in range(shards)
        ]
    )
    logits = dot(all_normed, router, NN) + noise
    gates = jax.nn.softmax(logits, axis=-1)
    own_hot = (slot_ids[:, None] == near_targets[0][None, :]) | (
        slot_ids[:, None] == near_targets[1][None, :]
    )
    side_gates = lax.dynamic_index_in_dim(
        gates.T.reshape(experts // 2, 2, -1), chip_side, axis=1, keepdims=False
    )
    hot_gates = own_hot.reshape(experts // 2, 2 * part, -1).astype(F32) * side_gates[:, None, :]
    slot_gate = jnp.sum(hot_gates, axis=2).reshape(-1, 1)

    def two_parts(value):
        high = lax.reduce_precision(value, 8, 7)
        rest = jnp.zeros((value.shape[0], 126), BF)
        return jnp.concatenate([high.astype(BF), (value - high).astype(BF), rest], axis=1)

    def swap_rows(value):
        wide = value.shape[-1]
        return swap_ep(value.reshape(experts, part, wide)).reshape(experts * part, wide)

    rows = dot(own_hot.astype(BF), all_normed, NN).astype(BF)
    arrived = swap_rows(jnp.concatenate([rows, two_parts(slot_gate)], axis=1))
    cot_hot = (slot_ids[:, None] == targets[0][None, :]) | (slot_ids[:, None] == targets[1][None, :])
    cot_sent = dot(after(cot_hot.astype(BF), rows), cotangent, NN).astype(BF)
    cot_rows = swap_rows(cot_sent)
    exp_x, exp_y, exp_far = after((exp_x, exp_y, exp_far), cot_sent)
    exp_mine = jnp.stack([home_exp, exp_x, exp_y, exp_far])
    exp_other = jnp.stack(
        [other_home, hop(exp_x, "ep", 1), hop(exp_y, "ep", 1), hop(exp_far, "ep", 1)]
    )
    inputs = arrived[:, :depth]
    gate_in = arrived[:, depth : depth + 2].astype(F32)
    gate_in = gate_in[:, 0:1] + gate_in[:, 1:2]
    outputs, exp_hidden, exp_slope = expert_forward(inputs, exp_mine, exp_other, b_exp, b_exp_out)
    weighted, grad_outputs, grad_inputs, slot_dot, exp_du, small_exp = (
        expert_input(outputs, cot_rows, gate_in, exp_mine, exp_other, exp_slope)
    )
    sent = jnp.concatenate([grad_inputs, two_parts(slot_dot)], axis=1)
    g_exp, grad_slots = expert_return(
        inputs, grad_outputs, exp_hidden, exp_du, sent.reshape(experts, part, sent.shape[1])
    )
    grad_slots = grad_slots.reshape(shards * experts * part, sent.shape[1])
    part_exp = core_sum(g_exp)
    exp_from_y = hop(part_exp[3], "tp", 2)
    dot_slots = grad_slots[:, depth : depth + 2].astype(F32)
    dot_slots = dot_slots[:, 0] + dot_slots[:, 1]
    weighted = swap_rows(after(weighted, grad_slots))
    grad_slots = grad_slots[:, :depth]

    grad_stream = pad_images(own_rows(cotangent)).astype(F32)
    own_gates = gates[:own_pad]
    hot_dots = jnp.where(back_hot, dot_slots[None, :], 0.0).reshape(
        own_pad, 2, 2, experts // 2, 2 * part
    )
    by_side = jnp.sum(hot_dots, axis=(1, 4))
    by_side = jnp.where(chip_side == 0, by_side, by_side[:, ::-1])
    grad_gates = by_side.transpose(0, 2, 1).reshape(own_pad, experts)
    grad_logits = own_gates * (grad_gates - jnp.sum(own_gates * grad_gates, axis=1, keepdims=True))
    grad_logits = grad_logits.astype(BF)
    g_router = dot(grad_logits, route_normed, TN)
    grad_normed = dot(grad_logits, router, NT) + dot(back_hot_bf, grad_slots, NN)
    hat, scale = norm_parts(level_three)
    g_route_gain = jnp.sum(grad_normed * hat, axis=0)
    g_route_bias = jnp.sum(grad_normed, axis=0)
    grad_stream = grad_stream + norm_back(hat, scale, route_norm_gain, grad_normed)

    near_weighted = near(after(weighted, grad_stream))
    grad_stream, g_two, small_two = attend_backward(
        grad_stream, level_two, row(sparse_norm_gain), row(sparse_norm_bias), w_two, kept_two
    )
    near_weighted = after(near_weighted, g_two)
    far_weighted = far(*near_weighted)
    exp_from_y = after(exp_from_y, g_two)
    exp_from_y2 = hop(after(part_exp[2], g_two), "tp", 2)
    exp_give = plus(part_exp[1], exp_from_y)
    exp_away = hop(exp_give, "tp", 1)
    grad_stream, g_feed, small_feed = feed_backward(
        grad_stream, level_one, row(feed_norm_gain), row(feed_norm_bias), w_feed, kept_feed
    )
    far_weighted, exp_from_y2, exp_away = lax.optimization_barrier(
        ((far_weighted, exp_from_y2, exp_away), g_feed)
    )[0]
    exp_keep = plus(part_exp[0], exp_from_y2)
    keep_sum = jnp.where(same, exp_keep, exp_away)
    other_sum = hop(jnp.where(same, exp_away, exp_keep), "ep", 1)
    weighted_slots = jnp.concatenate([weighted, *near_weighted, far_weighted])
    level_four = level_three + dot(back_hot_bf, weighted_slots, NN)
    own_final = drop_pad(level_four.astype(BF))
    near_final = near(own_final)
    grad_stream = after(grad_stream, own_final)
    grad_stream, g_one, small_one = attend_backward(
        grad_stream, level_zero, row(dense_norm_gain), row(dense_norm_bias), w_one, kept_one
    )
    near_final = after(near_final, g_one)

    blank = jnp.zeros_like(small_exp)
    first = chip_side == 0
    small = jnp.concatenate(
        [
            small_one,
            small_feed,
            small_two,
            jnp.where(first, small_exp, blank),
            jnp.where(first, blank, small_exp),
            g_router,
            jnp.pad(jnp.stack([g_route_gain, g_route_bias]), ((0, 6), (0, 0))),
        ]
    )
    t_two, t_feed, t_one, ig_all, far_final, total, pair_total = tail(
        [g_two, g_feed, g_one], drop_pad(grad_stream.astype(BF)), *near_final, small, experts
    )
    input_grad = ig_all.reshape(rows_dev, depth).astype(F32)
    other_sum = after(other_sum, t_one)

    def absolute(blocks, kind):
        out = jnp.zeros((rows_dev, depth), kind)
        for r in range(shards):
            out = lax.dynamic_update_slice_in_dim(
                out, blocks[r].astype(kind), (mine ^ r) * own, axis=0
            )
        return out

    final = absolute([own_final, *near_final, far_final], BF)

    def attend_split(value):
        value = value.astype(F32)
        return (
            value[: 3 * width].reshape(3, width, depth).transpose(2, 0, 1),
            value[3 * width :],
        )

    t_exp_in = jnp.where(pair_side == 0, keep_sum, other_sum).astype(F32)
    t_exp_out = jnp.where(pair_side == 0, other_sum, keep_sum).astype(F32)
    t_in_two, t_out_two = attend_split(t_two)
    t_in_one, t_out_one = attend_split(t_one)
    t_feed = t_feed.astype(F32)

    def own_line(value, start):
        return lax.dynamic_slice_in_dim(value, start + mine, 1, axis=0)[0]

    def two_biases(start):
        line = own_line(total, start)
        return jnp.stack([line[:width], line[2 * width : 3 * width]])

    s_one, s_feed, s_two = total[0:8], total[8:16], total[16:24]
    s_exp = lax.dynamic_slice_in_dim(pair_total, 24 + 8 * pair_side, 8, axis=0)
    s_router = total[40 : 40 + experts].T
    s_route = total[40 + experts :]
    return (
        final,
        input_grad,
        s_one[0],
        s_one[1],
        t_in_one,
        two_biases(3),
        t_out_one,
        s_one[2],
        s_feed[0],
        s_feed[1],
        t_feed[:depth],
        own_line(total, 11),
        t_feed[depth:],
        s_feed[2],
        s_two[0],
        s_two[1],
        t_in_two,
        two_biases(19),
        t_out_two,
        s_two[2],
        s_route[0],
        s_route[1],
        s_router,
        t_exp_in[None],
        own_line(s_exp, 0)[None],
        t_exp_out[None],
        s_exp[4][None],
    )


def solution(mesh):
    in_specs = (
        P("ep", None),
        P("ep", None),
        P("ep", None),
        P("ep", None),
        P("ep", None),
        P(),
        P(),
        P(None, None, "tp"),
        P(None, "tp"),
        P("tp", None),
        P(),
        P(),
        P(),
        P(None, "tp"),
        P("tp"),
        P("tp", None),
        P(),
        P(),
        P(),
        P(None, None, "tp"),
        P(None, "tp"),
        P("tp", None),
        P(),
        P(),
        P(),
        P(),
        P("ep", None, "tp"),
        P("ep", "tp"),
        P("ep", "tp", None),
        P("ep", None),
    )
    out_specs = (
        P("ep", None),
        P("ep", None),
        P(),
        P(),
        P(None, None, "tp"),
        P(None, "tp"),
        P("tp", None),
        P(),
        P(),
        P(),
        P(None, "tp"),
        P("tp"),
        P("tp", None),
        P(),
        P(),
        P(),
        P(None, None, "tp"),
        P(None, "tp"),
        P("tp", None),
        P(),
        P(),
        P(),
        P(),
        P("ep", None, "tp"),
        P("ep", "tp"),
        P("ep", "tp", None),
        P("ep", None),
    )
    return jax.shard_map(body, mesh=mesh, in_specs=in_specs, out_specs=out_specs, check_vma=False)
```

```python
import jax
import jax.numpy as jnp
from jax import lax
from jax.experimental import pallas as pl
from jax.experimental.pallas import tpu as pltpu
from jax.sharding import PartitionSpec as P

HEAD = 64
LEN = 196
PAD = 208
EPSILON = 1e-06
BF = jnp.bfloat16
F32 = jnp.float32
NN = ((1,), (0,))
NT = ((1,), (1,))
TN = ((0,), (0,))
SQRT_HALF = 0.7071067811865476
VMEM_LIMIT = 60 * 1024 * 1024


def dot(a, b, dims):
    return lax.dot_general(a, b, (dims, ((), ())), preferred_element_type=F32)


def norm_parts(x):
    average = jnp.mean(x, axis=-1, keepdims=True)
    centred = x - average
    variance = jnp.mean(centred * centred, axis=-1, keepdims=True)
    scale = lax.rsqrt(variance + EPSILON)
    return centred * scale, scale


def norm_back(hat, scale, gain, grad):
    inner = grad * gain
    first = jnp.mean(inner, axis=-1, keepdims=True)
    second = jnp.mean(inner * hat, axis=-1, keepdims=True)
    return scale * (inner - first - hat * second)


def gelu_parts(u):
    z = jnp.abs(u) * SQRT_HALF
    t = 1.0 / (1.0 + 0.3275911 * z)
    bell = jnp.exp(-(z * z))
    poly = t * (
        0.254829592
        + t * (-0.284496736 + t * (1.421413741 + t * (-1.453152027 + t * 1.061405429)))
    )
    tail = 0.5 * poly * bell
    cdf = jnp.where(u >= 0.0, 1.0 - tail, tail)
    return u * cdf, cdf + u * (bell * 0.3989422804014327)


def whole():
    return pl.BlockSpec(memory_space=pltpu.VMEM)


def params(semantics=1):
    return pltpu.CompilerParams(
        dimension_semantics=("arbitrary",) * semantics, vmem_limit_bytes=VMEM_LIMIT
    )


def key_mask():
    rows = lax.broadcasted_iota(jnp.int32, (PAD, 1), 0)
    return jnp.where(rows < LEN, 0.0, -1e30)


def attend_backward_kernel(
    g_ref,
    h_ref,
    gain_ref,
    bias_ref,
    w_ref,
    qkv_ref,
    lse_ref,
    ctx_ref,
    gout_ref,
    dw_ref,
    small_ref,
    acc_ref,
    dqkv_ref,
    dc_ref,
    db_ref,
):
    step = pl.program_id(0)
    mine = lax.axis_index("tp")
    shards = w_ref.shape[0]
    width = w_ref.shape[1] // 4
    heads = width // HEAD

    @pl.when(step == 0)
    def _():
        acc_ref[...] = jnp.zeros_like(acc_ref)
        db_ref[...] = jnp.zeros_like(db_ref)
        small_ref[...] = jnp.zeros_like(small_ref)

    grad = g_ref[...]
    hat, scale = norm_parts(h_ref[...])
    a = (hat * gain_ref[...] + bias_ref[...]).astype(BF)
    gr = grad.astype(BF)
    mask = key_mask()
    da = jnp.zeros(grad.shape, F32)
    factor = HEAD**-0.5
    for r in range(shards):
        dc_ref[...] = dot(w_ref[r, 3 * width :, :], gr, NT).astype(BF)
        acc_ref[r, 3 * width :, :] += dot(ctx_ref[0, r], gr, NN)
        for h in range(heads):
            lo = HEAD * h
            q = qkv_ref[0, r, lo : lo + HEAD, :]
            k = qkv_ref[0, r, width + lo : width + lo + HEAD, :]
            v = qkv_ref[0, r, 2 * width + lo : 2 * width + lo + HEAD, :]
            dc = dc_ref[lo : lo + HEAD, :]
            s = dot(k, q, TN) * factor + mask
            p = jnp.exp(s - lse_ref[0, r, h : h + 1, :])
            pb = p.astype(BF)
            dp = dot(v, dc, TN)
            dv = dot(dc, pb, NT)
            pdp = p * dp
            delta = jnp.sum(pdp, axis=0, keepdims=True)
            ds = (pdp - p * delta).astype(BF)
            dq = dot(k, ds, NN) * factor
            dk = dot(q, ds, NT) * factor
            dqkv_ref[lo : lo + HEAD, :] = dq.astype(BF)
            dqkv_ref[width + lo : width + lo + HEAD, :] = dk.astype(BF)
            dqkv_ref[2 * width + lo : 2 * width + lo + HEAD, :] = dv.astype(BF)
        dqkv = dqkv_ref[...]
        acc_ref[r, : 3 * width, :] += dot(dqkv, a, NN)
        db_ref[r] += jnp.sum(dqkv.astype(F32), axis=1, keepdims=True)
        da += dot(dqkv, w_ref[r, : 3 * width, :], TN)
    gout_ref[...] = grad + norm_back(hat, scale, gain_ref[...], da)
    small_ref[0:1, :] += jnp.sum(da * hat, axis=0, keepdims=True)
    small_ref[1:2, :] += jnp.sum(da, axis=0, keepdims=True)
    small_ref[2:3, :] += jnp.sum(gr.astype(F32), axis=0, keepdims=True)

    @pl.when(step == pl.num_programs(0) - 1)
    def _():
        dw_ref[...] = acc_ref[...].astype(BF)
        for r in range(shards):
            line = jnp.transpose(jnp.broadcast_to(db_ref[r], (3 * width, 128)))[0:1, :]
            line = jnp.concatenate([line, jnp.zeros((1, width), F32)], axis=1)
            small_ref[pl.ds(3 + (mine ^ r), 1), :] = line


def attend_backward(grad, h, gain, bias, w, kept):
    qkv, lse, ctx = kept
    rows, depth = h.shape
    images = rows // PAD
    shards, four, _ = w.shape
    width = four // 4
    heads = width // HEAD
    row_block = pl.BlockSpec((PAD, depth), lambda i: (i, 0))
    flops = 2 * rows * depth * depth * 4 + 4 * rows * PAD * depth
    return pl.pallas_call(
        attend_backward_kernel,
        grid=(images,),
        in_specs=[
            row_block,
            row_block,
            whole(),
            whole(),
            whole(),
            pl.BlockSpec((1, shards, 3 * width, PAD), lambda i: (i, 0, 0, 0)),
            pl.BlockSpec((1, shards, heads, PAD), lambda i: (i, 0, 0, 0)),
            pl.BlockSpec((1, shards, width, PAD), lambda i: (i, 0, 0, 0)),
        ],
        out_specs=[row_block, whole(), whole()],
        out_shape=[
            jax.ShapeDtypeStruct((rows, depth), F32),
            jax.ShapeDtypeStruct((shards, four, depth), BF),
            jax.ShapeDtypeStruct((8, depth), F32),
        ],
        scratch_shapes=[
            pltpu.VMEM((shards, four, depth), F32),
            pltpu.VMEM((3 * width, PAD), BF),
            pltpu.VMEM((width, PAD), BF),
            pltpu.VMEM((shards, 3 * width, 1), F32),
        ],
        compiler_params=params(),
        cost_estimate=pl.CostEstimate(
            flops=flops * 6, bytes_accessed=30_000_000, transcendentals=rows * PAD * 12
        ),
        name="attend_backward",
    )(grad, h, gain, bias, w, qkv, lse, ctx)


def feed_backward_kernel(
    g_ref,
    h_ref,
    gain_ref,
    bias_ref,
    w_ref,
    hid_ref,
    slope_ref,
    gout_ref,
    dw_ref,
    small_ref,
    m_ref,
    gr_ref,
    dm_ref,
):
    step = pl.program_id(0)
    depth = h_ref.shape[1]
    mine = lax.axis_index("tp")

    @pl.when(step == 0)
    def _():
        hat, _ = norm_parts(h_ref[...])
        m_ref[...] = (hat * gain_ref[...] + bias_ref[...]).astype(BF)
        gr_ref[...] = g_ref[...].astype(BF)
        dm_ref[...] = jnp.zeros_like(dm_ref)

    gr = gr_ref[...]
    dw_ref[0, depth:, :] = dot(hid_ref[0], gr, TN).astype(BF)
    dr = dot(gr, w_ref[0, depth:, :], NT)
    du = (slope_ref[0].astype(F32) * dr).astype(BF)
    small_ref[pl.ds(3 + (mine ^ step), 1), :] = jnp.sum(du.astype(F32), axis=0, keepdims=True)
    dw_ref[0, :depth, :] = dot(m_ref[...], du, TN).astype(BF)
    dm_ref[...] += dot(du, w_ref[0, :depth, :], NT)

    @pl.when(step == pl.num_programs(0) - 1)
    def _():
        hat, scale = norm_parts(h_ref[...])
        dm = dm_ref[...]
        gout_ref[...] = g_ref[...] + norm_back(hat, scale, gain_ref[...], dm)
        small_ref[0:1, :] = jnp.sum(dm * hat, axis=0, keepdims=True)
        small_ref[1:2, :] = jnp.sum(dm, axis=0, keepdims=True)
        small_ref[2:3, :] = jnp.sum(gr_ref[...].astype(F32), axis=0, keepdims=True)
        small_ref[7:8, :] = jnp.zeros((1, depth), F32)


def feed_backward(grad, h, gain, bias, w, kept):
    hid, slope = kept
    rows, depth = h.shape
    shards, double, hidden = w.shape
    shard = lambda i: (i, 0, 0)
    return pl.pallas_call(
        feed_backward_kernel,
        grid=(shards,),
        in_specs=[
            whole(),
            whole(),
            whole(),
            whole(),
            pl.BlockSpec((1, double, hidden), shard),
            pl.BlockSpec((1, rows, hidden), shard),
            pl.BlockSpec((1, rows, hidden), shard),
        ],
        out_specs=[
            whole(),
            pl.BlockSpec((1, double, hidden), shard),
            whole(),
        ],
        out_shape=[
            jax.ShapeDtypeStruct((rows, depth), F32),
            jax.ShapeDtypeStruct((shards, double, hidden), BF),
            jax.ShapeDtypeStruct((8, depth), F32),
        ],
        scratch_shapes=[
            pltpu.VMEM((rows, depth), BF),
            pltpu.VMEM((rows, depth), BF),
            pltpu.VMEM((rows, depth), F32),
        ],
        compiler_params=params(),
        cost_estimate=pl.CostEstimate(
            flops=8 * rows * depth * hidden * shards * 2,
            bytes_accessed=35_000_000,
            transcendentals=0,
        ),
        name="feed_backward",
    )(grad, h, gain, bias, w, hid, slope)


def expert_pair(mine_ref, other_ref):
    first = lax.rem(lax.axis_index("ep"), 2) == 0
    mine, other = mine_ref[0], other_ref[0]
    return jnp.where(first, mine, other), jnp.where(first, other, mine)


def expert_forward_kernel(x_ref, mine_ref, other_ref, b1_ref, b2_ref, y_ref, hid_ref, slope_ref, acc_ref):
    r = pl.program_id(0)

    @pl.when(r == 0)
    def _():
        acc_ref[...] = jnp.zeros_like(acc_ref)

    w_in, w_out = expert_pair(mine_ref, other_ref)
    u = dot(x_ref[...], w_in, NN) + b1_ref[0]
    value, slope = gelu_parts(u)
    value = value.astype(BF)
    hid_ref[0] = value
    slope_ref[0] = slope.astype(BF)
    acc_ref[...] += dot(value, w_out, NN)

    @pl.when(r == pl.num_programs(0) - 1)
    def _():
        y_ref[...] = (acc_ref[...] + b2_ref[...]).astype(BF)


def expert_forward(x, mine, other, b1, b2):
    rows, depth = x.shape
    shards, _, hidden = mine.shape
    shard = lambda r: (r, 0, 0)
    wide = pl.BlockSpec((1, rows, hidden), shard)
    weight = pl.BlockSpec((1, depth, hidden), shard)
    return pl.pallas_call(
        expert_forward_kernel,
        grid=(shards,),
        in_specs=[whole(), weight, weight, pl.BlockSpec((1, 1, hidden), shard), whole()],
        out_specs=[whole(), wide, wide],
        out_shape=[
            jax.ShapeDtypeStruct((rows, depth), BF),
            jax.ShapeDtypeStruct((shards, rows, hidden), BF),
            jax.ShapeDtypeStruct((shards, rows, hidden), BF),
        ],
        scratch_shapes=[pltpu.VMEM((rows, depth), F32)],
        compiler_params=params(),
        cost_estimate=pl.CostEstimate(
            flops=4 * rows * depth * hidden * shards * 2,
            bytes_accessed=25_000_000,
            transcendentals=rows * hidden * shards,
        ),
        name="expert_forward",
    )(x, mine, other, b1, b2)


def expert_input_kernel(
    y_ref,
    cot_ref,
    gate_ref,
    mine_ref,
    other_ref,
    slope_ref,
    wy_ref,
    dy_ref,
    dx_ref,
    dgate_ref,
    du_ref,
    small_ref,
    acc_ref,
):
    r = pl.program_id(0)
    mine = lax.axis_index("tp")

    @pl.when(r == 0)
    def _():
        y = y_ref[...].astype(F32)
        cot = cot_ref[...].astype(F32)
        gate = gate_ref[...]
        dgate_ref[...] = jnp.sum(cot * y, axis=1, keepdims=True)
        wy_ref[...] = (gate * y).astype(BF)
        dy = (gate * cot).astype(BF)
        dy_ref[...] = dy
        small_ref[4:5, :] = jnp.sum(dy.astype(F32), axis=0, keepdims=True)
        small_ref[5:8, :] = jnp.zeros((3, dy.shape[1]), F32)
        acc_ref[...] = jnp.zeros_like(acc_ref)

    w_in, w_out = expert_pair(mine_ref, other_ref)
    dr = dot(dy_ref[...], w_out, NT)
    du = (slope_ref[0].astype(F32) * dr).astype(BF)
    du_ref[0] = du
    small_ref[pl.ds(mine ^ r, 1), :] = jnp.sum(du.astype(F32), axis=0, keepdims=True)
    acc_ref[...] += dot(du, w_in, NT)

    @pl.when(r == pl.num_programs(0) - 1)
    def _():
        dx_ref[...] = acc_ref[...].astype(BF)


def expert_input(y, cot, gate, mine, other, slope):
    rows, depth = y.shape
    shards, _, hidden = mine.shape
    shard = lambda r: (r, 0, 0)
    wide = pl.BlockSpec((1, rows, hidden), shard)
    weight = pl.BlockSpec((1, depth, hidden), shard)
    return pl.pallas_call(
        expert_input_kernel,
        grid=(shards,),
        in_specs=[whole(), whole(), whole(), weight, weight, wide],
        out_specs=[
            whole(),
            whole(),
            whole(),
            whole(),
            wide,
            whole(),
        ],
        out_shape=[
            jax.ShapeDtypeStruct((rows, depth), BF),
            jax.ShapeDtypeStruct((rows, depth), BF),
            jax.ShapeDtypeStruct((rows, depth), BF),
            jax.ShapeDtypeStruct((rows, 1), F32),
            jax.ShapeDtypeStruct((shards, rows, hidden), BF),
            jax.ShapeDtypeStruct((8, depth), F32),
        ],
        scratch_shapes=[pltpu.VMEM((rows, depth), F32)],
        compiler_params=params(),
        cost_estimate=pl.CostEstimate(
            flops=4 * rows * depth * hidden * shards * 2,
            bytes_accessed=25_000_000,
            transcendentals=0,
        ),
        name="expert_input",
    )(y, cot, gate, mine, other, slope)


def expert_return_kernel(
    size,
    x_ref,
    dy_ref,
    hid_ref,
    du_ref,
    sent_ref,
    y_ref,
    dw_ref,
    out_ref,
    y_out,
    stage_ref,
    came_ref,
    swap_send,
    swap_recv,
    pass_send,
    pass_recv,
    y_send,
    y_recv,
    core_send,
    core_recv,
    local_sem,
):
    step = pl.program_id(0)
    depth = x_ref.shape[1]
    mine = lax.axis_index("tp")
    place = lax.axis_index("ep")
    to_x = {"tp": mine ^ 1}
    to_y = {"tp": mine ^ 2}

    def remote(src, dst, sends, recvs, index, peer):
        return pltpu.make_async_remote_copy(
            src_ref=src,
            dst_ref=dst,
            send_sem=sends.at[index],
            recv_sem=recvs.at[index],
            device_id=peer,
            device_id_type=pl.DeviceIdType.MESH,
        )

    def exchange(k):
        peer = place ^ k
        return remote(
            sent_ref.at[peer], out_ref.at[0, place], swap_send, swap_recv, k, {"ep": peer}
        )

    def keep():
        return pltpu.make_async_copy(sent_ref.at[place], out_ref.at[0, place], local_sem.at[0])

    def y_exchange(k):
        peer = place ^ k
        return remote(y_ref.at[peer], y_out.at[place], y_send, y_recv, k, {"ep": peer})

    def y_keep():
        return pltpu.make_async_copy(y_ref.at[place], y_out.at[place], local_sem.at[1])

    core = lax.rem(place, 2)
    own_half = pl.ds(pl.multiple_of(core * depth, depth), depth)
    other_half = pl.ds(pl.multiple_of((1 - core) * depth, depth), depth)

    def give(r):
        return remote(
            stage_ref.at[r, other_half], came_ref.at[r], core_send, core_recv, r, {"ep": place ^ 1}
        )

    def save(r):
        return pltpu.make_async_copy(stage_ref.at[r, own_half], dw_ref.at[r], local_sem.at[2 + r])

    def along(k, way):
        slab = place ^ k
        return remote(
            out_ref.at[0, slab],
            out_ref.at[1 + way, slab],
            pass_send,
            pass_recv,
            (way, k),
            (to_x, to_y)[way],
        )

    def relay(k):
        slab = place ^ k
        way = k % 2
        return remote(
            out_ref.at[1 + way, slab],
            out_ref.at[3, slab],
            pass_send,
            pass_recv,
            (2, k),
            (to_y, to_x)[way],
        )

    def forward(group):
        for k in range(size // 4 * group, size // 4 * (group + 1)):
            if k == 0:
                keep().wait()
            else:
                exchange(k).wait_recv()
            along(k, 0).start()
            along(k, 1).start()

    @pl.when(step == 0)
    def _():
        barrier = pltpu.get_barrier_semaphore()
        for peer in [to_x, to_y] + [{"ep": place ^ k} for k in range(1, size)]:
            pl.semaphore_signal(barrier, inc=1, device_id=peer, device_id_type=pl.DeviceIdType.MESH)
        pl.semaphore_wait(barrier, size + 1)
        keep().start()
        for k in range(1, size):
            exchange(k).start()

    for group in range(3):

        @pl.when(step == group + 1)
        def _(group=group):
            forward(group)

    @pl.when(step == 2)
    def _():
        y_keep().start()
        for k in range(1, size):
            y_exchange(k).start()

    stage_ref[step, depth:, :] = dot(hid_ref[0], dy_ref[...], TN).astype(BF)
    stage_ref[step, :depth, :] = dot(x_ref[...], du_ref[0], TN).astype(BF)
    for r in range(stage_ref.shape[0]):

        @pl.when(step == r)
        def _(r=r):
            give(r).start()

    @pl.when(step == 3)
    def _():
        forward(3)
        for r in range(stage_ref.shape[0]):
            give(r).wait_recv()
            add_rows(stage_ref.at[r, own_half], came_ref.at[r], depth)
            save(r).start()
        for k in range(size):
            along(k, k % 2).wait_recv()
            relay(k).start()
        y_keep().wait()
        for k in range(1, size):
            y_exchange(k).wait_recv()
            y_exchange(k).wait_send()
        for r in range(stage_ref.shape[0]):
            give(r).wait_send()
            save(r).wait()
        for k in range(size):
            along(k, 1 - k % 2).wait_recv()
            relay(k).wait_recv()
        for k in range(size):
            if k > 0:
                exchange(k).wait_send()
            along(k, 0).wait_send()
            along(k, 1).wait_send()
            relay(k).wait_send()


def expert_return(x, dy, hid, du, sent, y):
    rows, depth = x.shape
    shards, _, hidden = hid.shape
    size = sent.shape[0]
    shard = lambda r: (r, 0, 0)
    wide = pl.BlockSpec((1, rows, hidden), shard)
    any_spec = pl.BlockSpec(memory_space=pl.ANY)
    return pl.pallas_call(
        lambda *refs: expert_return_kernel(size, *refs),
        grid=(shards,),
        in_specs=[whole(), whole(), wide, wide, any_spec, any_spec],
        out_specs=[any_spec] * 3,
        out_shape=[
            jax.ShapeDtypeStruct((shards, depth, hidden), BF),
            jax.ShapeDtypeStruct((shards,) + sent.shape, BF),
            jax.ShapeDtypeStruct(y.shape, BF),
        ],
        scratch_shapes=[
            pltpu.VMEM((shards, 2 * depth, hidden), BF),
            pltpu.VMEM((shards, depth, hidden), BF),
            pltpu.SemaphoreType.DMA((size,)),
            pltpu.SemaphoreType.DMA((size,)),
            pltpu.SemaphoreType.DMA((3, size)),
            pltpu.SemaphoreType.DMA((3, size)),
            pltpu.SemaphoreType.DMA((size,)),
            pltpu.SemaphoreType.DMA((size,)),
            pltpu.SemaphoreType.DMA((shards,)),
            pltpu.SemaphoreType.DMA((shards,)),
            pltpu.SemaphoreType.DMA((2 + shards,)),
        ],
        compiler_params=pltpu.CompilerParams(
            dimension_semantics=("arbitrary",),
            vmem_limit_bytes=VMEM_LIMIT,
            collective_id=2,
            has_side_effects=True,
        ),
        cost_estimate=pl.CostEstimate(
            flops=4 * rows * depth * hidden * shards * 2,
            bytes_accessed=40_000_000,
            transcendentals=0,
        ),
        name="expert_return",
    )(x, dy, hid, du, sent, y)


ROUTES = 6


def attend_image(x, gain, bias, w_ref, biases_ref, bias_row, bout, qkv_ref, lse_ref, ctx_ref):
    shards = w_ref.shape[0]
    width = w_ref.shape[1] // 4
    heads = width // HEAD
    hat, _ = norm_parts(x)
    a = (hat * gain + bias).astype(BF)
    mask = key_mask()
    branch = jnp.zeros(x.shape, F32)
    for r in range(shards):
        column = jnp.transpose(biases_ref[r])[: 3 * width, bias_row : bias_row + 1]
        qkv = (dot(w_ref[r, : 3 * width, :], a, NT) + column).astype(BF)
        qkv_ref[0, r] = qkv
        for h in range(heads):
            q = qkv[HEAD * h : HEAD * (h + 1)]
            k = qkv[width + HEAD * h : width + HEAD * (h + 1)]
            v = qkv[2 * width + HEAD * h : 2 * width + HEAD * (h + 1)]
            s = dot(k, q, TN) * (HEAD**-0.5) + mask
            peak = jnp.max(s, axis=0, keepdims=True)
            e = jnp.exp(s - peak)
            total = jnp.sum(e, axis=0, keepdims=True)
            lse_ref[0, r, h : h + 1, :] = peak + jnp.log(total)
            c = dot(v, e.astype(BF), NN) * (1.0 / total)
            ctx_ref[0, r, HEAD * h : HEAD * (h + 1), :] = c.astype(BF)
        branch += dot(ctx_ref[0, r], w_ref[r, 3 * width :, :], TN)
    return x + branch + bout


def forward_kernel(
    x_ref,
    vec_ref,
    bias_ref,
    one_ref,
    feed_ref,
    two_ref,
    h1_ref,
    h2_ref,
    h3_ref,
    qkv1_ref,
    lse1_ref,
    ctx1_ref,
    hid_ref,
    slope_ref,
    qkv2_ref,
    lse2_ref,
    ctx2_ref,
    w1_out,
    wf_out,
    w2_out,
    normed_out,
    biases_out,
    h_ref,
    w1_ref,
    wf_ref,
    w2_ref,
    b_ref,
    n_ref,
    send_sem,
    recv_sem,
    n_send,
    n_recv,
    small_send,
    small_recv,
    local_sem,
):
    step = pl.program_id(0)
    images = 4
    mine = lax.axis_index("tp")
    place = lax.axis_index("ep")
    core = lax.rem(place, 2)
    side = lax.rem(mine, 2)
    to_x = {"tp": mine ^ 1}
    to_y = {"tp": mine ^ 2}
    to_far = {"tp": mine ^ 3}
    to_core = {"ep": place ^ 1}
    depth = x_ref.shape[1]

    def remote(src, dst, sends, recvs, index, peer):
        return pltpu.make_async_remote_copy(
            src_ref=src,
            dst_ref=dst,
            send_sem=sends.at[index],
            recv_sem=recvs.at[index],
            device_id=peer,
            device_id_type=pl.DeviceIdType.MESH,
        )

    def copies(group, own, full):
        rows = own.shape[0] // 2
        start = pl.multiple_of(core * rows, rows)
        quarter = rows // 2
        middle = pl.multiple_of(start + quarter, quarter)
        half = pl.ds(start, rows)
        low = pl.ds(start, quarter)
        high = pl.ds(middle, quarter)

        def make(k, src, dst, peer):
            return remote(src, dst, send_sem, recv_sem, (group, k), peer)

        return [
            make(0, own.at[half], full.at[1, half], to_x),
            make(1, own.at[half], full.at[2, half], to_y),
            make(2, full.at[1, low], full.at[3, low], to_y),
            make(3, full.at[2, high], full.at[3, high], to_x),
            make(4, full.at[pl.ds(1, 2), half], full.at[pl.ds(1, 2), half], to_core),
            make(5, full.at[3, half], full.at[3, half], to_core),
        ]

    one = copies(0, one_ref, w1_ref)
    feed = copies(1, feed_ref, wf_ref)
    two = copies(2, two_ref, w2_ref)

    small = [
        remote(bias_ref, b_ref.at[r], small_send, small_recv, r - 1, peer)
        for r, peer in ((1, to_x), (2, to_y), (3, to_far))
    ]
    own_local = [
        pltpu.make_async_copy(one_ref, w1_ref.at[0], local_sem.at[0]),
        pltpu.make_async_copy(feed_ref, wf_ref.at[0], local_sem.at[1]),
        pltpu.make_async_copy(two_ref, w2_ref.at[0], local_sem.at[2]),
    ]
    saves = [
        pltpu.make_async_copy(w1_ref, w1_out, local_sem.at[4]),
        pltpu.make_async_copy(wf_ref, wf_out, local_sem.at[5]),
        pltpu.make_async_copy(w2_ref, w2_out, local_sem.at[6]),
    ]

    def rows_copy(i):
        rows = pl.ds(PAD * i, PAD)
        low, high = pl.ds(PAD * i, 96), pl.ds(PAD * i + 96, PAD - 96)
        return [
            remote(n_ref.at[i], normed_out.at[1, rows], n_send, n_recv, (0, i), to_x),
            remote(n_ref.at[i], normed_out.at[2, rows], n_send, n_recv, (1, i), to_y),
            remote(normed_out.at[1, low], normed_out.at[3, low], n_send, n_recv, (2, i), to_y),
            remote(normed_out.at[2, high], normed_out.at[3, high], n_send, n_recv, (3, i), to_x),
            pltpu.make_async_copy(n_ref.at[i], normed_out.at[0, rows], local_sem.at[8 + i]),
        ]

    def vec(k):
        return vec_ref[k : k + 1, :]

    @pl.when(step == 0)
    def _():
        barrier = pltpu.get_barrier_semaphore()
        for peer in (to_x, to_y, to_far, to_core):
            pl.semaphore_signal(barrier, inc=1, device_id=peer, device_id_type=pl.DeviceIdType.MESH)
        pl.semaphore_wait(barrier, 4)
        one[0].start()
        one[1].start()
        own_local[0].start()
        for copy in small:
            copy.start()
        b_ref[0] = bias_ref[...]
        one[0].wait_recv()
        one[1].wait_recv()
        one[2].start()
        one[3].start()
        one[4].start()
        feed[0].start()
        feed[1].start()
        one[2].wait_recv()
        one[3].wait_recv()
        one[5].start()
        own_local[1].start()
        own_local[2].start()
        own_local[0].wait()
        for copy in small:
            copy.wait_recv()
        one[4].wait_recv()
        one[5].wait_recv()

    @pl.when(step == 2)
    def _():
        saves[0].start()
        feed[0].wait_recv()
        feed[1].wait_recv()
        feed[2].start()
        feed[3].start()
        feed[4].start()

    @pl.when(step == 4)
    def _():
        feed[2].wait_recv()
        feed[3].wait_recv()
        feed[5].start()
        two[0].start()
        two[1].start()
        own_local[1].wait()
        feed[4].wait_recv()
        feed[5].wait_recv()

    @pl.when(step == 6)
    def _():
        saves[1].start()
        two[0].wait_recv()
        two[1].wait_recv()
        two[2].start()
        two[3].start()
        two[4].start()

    @pl.when(step == 7)
    def _():
        two[2].wait_recv()
        two[3].wait_recv()
        two[5].start()

    @pl.when(step == 8)
    def _():
        own_local[2].wait()
        two[4].wait_recv()
        two[5].wait_recv()

    @pl.when(step == 10)
    def _():
        saves[2].start()

    @pl.when(step < images)
    def _():
        x = x_ref[pl.ds(pl.multiple_of(step * PAD, PAD), PAD), :].astype(F32)
        h = attend_image(
            x, vec(0), vec(1), w1_ref, b_ref, 0, vec(2), qkv1_ref, lse1_ref, ctx1_ref
        )
        h_ref[step] = h
        h1_ref[...] = h

    @pl.when((step >= images) & (step < 2 * images))
    def _():
        tile = step - images
        x = h_ref[tile]
        hat, _ = norm_parts(x)
        m = (hat * vec(3) + vec(4)).astype(BF)
        acc = x + vec(5)
        for r in range(wf_ref.shape[0]):
            u = dot(m, wf_ref[r, :depth, :], NN) + b_ref[r, 2:3, :]
            value, slope = gelu_parts(u)
            value = value.astype(BF)
            hid_ref[r] = value
            slope_ref[r] = slope.astype(BF)
            acc += dot(value, wf_ref[r, depth:, :], NN)
        h_ref[tile] = acc
        h2_ref[...] = acc

    @pl.when(step >= 2 * images)
    def _():
        image = step - 2 * images
        h = attend_image(
            h_ref[image], vec(6), vec(7), w2_ref, b_ref, 1, vec(8), qkv2_ref, lse2_ref, ctx2_ref
        )
        h3_ref[...] = h
        hat, _ = norm_parts(h)
        n_ref[image] = (hat * vec(9) + vec(10)).astype(BF)

    for i in range(images):

        @pl.when(step == 2 * images + i)
        def _(i=i):
            to_send = rows_copy(i)
            to_send[0].start()
            to_send[1].start()
            to_send[4].start()
            if i > 0:
                before = rows_copy(i - 1)
                before[0].wait_recv()
                before[1].wait_recv()
                before[2].start()
                before[3].start()

    @pl.when(step == 3 * images - 1)
    def _():
        last = rows_copy(images - 1)
        last[0].wait_recv()
        last[1].wait_recv()
        last[2].start()
        last[3].start()
        pltpu.make_async_copy(b_ref, biases_out, local_sem.at[7]).start()
        for i in range(images):
            moved = rows_copy(i)
            moved[2].wait_recv()
            moved[3].wait_recv()
            for k in range(4):
                moved[k].wait_send()
            moved[4].wait()
        for group in (one, feed, two):
            for copy in group:
                copy.wait_send()
        for copy in small:
            copy.wait_send()
        for copy in saves:
            copy.wait()
        pltpu.make_async_copy(b_ref, biases_out, local_sem.at[7]).wait()


def dense_forward(x, vectors, bias, pack_one, pack_feed, pack_two):
    rows, depth = x.shape
    images = rows // PAD
    shards = 4
    four = pack_one.shape[0]
    width = four // 4
    heads = width // HEAD
    double, hidden = pack_feed.shape
    any_spec = pl.BlockSpec(memory_space=pl.ANY)

    def part(number):
        return lambda s: jnp.clip(s - images * number, 0, images - 1)

    def row_spec(number):
        at = part(number)
        return pl.BlockSpec((PAD, depth), lambda s: (at(s), 0))

    def attend_specs(number):
        at = part(number)
        return [
            pl.BlockSpec((1, shards, 3 * width, PAD), lambda s: (at(s), 0, 0, 0)),
            pl.BlockSpec((1, shards, heads, PAD), lambda s: (at(s), 0, 0, 0)),
            pl.BlockSpec((1, shards, width, PAD), lambda s: (at(s), 0, 0, 0)),
        ]

    tile_at = part(1)
    hid_spec = pl.BlockSpec((shards, PAD, hidden), lambda s: (0, tile_at(s), 0))
    shape = jax.ShapeDtypeStruct
    attend_shapes = [
        shape((images, shards, 3 * width, PAD), BF),
        shape((images, shards, heads, PAD), F32),
        shape((images, shards, width, PAD), BF),
    ]
    out = pl.pallas_call(
        forward_kernel,
        grid=(3 * images,),
        in_specs=[whole(), whole(), whole()] + [any_spec] * 3,
        out_specs=[row_spec(0), row_spec(1), row_spec(2)]
        + attend_specs(0)
        + [hid_spec, hid_spec]
        + attend_specs(2)
        + [any_spec] * 5,
        out_shape=[shape((rows, depth), F32)] * 3
        + attend_shapes
        + [shape((shards, rows, hidden), BF)] * 2
        + attend_shapes
        + [
            shape((shards, four, depth), BF),
            shape((shards, double, hidden), BF),
            shape((shards, four, depth), BF),
            shape((shards, rows, depth), BF),
            shape((shards, 8, depth), F32),
        ],
        scratch_shapes=[
            pltpu.VMEM((images, PAD, depth), F32),
            pltpu.VMEM((shards, four, depth), BF),
            pltpu.VMEM((shards, double, hidden), BF),
            pltpu.VMEM((shards, four, depth), BF),
            pltpu.VMEM((shards, 8, depth), F32),
            pltpu.VMEM((images, PAD, depth), BF),
            pltpu.SemaphoreType.DMA((3, ROUTES)),
            pltpu.SemaphoreType.DMA((3, ROUTES)),
            pltpu.SemaphoreType.DMA((4, 4)),
            pltpu.SemaphoreType.DMA((4, 4)),
            pltpu.SemaphoreType.DMA((3,)),
            pltpu.SemaphoreType.DMA((3,)),
            pltpu.SemaphoreType.DMA((12,)),
        ],
        compiler_params=pltpu.CompilerParams(
            dimension_semantics=("arbitrary",),
            vmem_limit_bytes=VMEM_LIMIT,
            collective_id=0,
            has_side_effects=True,
        ),
        cost_estimate=pl.CostEstimate(
            flops=60_000_000_000, bytes_accessed=60_000_000, transcendentals=10_000_000
        ),
        name="dense_forward",
    )(x, vectors, bias, pack_one, pack_feed, pack_two)
    (h1, h2, h3, q1, l1, c1, hid, slope, q2, l2, c2, w1, wf, w2, normed, biases) = out
    return (h1, h2, h3), (q1, l1, c1), (hid, slope), (q2, l2, c2), (w1, wf, w2), normed, biases


TAIL_ORDER = (0, 3, 0, 1, 3, 0, 1, 2, 0, 3, 0, 2, 0, 0, 1, 3, 0, 2, 1, 2, 4, 0, 1, 2, 3, 1, 2, 4, 1, 2, 3, 1, 2, 4)


def add_rows(dst, src, rows):
    tile = 48

    def body(i, carry):
        at = pl.ds(pl.multiple_of(i * tile, 16), tile)
        dst[at] = (dst[at].astype(F32) + src[at].astype(F32)).astype(BF)
        return carry

    lax.fori_loop(0, rows // tile, body, 0)


def plane_bits(size):
    return [1 << k for k in range(1, size.bit_length() - 1)]


def halvings(rows, bits):
    count = 0
    while count < len(bits) and rows % 32 == 0:
        rows //= 2
        count += 1
    return count


def tail_kernel(size, rows_list, *refs):
    groups = len(rows_list)
    bits = plane_bits(size)
    take = iter(refs)
    sources = [next(take) for _ in range(groups)]
    ig_ref, act_x, act_y, small_ref = [next(take) for _ in range(4)]
    outs = [next(take) for _ in range(groups)]
    ig_out, act_out, total_ref, pair_ref = [next(take) for _ in range(4)]
    keeps = [next(take) for _ in range(groups)]
    cores = [next(take) for _ in range(groups)]
    firsts = [next(take) for _ in range(groups)]
    seconds = [next(take) for _ in range(groups)]
    planes = [next(take) for _ in range(groups)]
    halves = [next(take) for _ in range(groups)]
    landed = next(take)
    send_sem, recv_sem, local_sem, ig_send, ig_recv, small_send, small_recv = take

    mine = lax.axis_index("tp")
    place = lax.axis_index("ep")
    core = lax.rem(place, 2)
    to_x = {"tp": mine ^ 1}
    to_y = {"tp": mine ^ 2}
    to_core = {"ep": place ^ 1}
    to_plane = [{"ep": place ^ bit} for bit in bits]

    barrier = pltpu.get_barrier_semaphore()
    for peer in [to_x, to_y, to_core] + to_plane:
        pl.semaphore_signal(barrier, inc=1, device_id=peer, device_id_type=pl.DeviceIdType.MESH)
    pl.semaphore_wait(barrier, 3 + len(bits))

    def remote(src, dst, sends, recvs, index, peer):
        return pltpu.make_async_remote_copy(
            src_ref=src,
            dst_ref=dst,
            send_sem=sends.at[index],
            recv_sem=recvs.at[index],
            device_id=peer,
            device_id_type=pl.DeviceIdType.MESH,
        )

    def group_steps(g):
        rows = rows_list[g]
        half, quarter = rows // 2, rows // 4
        source, keep, came, first, second = sources[g], keeps[g], cores[g], firsts[g], seconds[g]
        plane, out, whole_half = planes[g], outs[g], halves[g]
        own_half = pl.ds(pl.multiple_of(core * half, half), half)
        other_half = pl.ds(pl.multiple_of((1 - core) * half, half), half)
        number = iter(range(100))
        sent = []

        def send(src, dst, peer):
            copy = remote(src, dst, send_sem, recv_sem, (g, next(number)), peer)
            copy.start()
            sent.append(copy)
            return copy

        every = pl.ds(0, keep.shape[0])
        local = pltpu.make_async_copy(source.at[every, own_half], keep, local_sem.at[g])
        local.start()
        swap = send(source.at[every, other_half], came, to_core)
        yield
        local.wait()
        swap.wait_recv()
        for r in range(keep.shape[0]):
            add_rows(keep.at[r], came.at[r], half)
        low, high = pl.ds(0, quarter), pl.ds(quarter, quarter)
        waits = [
            send(keep.at[1, low], first.at[0], to_x),
            send(keep.at[3, low], first.at[1], to_x),
            send(keep.at[pl.ds(2, 2), high], first.at[pl.ds(2, 2)], to_y),
        ]
        yield
        for copy in waits:
            copy.wait_recv()
        add_rows(keep.at[2, low], first.at[1], quarter)
        add_rows(keep.at[1, high], first.at[3], quarter)
        waits = [
            send(keep.at[2, low], second.at[0], to_y),
            send(keep.at[1, high], second.at[1], to_x),
        ]
        add_rows(keep.at[0, low], first.at[0], quarter)
        add_rows(keep.at[0, high], first.at[2], quarter)
        yield
        for copy in waits:
            copy.wait_recv()
        add_rows(keep.at[0, low], second.at[0], quarter)
        add_rows(keep.at[0, high], second.at[1], quarter)
        start, length, done = 0, half, []
        offset = 0
        for k, bit in enumerate(bits):
            if k < halvings(half, bits):
                length //= 2
                side = lax.rem(place // bit, 2)
                mine_at = pl.ds(pl.multiple_of(start + side * length, 16), length)
                give_at = pl.ds(pl.multiple_of(start + (1 - side) * length, 16), length)
                land = plane.at[pl.ds(offset, length)]
                copy = send(keep.at[0, give_at], land, to_plane[k])
                done.append((mine_at, k))
                start = start + side * length
            else:
                mine_at = pl.ds(pl.multiple_of(start + 0 * place, 16), length)
                land = plane.at[pl.ds(offset, length)]
                copy = send(keep.at[0, mine_at], land, to_plane[k])
            yield
            copy.wait_recv()
            if k >= halvings(half, bits):
                copy.wait_send()
                sent.pop()
            add_rows(keep.at[0, mine_at], land, length)
            offset += length
        at = done[-1][0]
        whole_half[at] = keep[0, at, :]
        for at, k in done[::-1]:
            copy = send(whole_half.at[at], whole_half.at[at], to_plane[k])
            yield
            copy.wait_recv()
        copy = send(whole_half, out.at[own_half], to_core)
        local = pltpu.make_async_copy(whole_half, out.at[own_half], local_sem.at[groups + g])
        local.start()
        yield
        copy.wait_recv()
        local.wait()
        for copy in sent:
            copy.wait_send()

    def ig_steps():
        half = ig_ref.shape[0] // 32 * 16
        low, high = pl.ds(0, half), pl.ds(half, ig_ref.shape[0] - half)
        near = [
            remote(ig_ref, ig_out.at[mine], ig_send, ig_recv, 0, to_x),
            remote(ig_ref, ig_out.at[mine], ig_send, ig_recv, 1, to_y),
        ]
        local = pltpu.make_async_copy(ig_ref, ig_out.at[mine], local_sem.at[2 * groups])
        local.start()
        for copy in near:
            copy.start()
        yield
        passed = [
            remote(act_x.at[low], act_out.at[low], ig_send, ig_recv, 4, to_y),
            remote(act_y.at[high], act_out.at[high], ig_send, ig_recv, 5, to_x),
        ]
        for copy in passed:
            copy.start()
        for copy in near:
            copy.wait_recv()
        relay = [
            remote(ig_out.at[mine ^ 1, low], ig_out.at[mine ^ 1, low], ig_send, ig_recv, 2, to_y),
            remote(ig_out.at[mine ^ 2, high], ig_out.at[mine ^ 2, high], ig_send, ig_recv, 3, to_x),
        ]
        for copy in relay:
            copy.start()
        yield
        for copy in relay:
            copy.wait_recv()
        for copy in passed:
            copy.wait_recv()
        for copy in near + relay + passed:
            copy.wait_send()
        local.wait()

    def small_steps():
        total_ref[...] = small_ref[...]
        peers = [to_x, to_y, to_core] + to_plane
        for k, peer in enumerate(peers):
            copy = remote(total_ref, landed.at[k], small_send, small_recv, k, peer)
            copy.start()
            yield
            copy.wait()
            total_ref[...] += landed[k]
            if k == 2:
                pair_ref[...] = total_ref[...]

    running = [group_steps(g) for g in range(groups)] + [small_steps(), ig_steps()]
    ended = set()

    def advance(which):
        if which not in ended:
            try:
                next(running[which])
            except StopIteration:
                ended.add(which)

    for which in TAIL_ORDER:
        advance(which)
    while len(ended) < len(running):
        for which in range(len(running)):
            advance(which)


def tail(grads, ig, act_x, act_y, small, size):
    shards, _, depth = grads[0].shape
    rows_list = [g.shape[1] for g in grads]
    groups = len(grads)
    bits = plane_bits(size)
    any_spec = pl.BlockSpec(memory_space=pl.ANY)
    shape = jax.ShapeDtypeStruct

    def plane_rows(rows):
        half, total = rows // 2, 0
        for k in range(len(bits)):
            if k < halvings(rows // 2, bits):
                half //= 2
            total += half
        return total

    copies = 4 + 2 + 2 * len(bits) + 1
    return pl.pallas_call(
        lambda *refs: tail_kernel(size, rows_list, *refs),
        in_specs=[any_spec] * (groups + 3) + [whole()],
        out_specs=[any_spec] * (groups + 2) + [whole(), whole()],
        out_shape=[shape((rows, depth), BF) for rows in rows_list]
        + [shape((shards,) + ig.shape, BF), shape(ig.shape, BF), shape(small.shape, F32), shape(small.shape, F32)],
        scratch_shapes=[pltpu.VMEM((shards, rows // 2, depth), BF) for rows in rows_list]
        + [pltpu.VMEM((shards, rows // 2, depth), BF) for rows in rows_list]
        + [pltpu.VMEM((4, rows // 4, depth), BF) for rows in rows_list]
        + [pltpu.VMEM((2, rows // 4, depth), BF) for rows in rows_list]
        + [pltpu.VMEM((plane_rows(rows), depth), BF) for rows in rows_list]
        + [pltpu.VMEM((rows // 2, depth), BF) for rows in rows_list]
        + [
            pltpu.VMEM((3 + len(bits),) + small.shape, F32),
            pltpu.SemaphoreType.DMA((groups, copies)),
            pltpu.SemaphoreType.DMA((groups, copies)),
            pltpu.SemaphoreType.DMA((2 * groups + 1,)),
            pltpu.SemaphoreType.DMA((6,)),
            pltpu.SemaphoreType.DMA((6,)),
            pltpu.SemaphoreType.DMA((3 + len(bits),)),
            pltpu.SemaphoreType.DMA((3 + len(bits),)),
        ],
        compiler_params=pltpu.CompilerParams(
            vmem_limit_bytes=VMEM_LIMIT, collective_id=1, has_side_effects=True
        ),
        cost_estimate=pl.CostEstimate(flops=30_000_000, bytes_accessed=60_000_000, transcendentals=0),
        name="tail",
    )(*grads, ig, act_x, act_y, small)


def hop(value, axis, bit):
    size = lax.axis_size(axis)
    return lax.ppermute(value, axis, [(i, i ^ bit) for i in range(size)])


def after(value, *deps):
    return lax.optimization_barrier((value, deps))[0]


def near(value):
    return hop(value, "tp", 1), hop(value, "tp", 2)


def far(from_x, from_y):
    half = from_x.shape[0] // 2
    low = hop(from_x[:half], "tp", 2)
    high = hop(from_y[half:], "tp", 1)
    return jnp.concatenate([low, high])


def gather_tp_small(value):
    return jnp.stack([value, hop(value, "tp", 1), hop(value, "tp", 2), hop(value, "tp", 3)])


def take_half(value, which, axis=0):
    half = value.shape[axis] // 2
    return lax.dynamic_slice_in_dim(value, which * half, half, axis=axis)


def join_halves(value, other, which, axis=0):
    half = value.shape[axis]
    three = jnp.concatenate([value, other, value], axis=axis)
    return lax.dynamic_slice_in_dim(three, which * half, 2 * half, axis=axis)


def plus(a, b):
    return (a.astype(F32) + b.astype(F32)).astype(BF)


def core_sum(value):
    core = lax.axis_index("ep") % 2
    return plus(take_half(value, core, 1), hop(take_half(value, 1 - core, 1), "ep", 1))


def swap_ep(value):
    return lax.all_to_all(value, "ep", split_axis=0, concat_axis=0, tiled=True)


def route_kernel(order_ref, index_ref, hot_ref, out_ref, rank_ref):
    rows = order_ref.shape[1]
    tile = rows // 7
    half = hot_ref.shape[1] // 2
    for i in range(7):
        ids = lax.broadcasted_iota(jnp.int32, (tile, 1), 0) + tile * i
        match = jnp.where(order_ref[...] == ids, 1.0, 0.0).astype(BF)
        rank_ref[tile * i : tile * (i + 1), :] = dot(match, index_ref[...], NN)
    parts = rank_ref[...]
    rank = parts[:, 0:1] * 64.0 + parts[:, 1:2]
    rank_row = jnp.transpose(jnp.broadcast_to(rank, parts.shape))[0:1, :]
    hot = hot_ref[...]
    total = jnp.sum(hot.astype(F32), axis=0, keepdims=True)
    lanes = lax.broadcasted_iota(jnp.int32, (1, 2 * half), 1)
    firsts = jnp.where(lanes < half, total, 0.0)
    firsts = jnp.concatenate([jnp.zeros((1, half), F32), firsts[:, :half]], axis=1)
    for i in range(7):
        at = slice(tile * i, tile * (i + 1))
        earlier = jnp.where(rank_row < rank[at], 1.0, 0.0).astype(BF)
        count = dot(earlier, hot, NN) + firsts
        picked = count * hot[at].astype(F32)
        first = jnp.sum(jnp.where(lanes < half, picked, 0.0), axis=1, keepdims=True)
        second = jnp.sum(jnp.where(lanes < half, 0.0, picked), axis=1, keepdims=True)
        out_ref[at, :] = jnp.where(lanes == 0, first, second)


def route(picks, order):
    rows = picks.shape[0]
    half = 64
    ids = jnp.arange(half, dtype=jnp.int32)[None, :]
    hot = jnp.concatenate([picks[:, 0:1] == ids, picks[:, 1:2] == ids], axis=1).astype(BF)
    line = jnp.arange(rows, dtype=jnp.int32)[:, None]
    column = jnp.arange(2 * half, dtype=jnp.int32)[None, :]
    index = jnp.where(column == 0, line // 64, jnp.where(column == 1, line % 64, 0)).astype(BF)
    out = pl.pallas_call(
        route_kernel,
        in_specs=[whole(), whole(), whole()],
        out_specs=whole(),
        out_shape=jax.ShapeDtypeStruct((rows, 2 * half), F32),
        scratch_shapes=[pltpu.VMEM((rows, 2 * half), F32)],
        compiler_params=pltpu.CompilerParams(vmem_limit_bytes=VMEM_LIMIT),
        cost_estimate=pl.CostEstimate(
            flops=4 * rows * rows * 128, bytes_accessed=4_000_000, transcendentals=0
        ),
        name="route",
    )(order.reshape(1, rows), after(index, hot), hot)
    return out[:, :2].astype(jnp.int32)


def body(
    tokens,
    cotangent,
    picks,
    priority,
    router_noise,
    dense_norm_gain,
    dense_norm_bias,
    dense_attend_in,
    dense_attend_bias,
    dense_attend_out,
    dense_attend_out_bias,
    feed_norm_gain,
    feed_norm_bias,
    feed_in,
    feed_in_bias,
    feed_out,
    feed_out_bias,
    sparse_norm_gain,
    sparse_norm_bias,
    sparse_attend_in,
    sparse_attend_bias,
    sparse_attend_out,
    sparse_attend_out_bias,
    route_norm_gain,
    route_norm_bias,
    router,
    expert_in,
    expert_in_bias,
    expert_out,
    expert_out_bias,
):
    shards = lax.axis_size("tp")
    experts = lax.axis_size("ep")
    mine = lax.axis_index("tp")
    rows_dev, depth = tokens.shape
    own = rows_dev // shards
    images = own // LEN
    own_pad = images * PAD
    capacity = rows_dev // experts
    part = -(-capacity // (8 * shards)) * 8
    width = dense_attend_bias.shape[1]
    hidden = feed_in_bias.shape[0]

    def pad_images(value):
        blocks = value.reshape(-1, LEN, value.shape[-1])
        return jnp.pad(blocks, ((0, 0), (0, PAD - LEN), (0, 0))).reshape(-1, value.shape[-1])

    def drop_pad(value):
        return value.reshape(images, PAD, depth)[:, :LEN].reshape(own, depth)

    def own_rows(value):
        return lax.dynamic_slice_in_dim(value, mine * own, own, axis=0)

    def by_index(value):
        return jnp.stack(
            [
                lax.dynamic_index_in_dim(value, mine ^ r, axis=0, keepdims=False)
                for r in range(shards)
            ]
        )

    def row(value):
        return value.reshape(1, -1)

    def attend_pack(proj_in, proj_out):
        return jnp.concatenate([proj_in.transpose(1, 2, 0).reshape(3 * width, depth), proj_out])

    pair_side = lax.axis_index("ep") % 2
    chip_side = mine % 2
    same = pair_side == chip_side
    keep_exp = jnp.where(pair_side == 0, expert_in[0], expert_out[0])
    give_exp = jnp.where(pair_side == 0, expert_out[0], expert_in[0])
    vectors = jnp.stack(
        [
            dense_norm_gain,
            dense_norm_bias,
            dense_attend_out_bias,
            feed_norm_gain,
            feed_norm_bias,
            feed_out_bias,
            sparse_norm_gain,
            sparse_norm_bias,
            sparse_attend_out_bias,
            route_norm_gain,
            route_norm_bias,
        ]
    )
    vectors = jnp.pad(vectors, ((0, 5), (0, 0)))

    def bias_line(value):
        gap = jnp.zeros((width,), F32)
        return jnp.concatenate([value[0], gap, value[1], jnp.zeros((depth - 3 * width,), F32)])

    own_biases = jnp.stack(
        [
            bias_line(dense_attend_bias),
            bias_line(sparse_attend_bias),
            feed_in_bias,
            expert_in_bias[0],
            expert_out_bias[0],
        ]
    )
    own_biases = jnp.pad(own_biases, ((0, 3), (0, 0)))
    swapped = hop(give_exp, "ep", 1)
    home_exp = jnp.where(same, keep_exp, swapped)
    away_exp = jnp.where(same, swapped, keep_exp)
    level_zero = after(pad_images(own_rows(tokens)), home_exp, away_exp)
    (level_one, level_two, level_three), kept_one, kept_feed, kept_two, gathered, normed, biases = (
        dense_forward(
            level_zero,
            vectors,
            own_biases,
            attend_pack(dense_attend_in, dense_attend_out),
            jnp.concatenate([feed_in, feed_out]),
            attend_pack(sparse_attend_in, sparse_attend_out),
        )
    )
    w_one, w_feed, w_two = gathered
    level_zero = level_zero.astype(F32)
    exp_small = biases[:, 3:5]
    exp_small = jnp.where(same, exp_small, hop(exp_small, "ep", 1))
    b_exp = exp_small[:, 0:1]
    b_exp_out = exp_small[0, 1:2]

    home_exp = after(home_exp, normed)
    away_exp = after(away_exp, normed)
    exp_x = hop(away_exp, "tp", 1)
    exp_far = hop(away_exp, "tp", 3)
    exp_y = hop(home_exp, "tp", 2)
    other_home = hop(home_exp, "ep", 1)

    position = route(after(picks, normed), priority[0])
    targets = jnp.where(position < capacity, picks * (part * shards) + position, -1).T
    slots = jnp.arange(experts * part, dtype=jnp.int32)

    def slots_of(index):
        block, inside = slots // part, slots % part
        expert = 2 * (block // 2) + index % 2
        quarter = 2 * (index // 2) + block % 2
        return expert * (part * shards) + quarter * part + inside

    slot_ids = slots_of(mine)
    pad_targets = jnp.pad(
        targets.reshape(2, -1, LEN), ((0, 0), (0, 0), (0, PAD - LEN)), constant_values=-1
    ).reshape(2, -1)
    near_targets = jnp.concatenate(
        [
            lax.dynamic_slice_in_dim(pad_targets, (mine ^ r) * own_pad, own_pad, axis=1)
            for r in range(shards)
        ],
        axis=1,
    )
    noise_pad = pad_images(router_noise)
    all_slots = jnp.concatenate([slots_of(mine ^ r) for r in range(shards)])
    own_targets = near_targets[:, :own_pad].T
    back_hot = (own_targets[:, 0:1] == all_slots[None, :]) | (
        own_targets[:, 1:2] == all_slots[None, :]
    )
    back_hot_bf = back_hot.astype(BF)

    all_normed = normed.reshape(shards * own_pad, depth)
    route_normed = normed[0]
    noise = jnp.concatenate(
        [
            lax.dynamic_slice_in_dim(noise_pad, (mine ^ r) * own_pad, own_pad, axis=0)
            for r in range(shards)
        ]
    )
    logits = dot(all_normed, router, NN) + noise
    gates = jax.nn.softmax(logits, axis=-1)
    own_hot = (slot_ids[:, None] == near_targets[0][None, :]) | (
        slot_ids[:, None] == near_targets[1][None, :]
    )
    side_gates = lax.dynamic_index_in_dim(
        gates.T.reshape(experts // 2, 2, -1), chip_side, axis=1, keepdims=False
    )
    hot_gates = own_hot.reshape(experts // 2, 2 * part, -1).astype(F32) * side_gates[:, None, :]
    slot_gate = jnp.sum(hot_gates, axis=2).reshape(-1, 1)

    def two_parts(value):
        high = lax.reduce_precision(value, 8, 7)
        rest = jnp.zeros((value.shape[0], 126), BF)
        return jnp.concatenate([high.astype(BF), (value - high).astype(BF), rest], axis=1)

    def swap_rows(value):
        wide = value.shape[-1]
        return swap_ep(value.reshape(experts, part, wide)).reshape(experts * part, wide)

    rows = dot(own_hot.astype(BF), all_normed, NN).astype(BF)
    arrived = swap_rows(jnp.concatenate([rows, two_parts(slot_gate)], axis=1))
    cot_hot = (slot_ids[:, None] == targets[0][None, :]) | (slot_ids[:, None] == targets[1][None, :])
    cot_sent = dot(after(cot_hot.astype(BF), rows), cotangent, NN).astype(BF)
    cot_rows = swap_rows(cot_sent)
    exp_x, exp_y, exp_far = after((exp_x, exp_y, exp_far), cot_sent)
    exp_mine = jnp.stack([home_exp, exp_x, exp_y, exp_far])
    exp_other = jnp.stack(
        [other_home, hop(exp_x, "ep", 1), hop(exp_y, "ep", 1), hop(exp_far, "ep", 1)]
    )
    inputs = arrived[:, :depth]
    gate_in = arrived[:, depth : depth + 2].astype(F32)
    gate_in = gate_in[:, 0:1] + gate_in[:, 1:2]
    outputs, exp_hidden, exp_slope = expert_forward(inputs, exp_mine, exp_other, b_exp, b_exp_out)
    weighted, grad_outputs, grad_inputs, slot_dot, exp_du, small_exp = (
        expert_input(outputs, cot_rows, gate_in, exp_mine, exp_other, exp_slope)
    )
    sent = jnp.concatenate([grad_inputs, two_parts(slot_dot)], axis=1)
    part_exp, grad_slots, weighted = expert_return(
        inputs,
        grad_outputs,
        exp_hidden,
        exp_du,
        sent.reshape(experts, part, sent.shape[1]),
        weighted.reshape(experts, part, depth),
    )
    weighted = weighted.reshape(experts * part, depth)
    grad_slots = grad_slots.reshape(shards * experts * part, sent.shape[1])
    exp_from_y = hop(part_exp[3], "tp", 2)
    dot_slots = grad_slots[:, depth : depth + 2].astype(F32)
    dot_slots = dot_slots[:, 0] + dot_slots[:, 1]
    grad_slots = grad_slots[:, :depth]

    grad_stream = pad_images(own_rows(after(cotangent, cot_sent))).astype(F32)
    own_gates = gates[:own_pad]
    hot_dots = jnp.where(back_hot, dot_slots[None, :], 0.0).reshape(
        own_pad, 2, 2, experts // 2, 2 * part
    )
    by_side = jnp.sum(hot_dots, axis=(1, 4))
    by_side = jnp.where(chip_side == 0, by_side, by_side[:, ::-1])
    grad_gates = by_side.transpose(0, 2, 1).reshape(own_pad, experts)
    grad_logits = own_gates * (grad_gates - jnp.sum(own_gates * grad_gates, axis=1, keepdims=True))
    grad_logits = grad_logits.astype(BF)
    g_router = dot(grad_logits, route_normed, TN)
    grad_normed = dot(grad_logits, router, NT) + dot(back_hot_bf, grad_slots, NN)
    hat, scale = norm_parts(level_three)
    g_route_gain = jnp.sum(grad_normed * hat, axis=0)
    g_route_bias = jnp.sum(grad_normed, axis=0)
    grad_stream = grad_stream + norm_back(hat, scale, route_norm_gain, grad_normed)

    near_weighted = near(after(weighted, grad_stream))
    grad_stream, g_two, small_two = attend_backward(
        grad_stream, level_two, row(sparse_norm_gain), row(sparse_norm_bias), w_two, kept_two
    )
    near_weighted = after(near_weighted, g_two)
    far_weighted = far(*near_weighted)
    exp_from_y = after(exp_from_y, g_two)
    exp_from_y2 = hop(after(part_exp[2], g_two), "tp", 2)
    exp_give = plus(part_exp[1], exp_from_y)
    exp_away = hop(exp_give, "tp", 1)
    grad_stream, g_feed, small_feed = feed_backward(
        grad_stream, level_one, row(feed_norm_gain), row(feed_norm_bias), w_feed, kept_feed
    )
    far_weighted, exp_from_y2, exp_away = lax.optimization_barrier(
        ((far_weighted, exp_from_y2, exp_away), g_feed)
    )[0]
    exp_keep = plus(part_exp[0], exp_from_y2)
    keep_sum = jnp.where(same, exp_keep, exp_away)
    other_sum = hop(jnp.where(same, exp_away, exp_keep), "ep", 1)
    weighted_slots = jnp.concatenate([weighted, *near_weighted, far_weighted])
    level_four = level_three + dot(back_hot_bf, weighted_slots, NN)
    own_final = drop_pad(level_four.astype(BF))
    near_final = near(own_final)
    grad_stream = after(grad_stream, own_final)
    grad_stream, g_one, small_one = attend_backward(
        grad_stream, level_zero, row(dense_norm_gain), row(dense_norm_bias), w_one, kept_one
    )
    near_final = after(near_final, g_one)

    blank = jnp.zeros_like(small_exp)
    first = chip_side == 0
    small = jnp.concatenate(
        [
            small_one,
            small_feed,
            small_two,
            jnp.where(first, small_exp, blank),
            jnp.where(first, blank, small_exp),
            g_router,
            jnp.pad(jnp.stack([g_route_gain, g_route_bias]), ((0, 6), (0, 0))),
        ]
    )
    t_two, t_feed, t_one, ig_all, far_final, total, pair_total = tail(
        [g_two, g_feed, g_one], drop_pad(grad_stream.astype(BF)), *near_final, small, experts
    )
    input_grad = ig_all.reshape(rows_dev, depth).astype(F32)
    other_sum = after(other_sum, t_one)

    def absolute(blocks, kind):
        out = jnp.zeros((rows_dev, depth), kind)
        for r in range(shards):
            out = lax.dynamic_update_slice_in_dim(
                out, blocks[r].astype(kind), (mine ^ r) * own, axis=0
            )
        return out

    final = absolute([own_final, *near_final, far_final], BF)

    def attend_split(value):
        value = value.astype(F32)
        return (
            value[: 3 * width].reshape(3, width, depth).transpose(2, 0, 1),
            value[3 * width :],
        )

    t_exp_in = jnp.where(pair_side == 0, keep_sum, other_sum).astype(F32)
    t_exp_out = jnp.where(pair_side == 0, other_sum, keep_sum).astype(F32)
    t_in_two, t_out_two = attend_split(t_two)
    t_in_one, t_out_one = attend_split(t_one)
    t_feed = t_feed.astype(F32)

    def own_line(value, start):
        return lax.dynamic_slice_in_dim(value, start + mine, 1, axis=0)[0]

    def two_biases(start):
        line = own_line(total, start)
        return jnp.stack([line[:width], line[2 * width : 3 * width]])

    s_one, s_feed, s_two = total[0:8], total[8:16], total[16:24]
    s_exp = lax.dynamic_slice_in_dim(pair_total, 24 + 8 * pair_side, 8, axis=0)
    s_router = total[40 : 40 + experts].T
    s_route = total[40 + experts :]
    return (
        final,
        input_grad,
        s_one[0],
        s_one[1],
        t_in_one,
        two_biases(3),
        t_out_one,
        s_one[2],
        s_feed[0],
        s_feed[1],
        t_feed[:depth],
        own_line(total, 11),
        t_feed[depth:],
        s_feed[2],
        s_two[0],
        s_two[1],
        t_in_two,
        two_biases(19),
        t_out_two,
        s_two[2],
        s_route[0],
        s_route[1],
        s_router,
        t_exp_in[None],
        own_line(s_exp, 0)[None],
        t_exp_out[None],
        s_exp[4][None],
    )


def solution(mesh):
    in_specs = (
        P("ep", None),
        P("ep", None),
        P("ep", None),
        P("ep", None),
        P("ep", None),
        P(),
        P(),
        P(None, None, "tp"),
        P(None, "tp"),
        P("tp", None),
        P(),
        P(),
        P(),
        P(None, "tp"),
        P("tp"),
        P("tp", None),
        P(),
        P(),
        P(),
        P(None, None, "tp"),
        P(None, "tp"),
        P("tp", None),
        P(),
        P(),
        P(),
        P(),
        P("ep", None, "tp"),
        P("ep", "tp"),
        P("ep", "tp", None),
        P("ep", None),
    )
    out_specs = (
        P("ep", None),
        P("ep", None),
        P(),
        P(),
        P(None, None, "tp"),
        P(None, "tp"),
        P("tp", None),
        P(),
        P(),
        P(),
        P(None, "tp"),
        P("tp"),
        P("tp", None),
        P(),
        P(),
        P(),
        P(None, None, "tp"),
        P(None, "tp"),
        P("tp", None),
        P(),
        P(),
        P(),
        P(),
        P("ep", None, "tp"),
        P("ep", "tp"),
        P("ep", "tp", None),
        P("ep", None),
    )
    return jax.shard_map(body, mesh=mesh, in_specs=in_specs, out_specs=out_specs, check_vma=False)
```

```python
import jax
import jax.numpy as jnp
from jax import lax
from jax.experimental import pallas as pl
from jax.experimental.pallas import tpu as pltpu
from jax.sharding import PartitionSpec as P

HEAD = 64
LEN = 196
PAD = 208
EPSILON = 1e-06
BF = jnp.bfloat16
F32 = jnp.float32
NN = ((1,), (0,))
NT = ((1,), (1,))
TN = ((0,), (0,))
SQRT_HALF = 0.7071067811865476
VMEM_LIMIT = 60 * 1024 * 1024


def dot(a, b, dims):
    return lax.dot_general(a, b, (dims, ((), ())), preferred_element_type=F32)


def norm_parts(x):
    average = jnp.mean(x, axis=-1, keepdims=True)
    centred = x - average
    variance = jnp.mean(centred * centred, axis=-1, keepdims=True)
    scale = lax.rsqrt(variance + EPSILON)
    return centred * scale, scale


def norm_back(hat, scale, gain, grad):
    inner = grad * gain
    first = jnp.mean(inner, axis=-1, keepdims=True)
    second = jnp.mean(inner * hat, axis=-1, keepdims=True)
    return scale * (inner - first - hat * second)


def gelu_parts(u):
    z = jnp.abs(u) * SQRT_HALF
    t = 1.0 / (1.0 + 0.3275911 * z)
    bell = jnp.exp(-(z * z))
    poly = t * (
        0.254829592
        + t * (-0.284496736 + t * (1.421413741 + t * (-1.453152027 + t * 1.061405429)))
    )
    tail = 0.5 * poly * bell
    cdf = jnp.where(u >= 0.0, 1.0 - tail, tail)
    return u * cdf, cdf + u * (bell * 0.3989422804014327)


def whole():
    return pl.BlockSpec(memory_space=pltpu.VMEM)


def params(semantics=1):
    return pltpu.CompilerParams(
        dimension_semantics=("arbitrary",) * semantics, vmem_limit_bytes=VMEM_LIMIT
    )


def key_mask():
    rows = lax.broadcasted_iota(jnp.int32, (PAD, 1), 0)
    return jnp.where(rows < LEN, 0.0, -1e30)


def attend_backward_kernel(
    g_ref,
    h_ref,
    gain_ref,
    bias_ref,
    w_ref,
    qkv_ref,
    lse_ref,
    ctx_ref,
    gout_ref,
    dw_ref,
    small_ref,
    acc_ref,
    dqkv_ref,
    dc_ref,
    db_ref,
):
    step = pl.program_id(0)
    mine = lax.axis_index("tp")
    shards = w_ref.shape[0]
    width = w_ref.shape[1] // 4
    heads = width // HEAD

    @pl.when(step == 0)
    def _():
        acc_ref[...] = jnp.zeros_like(acc_ref)
        db_ref[...] = jnp.zeros_like(db_ref)
        small_ref[...] = jnp.zeros_like(small_ref)

    grad = g_ref[...]
    hat, scale = norm_parts(h_ref[...])
    a = (hat * gain_ref[...] + bias_ref[...]).astype(BF)
    gr = grad.astype(BF)
    mask = key_mask()
    da = jnp.zeros(grad.shape, F32)
    factor = HEAD**-0.5
    for r in range(shards):
        dc_ref[...] = dot(w_ref[r, 3 * width :, :], gr, NT).astype(BF)
        acc_ref[r, 3 * width :, :] += dot(ctx_ref[0, r], gr, NN)
        for h in range(heads):
            lo = HEAD * h
            q = qkv_ref[0, r, lo : lo + HEAD, :]
            k = qkv_ref[0, r, width + lo : width + lo + HEAD, :]
            v = qkv_ref[0, r, 2 * width + lo : 2 * width + lo + HEAD, :]
            dc = dc_ref[lo : lo + HEAD, :]
            s = dot(k, q, TN) * factor + mask
            p = jnp.exp(s - lse_ref[0, r, h : h + 1, :])
            pb = p.astype(BF)
            dp = dot(v, dc, TN)
            dv = dot(dc, pb, NT)
            pdp = p * dp
            delta = jnp.sum(pdp, axis=0, keepdims=True)
            ds = (pdp - p * delta).astype(BF)
            dq = dot(k, ds, NN) * factor
            dk = dot(q, ds, NT) * factor
            dqkv_ref[lo : lo + HEAD, :] = dq.astype(BF)
            dqkv_ref[width + lo : width + lo + HEAD, :] = dk.astype(BF)
            dqkv_ref[2 * width + lo : 2 * width + lo + HEAD, :] = dv.astype(BF)
        dqkv = dqkv_ref[...]
        acc_ref[r, : 3 * width, :] += dot(dqkv, a, NN)
        db_ref[r] += jnp.sum(dqkv.astype(F32), axis=1, keepdims=True)
        da += dot(dqkv, w_ref[r, : 3 * width, :], TN)
    gout_ref[...] = grad + norm_back(hat, scale, gain_ref[...], da)
    small_ref[0:1, :] += jnp.sum(da * hat, axis=0, keepdims=True)
    small_ref[1:2, :] += jnp.sum(da, axis=0, keepdims=True)
    small_ref[2:3, :] += jnp.sum(gr.astype(F32), axis=0, keepdims=True)

    @pl.when(step == pl.num_programs(0) - 1)
    def _():
        dw_ref[...] = acc_ref[...].astype(BF)
        for r in range(shards):
            line = jnp.transpose(jnp.broadcast_to(db_ref[r], (3 * width, 128)))[0:1, :]
            line = jnp.concatenate([line, jnp.zeros((1, width), F32)], axis=1)
            small_ref[pl.ds(3 + (mine ^ r), 1), :] = line


def attend_backward(grad, h, gain, bias, w, kept):
    qkv, lse, ctx = kept
    rows, depth = h.shape
    images = rows // PAD
    shards, four, _ = w.shape
    width = four // 4
    heads = width // HEAD
    row_block = pl.BlockSpec((PAD, depth), lambda i: (i, 0))
    flops = 2 * rows * depth * depth * 4 + 4 * rows * PAD * depth
    return pl.pallas_call(
        attend_backward_kernel,
        grid=(images,),
        in_specs=[
            row_block,
            row_block,
            whole(),
            whole(),
            whole(),
            pl.BlockSpec((1, shards, 3 * width, PAD), lambda i: (i, 0, 0, 0)),
            pl.BlockSpec((1, shards, heads, PAD), lambda i: (i, 0, 0, 0)),
            pl.BlockSpec((1, shards, width, PAD), lambda i: (i, 0, 0, 0)),
        ],
        out_specs=[row_block, whole(), whole()],
        out_shape=[
            jax.ShapeDtypeStruct((rows, depth), F32),
            jax.ShapeDtypeStruct((shards, four, depth), BF),
            jax.ShapeDtypeStruct((8, depth), F32),
        ],
        scratch_shapes=[
            pltpu.VMEM((shards, four, depth), F32),
            pltpu.VMEM((3 * width, PAD), BF),
            pltpu.VMEM((width, PAD), BF),
            pltpu.VMEM((shards, 3 * width, 1), F32),
        ],
        compiler_params=params(),
        cost_estimate=pl.CostEstimate(
            flops=flops * 6, bytes_accessed=30_000_000, transcendentals=rows * PAD * 12
        ),
        name="attend_backward",
    )(grad, h, gain, bias, w, qkv, lse, ctx)


def feed_backward_kernel(
    g_ref,
    h_ref,
    gain_ref,
    bias_ref,
    w_ref,
    hid_ref,
    slope_ref,
    gout_ref,
    dw_ref,
    small_ref,
    m_ref,
    gr_ref,
    dm_ref,
):
    step = pl.program_id(0)
    depth = h_ref.shape[1]
    mine = lax.axis_index("tp")

    @pl.when(step == 0)
    def _():
        hat, _ = norm_parts(h_ref[...])
        m_ref[...] = (hat * gain_ref[...] + bias_ref[...]).astype(BF)
        gr_ref[...] = g_ref[...].astype(BF)
        dm_ref[...] = jnp.zeros_like(dm_ref)

    gr = gr_ref[...]
    dw_ref[0, depth:, :] = dot(hid_ref[0], gr, TN).astype(BF)
    dr = dot(gr, w_ref[0, depth:, :], NT)
    du = (slope_ref[0].astype(F32) * dr).astype(BF)
    small_ref[pl.ds(3 + (mine ^ step), 1), :] = jnp.sum(du.astype(F32), axis=0, keepdims=True)
    dw_ref[0, :depth, :] = dot(m_ref[...], du, TN).astype(BF)
    dm_ref[...] += dot(du, w_ref[0, :depth, :], NT)

    @pl.when(step == pl.num_programs(0) - 1)
    def _():
        hat, scale = norm_parts(h_ref[...])
        dm = dm_ref[...]
        gout_ref[...] = g_ref[...] + norm_back(hat, scale, gain_ref[...], dm)
        small_ref[0:1, :] = jnp.sum(dm * hat, axis=0, keepdims=True)
        small_ref[1:2, :] = jnp.sum(dm, axis=0, keepdims=True)
        small_ref[2:3, :] = jnp.sum(gr_ref[...].astype(F32), axis=0, keepdims=True)
        small_ref[7:8, :] = jnp.zeros((1, depth), F32)


def feed_backward(grad, h, gain, bias, w, kept):
    hid, slope = kept
    rows, depth = h.shape
    shards, double, hidden = w.shape
    shard = lambda i: (i, 0, 0)
    return pl.pallas_call(
        feed_backward_kernel,
        grid=(shards,),
        in_specs=[
            whole(),
            whole(),
            whole(),
            whole(),
            pl.BlockSpec((1, double, hidden), shard),
            pl.BlockSpec((1, rows, hidden), shard),
            pl.BlockSpec((1, rows, hidden), shard),
        ],
        out_specs=[
            whole(),
            pl.BlockSpec((1, double, hidden), shard),
            whole(),
        ],
        out_shape=[
            jax.ShapeDtypeStruct((rows, depth), F32),
            jax.ShapeDtypeStruct((shards, double, hidden), BF),
            jax.ShapeDtypeStruct((8, depth), F32),
        ],
        scratch_shapes=[
            pltpu.VMEM((rows, depth), BF),
            pltpu.VMEM((rows, depth), BF),
            pltpu.VMEM((rows, depth), F32),
        ],
        compiler_params=params(),
        cost_estimate=pl.CostEstimate(
            flops=8 * rows * depth * hidden * shards * 2,
            bytes_accessed=35_000_000,
            transcendentals=0,
        ),
        name="feed_backward",
    )(grad, h, gain, bias, w, hid, slope)


def expert_pair(mine_ref, other_ref):
    first = lax.rem(lax.axis_index("ep"), 2) == 0
    mine, other = mine_ref[0], other_ref[0]
    return jnp.where(first, mine, other), jnp.where(first, other, mine)


def expert_forward_kernel(x_ref, mine_ref, other_ref, b1_ref, b2_ref, y_ref, hid_ref, slope_ref, acc_ref):
    r = pl.program_id(0)

    @pl.when(r == 0)
    def _():
        acc_ref[...] = jnp.zeros_like(acc_ref)

    w_in, w_out = expert_pair(mine_ref, other_ref)
    u = dot(x_ref[...], w_in, NN) + b1_ref[0]
    value, slope = gelu_parts(u)
    value = value.astype(BF)
    hid_ref[0] = value
    slope_ref[0] = slope.astype(BF)
    acc_ref[...] += dot(value, w_out, NN)

    @pl.when(r == pl.num_programs(0) - 1)
    def _():
        y_ref[...] = (acc_ref[...] + b2_ref[...]).astype(BF)


def expert_forward(x, mine, other, b1, b2):
    rows, depth = x.shape
    shards, _, hidden = mine.shape
    shard = lambda r: (r, 0, 0)
    wide = pl.BlockSpec((1, rows, hidden), shard)
    weight = pl.BlockSpec((1, depth, hidden), shard)
    return pl.pallas_call(
        expert_forward_kernel,
        grid=(shards,),
        in_specs=[whole(), weight, weight, pl.BlockSpec((1, 1, hidden), shard), whole()],
        out_specs=[whole(), wide, wide],
        out_shape=[
            jax.ShapeDtypeStruct((rows, depth), BF),
            jax.ShapeDtypeStruct((shards, rows, hidden), BF),
            jax.ShapeDtypeStruct((shards, rows, hidden), BF),
        ],
        scratch_shapes=[pltpu.VMEM((rows, depth), F32)],
        compiler_params=params(),
        cost_estimate=pl.CostEstimate(
            flops=4 * rows * depth * hidden * shards * 2,
            bytes_accessed=25_000_000,
            transcendentals=rows * hidden * shards,
        ),
        name="expert_forward",
    )(x, mine, other, b1, b2)


def expert_input_kernel(
    y_ref,
    cot_ref,
    gate_ref,
    mine_ref,
    other_ref,
    slope_ref,
    wy_ref,
    dy_ref,
    dx_ref,
    dgate_ref,
    du_ref,
    small_ref,
    acc_ref,
):
    r = pl.program_id(0)
    mine = lax.axis_index("tp")

    @pl.when(r == 0)
    def _():
        y = y_ref[...].astype(F32)
        cot = cot_ref[...].astype(F32)
        gate = gate_ref[...]
        dgate_ref[...] = jnp.sum(cot * y, axis=1, keepdims=True)
        wy_ref[...] = (gate * y).astype(BF)
        dy = (gate * cot).astype(BF)
        dy_ref[...] = dy
        small_ref[4:5, :] = jnp.sum(dy.astype(F32), axis=0, keepdims=True)
        small_ref[5:8, :] = jnp.zeros((3, dy.shape[1]), F32)
        acc_ref[...] = jnp.zeros_like(acc_ref)

    w_in, w_out = expert_pair(mine_ref, other_ref)
    dr = dot(dy_ref[...], w_out, NT)
    du = (slope_ref[0].astype(F32) * dr).astype(BF)
    du_ref[0] = du
    small_ref[pl.ds(mine ^ r, 1), :] = jnp.sum(du.astype(F32), axis=0, keepdims=True)
    acc_ref[...] += dot(du, w_in, NT)

    @pl.when(r == pl.num_programs(0) - 1)
    def _():
        dx_ref[...] = acc_ref[...].astype(BF)


def expert_input(y, cot, gate, mine, other, slope):
    rows, depth = y.shape
    shards, _, hidden = mine.shape
    shard = lambda r: (r, 0, 0)
    wide = pl.BlockSpec((1, rows, hidden), shard)
    weight = pl.BlockSpec((1, depth, hidden), shard)
    return pl.pallas_call(
        expert_input_kernel,
        grid=(shards,),
        in_specs=[whole(), whole(), whole(), weight, weight, wide],
        out_specs=[
            whole(),
            whole(),
            whole(),
            whole(),
            wide,
            whole(),
        ],
        out_shape=[
            jax.ShapeDtypeStruct((rows, depth), BF),
            jax.ShapeDtypeStruct((rows, depth), BF),
            jax.ShapeDtypeStruct((rows, depth), BF),
            jax.ShapeDtypeStruct((rows, 1), F32),
            jax.ShapeDtypeStruct((shards, rows, hidden), BF),
            jax.ShapeDtypeStruct((8, depth), F32),
        ],
        scratch_shapes=[pltpu.VMEM((rows, depth), F32)],
        compiler_params=params(),
        cost_estimate=pl.CostEstimate(
            flops=4 * rows * depth * hidden * shards * 2,
            bytes_accessed=25_000_000,
            transcendentals=0,
        ),
        name="expert_input",
    )(y, cot, gate, mine, other, slope)


def expert_return_kernel(
    size,
    x_ref,
    dy_ref,
    hid_ref,
    du_ref,
    sent_ref,
    y_ref,
    dw_ref,
    out_ref,
    y_out,
    stage_ref,
    came_ref,
    swap_send,
    swap_recv,
    pass_send,
    pass_recv,
    y_send,
    y_recv,
    core_send,
    core_recv,
    local_sem,
):
    step = pl.program_id(0)
    depth = x_ref.shape[1]
    mine = lax.axis_index("tp")
    place = lax.axis_index("ep")
    to_x = {"tp": mine ^ 1}
    to_y = {"tp": mine ^ 2}

    def remote(src, dst, sends, recvs, index, peer):
        return pltpu.make_async_remote_copy(
            src_ref=src,
            dst_ref=dst,
            send_sem=sends.at[index],
            recv_sem=recvs.at[index],
            device_id=peer,
            device_id_type=pl.DeviceIdType.MESH,
        )

    def exchange(k):
        peer = place ^ k
        return remote(
            sent_ref.at[peer], out_ref.at[0, place], swap_send, swap_recv, k, {"ep": peer}
        )

    def keep():
        return pltpu.make_async_copy(sent_ref.at[place], out_ref.at[0, place], local_sem.at[0])

    def y_exchange(k):
        peer = place ^ k
        return remote(y_ref.at[peer], y_out.at[place], y_send, y_recv, k, {"ep": peer})

    def y_keep():
        return pltpu.make_async_copy(y_ref.at[place], y_out.at[place], local_sem.at[1])

    core = lax.rem(place, 2)
    own_half = pl.ds(pl.multiple_of(core * depth, depth), depth)
    other_half = pl.ds(pl.multiple_of((1 - core) * depth, depth), depth)

    def give(r):
        return remote(
            stage_ref.at[r, other_half], came_ref.at[r], core_send, core_recv, r, {"ep": place ^ 1}
        )

    def save(r):
        return pltpu.make_async_copy(stage_ref.at[r, own_half], dw_ref.at[r], local_sem.at[2 + r])

    def along(k, way):
        slab = place ^ k
        return remote(
            out_ref.at[0, slab],
            out_ref.at[1 + way, slab],
            pass_send,
            pass_recv,
            (way, k),
            (to_x, to_y)[way],
        )

    def relay(k):
        slab = place ^ k
        way = k % 2
        return remote(
            out_ref.at[1 + way, slab],
            out_ref.at[3, slab],
            pass_send,
            pass_recv,
            (2, k),
            (to_y, to_x)[way],
        )

    def forward(group):
        for k in range(size // 4 * group, size // 4 * (group + 1)):
            if k == 0:
                keep().wait()
            else:
                exchange(k).wait_recv()
            along(k, 0).start()
            along(k, 1).start()

    @pl.when(step == 0)
    def _():
        barrier = pltpu.get_barrier_semaphore()
        for peer in [to_x, to_y] + [{"ep": place ^ k} for k in range(1, size)]:
            pl.semaphore_signal(barrier, inc=1, device_id=peer, device_id_type=pl.DeviceIdType.MESH)
        pl.semaphore_wait(barrier, size + 1)
        keep().start()
        for k in range(1, size):
            exchange(k).start()

    for group in range(3):

        @pl.when(step == group + 1)
        def _(group=group):
            forward(group)

    @pl.when(step == 2)
    def _():
        y_keep().start()
        for k in range(1, size):
            y_exchange(k).start()

    stage_ref[step, depth:, :] = dot(hid_ref[0], dy_ref[...], TN).astype(BF)
    stage_ref[step, :depth, :] = dot(x_ref[...], du_ref[0], TN).astype(BF)
    for r in range(stage_ref.shape[0]):

        @pl.when(step == r)
        def _(r=r):
            give(r).start()

    @pl.when(step == 3)
    def _():
        forward(3)
        for r in range(stage_ref.shape[0]):
            give(r).wait_recv()
            add_rows(stage_ref.at[r, own_half], came_ref.at[r], depth)
            save(r).start()
        for k in range(size):
            along(k, k % 2).wait_recv()
            relay(k).start()
        y_keep().wait()
        for k in range(1, size):
            y_exchange(k).wait_recv()
            y_exchange(k).wait_send()
        for r in range(stage_ref.shape[0]):
            give(r).wait_send()
            save(r).wait()
        for k in range(size):
            along(k, 1 - k % 2).wait_recv()
            relay(k).wait_recv()
        for k in range(size):
            if k > 0:
                exchange(k).wait_send()
            along(k, 0).wait_send()
            along(k, 1).wait_send()
            relay(k).wait_send()


def expert_return(x, dy, hid, du, sent, y):
    rows, depth = x.shape
    shards, _, hidden = hid.shape
    size = sent.shape[0]
    shard = lambda r: (r, 0, 0)
    wide = pl.BlockSpec((1, rows, hidden), shard)
    any_spec = pl.BlockSpec(memory_space=pl.ANY)
    return pl.pallas_call(
        lambda *refs: expert_return_kernel(size, *refs),
        grid=(shards,),
        in_specs=[whole(), whole(), wide, wide, any_spec, any_spec],
        out_specs=[any_spec] * 3,
        out_shape=[
            jax.ShapeDtypeStruct((shards, depth, hidden), BF),
            jax.ShapeDtypeStruct((shards,) + sent.shape, BF),
            jax.ShapeDtypeStruct(y.shape, BF),
        ],
        scratch_shapes=[
            pltpu.VMEM((shards, 2 * depth, hidden), BF),
            pltpu.VMEM((shards, depth, hidden), BF),
            pltpu.SemaphoreType.DMA((size,)),
            pltpu.SemaphoreType.DMA((size,)),
            pltpu.SemaphoreType.DMA((3, size)),
            pltpu.SemaphoreType.DMA((3, size)),
            pltpu.SemaphoreType.DMA((size,)),
            pltpu.SemaphoreType.DMA((size,)),
            pltpu.SemaphoreType.DMA((shards,)),
            pltpu.SemaphoreType.DMA((shards,)),
            pltpu.SemaphoreType.DMA((2 + shards,)),
        ],
        compiler_params=pltpu.CompilerParams(
            dimension_semantics=("arbitrary",),
            vmem_limit_bytes=VMEM_LIMIT,
            collective_id=2,
            has_side_effects=True,
        ),
        cost_estimate=pl.CostEstimate(
            flops=4 * rows * depth * hidden * shards * 2,
            bytes_accessed=40_000_000,
            transcendentals=0,
        ),
        name="expert_return",
    )(x, dy, hid, du, sent, y)


ROUTES = 6


def attend_image(x, gain, bias, w_ref, biases_ref, bias_row, bout, qkv_ref, lse_ref, ctx_ref):
    shards = w_ref.shape[0]
    width = w_ref.shape[1] // 4
    heads = width // HEAD
    hat, _ = norm_parts(x)
    a = (hat * gain + bias).astype(BF)
    mask = key_mask()
    branch = jnp.zeros(x.shape, F32)
    for r in range(shards):
        column = jnp.transpose(biases_ref[r])[: 3 * width, bias_row : bias_row + 1]
        qkv = (dot(w_ref[r, : 3 * width, :], a, NT) + column).astype(BF)
        qkv_ref[0, r] = qkv
        for h in range(heads):
            q = qkv[HEAD * h : HEAD * (h + 1)]
            k = qkv[width + HEAD * h : width + HEAD * (h + 1)]
            v = qkv[2 * width + HEAD * h : 2 * width + HEAD * (h + 1)]
            s = dot(k, q, TN) * (HEAD**-0.5) + mask
            peak = jnp.max(s, axis=0, keepdims=True)
            e = jnp.exp(s - peak)
            total = jnp.sum(e, axis=0, keepdims=True)
            lse_ref[0, r, h : h + 1, :] = peak + jnp.log(total)
            c = dot(v, e.astype(BF), NN) * (1.0 / total)
            ctx_ref[0, r, HEAD * h : HEAD * (h + 1), :] = c.astype(BF)
        branch += dot(ctx_ref[0, r], w_ref[r, 3 * width :, :], TN)
    return x + branch + bout


def forward_kernel(
    x_ref,
    vec_ref,
    bias_ref,
    one_ref,
    feed_ref,
    two_ref,
    h1_ref,
    h2_ref,
    h3_ref,
    qkv1_ref,
    lse1_ref,
    ctx1_ref,
    hid_ref,
    slope_ref,
    qkv2_ref,
    lse2_ref,
    ctx2_ref,
    w1_out,
    wf_out,
    w2_out,
    normed_out,
    biases_out,
    h_ref,
    w1_ref,
    wf_ref,
    w2_ref,
    b_ref,
    n_ref,
    send_sem,
    recv_sem,
    n_send,
    n_recv,
    small_send,
    small_recv,
    local_sem,
):
    step = pl.program_id(0)
    images = 4
    mine = lax.axis_index("tp")
    place = lax.axis_index("ep")
    core = lax.rem(place, 2)
    side = lax.rem(mine, 2)
    to_x = {"tp": mine ^ 1}
    to_y = {"tp": mine ^ 2}
    to_far = {"tp": mine ^ 3}
    to_core = {"ep": place ^ 1}
    depth = x_ref.shape[1]

    def remote(src, dst, sends, recvs, index, peer):
        return pltpu.make_async_remote_copy(
            src_ref=src,
            dst_ref=dst,
            send_sem=sends.at[index],
            recv_sem=recvs.at[index],
            device_id=peer,
            device_id_type=pl.DeviceIdType.MESH,
        )

    def copies(group, own, full):
        rows = own.shape[0] // 2
        start = pl.multiple_of(core * rows, rows)
        quarter = rows // 2
        middle = pl.multiple_of(start + quarter, quarter)
        half = pl.ds(start, rows)
        low = pl.ds(start, quarter)
        high = pl.ds(middle, quarter)

        def make(k, src, dst, peer):
            return remote(src, dst, send_sem, recv_sem, (group, k), peer)

        return [
            make(0, own.at[half], full.at[1, half], to_x),
            make(1, own.at[half], full.at[2, half], to_y),
            make(2, full.at[1, low], full.at[3, low], to_y),
            make(3, full.at[2, high], full.at[3, high], to_x),
            make(4, full.at[pl.ds(1, 2), half], full.at[pl.ds(1, 2), half], to_core),
            make(5, full.at[3, half], full.at[3, half], to_core),
        ]

    one = copies(0, one_ref, w1_ref)
    feed = copies(1, feed_ref, wf_ref)
    two = copies(2, two_ref, w2_ref)

    small = [
        remote(bias_ref, b_ref.at[r], small_send, small_recv, r - 1, peer)
        for r, peer in ((1, to_x), (2, to_y), (3, to_far))
    ]
    own_local = [
        pltpu.make_async_copy(one_ref, w1_ref.at[0], local_sem.at[0]),
        pltpu.make_async_copy(feed_ref, wf_ref.at[0], local_sem.at[1]),
        pltpu.make_async_copy(two_ref, w2_ref.at[0], local_sem.at[2]),
    ]
    saves = [
        pltpu.make_async_copy(w1_ref, w1_out, local_sem.at[4]),
        pltpu.make_async_copy(wf_ref, wf_out, local_sem.at[5]),
        pltpu.make_async_copy(w2_ref, w2_out, local_sem.at[6]),
    ]

    def rows_copy(i):
        rows = pl.ds(PAD * i, PAD)
        low, high = pl.ds(PAD * i, 96), pl.ds(PAD * i + 96, PAD - 96)
        return [
            remote(n_ref.at[i], normed_out.at[1, rows], n_send, n_recv, (0, i), to_x),
            remote(n_ref.at[i], normed_out.at[2, rows], n_send, n_recv, (1, i), to_y),
            remote(normed_out.at[1, low], normed_out.at[3, low], n_send, n_recv, (2, i), to_y),
            remote(normed_out.at[2, high], normed_out.at[3, high], n_send, n_recv, (3, i), to_x),
            pltpu.make_async_copy(n_ref.at[i], normed_out.at[0, rows], local_sem.at[8 + i]),
        ]

    def vec(k):
        return vec_ref[k : k + 1, :]

    @pl.when(step == 0)
    def _():
        barrier = pltpu.get_barrier_semaphore()
        for peer in (to_x, to_y, to_far, to_core):
            pl.semaphore_signal(barrier, inc=1, device_id=peer, device_id_type=pl.DeviceIdType.MESH)
        pl.semaphore_wait(barrier, 4)
        one[0].start()
        one[1].start()
        own_local[0].start()
        for copy in small:
            copy.start()
        b_ref[0] = bias_ref[...]
        one[0].wait_recv()
        one[1].wait_recv()
        one[2].start()
        one[3].start()
        one[4].start()
        feed[0].start()
        feed[1].start()
        one[2].wait_recv()
        one[3].wait_recv()
        one[5].start()
        own_local[1].start()
        own_local[2].start()
        own_local[0].wait()
        for copy in small:
            copy.wait_recv()
        one[4].wait_recv()
        one[5].wait_recv()

    @pl.when(step == 2)
    def _():
        saves[0].start()
        feed[0].wait_recv()
        feed[1].wait_recv()
        feed[2].start()
        feed[3].start()
        feed[4].start()

    @pl.when(step == 4)
    def _():
        feed[2].wait_recv()
        feed[3].wait_recv()
        feed[5].start()
        two[0].start()
        two[1].start()
        own_local[1].wait()
        feed[4].wait_recv()
        feed[5].wait_recv()

    @pl.when(step == 6)
    def _():
        saves[1].start()
        two[0].wait_recv()
        two[1].wait_recv()
        two[2].start()
        two[3].start()
        two[4].start()

    @pl.when(step == 7)
    def _():
        two[2].wait_recv()
        two[3].wait_recv()
        two[5].start()

    @pl.when(step == 8)
    def _():
        own_local[2].wait()
        two[4].wait_recv()
        two[5].wait_recv()

    @pl.when(step == 10)
    def _():
        saves[2].start()

    @pl.when(step < images)
    def _():
        x = x_ref[pl.ds(pl.multiple_of(step * PAD, PAD), PAD), :].astype(F32)
        h = attend_image(
            x, vec(0), vec(1), w1_ref, b_ref, 0, vec(2), qkv1_ref, lse1_ref, ctx1_ref
        )
        h_ref[step] = h
        h1_ref[...] = h

    @pl.when((step >= images) & (step < 2 * images))
    def _():
        tile = step - images
        x = h_ref[tile]
        hat, _ = norm_parts(x)
        m = (hat * vec(3) + vec(4)).astype(BF)
        acc = x + vec(5)
        for r in range(wf_ref.shape[0]):
            u = dot(m, wf_ref[r, :depth, :], NN) + b_ref[r, 2:3, :]
            value, slope = gelu_parts(u)
            value = value.astype(BF)
            hid_ref[r] = value
            slope_ref[r] = slope.astype(BF)
            acc += dot(value, wf_ref[r, depth:, :], NN)
        h_ref[tile] = acc
        h2_ref[...] = acc

    @pl.when(step >= 2 * images)
    def _():
        image = step - 2 * images
        h = attend_image(
            h_ref[image], vec(6), vec(7), w2_ref, b_ref, 1, vec(8), qkv2_ref, lse2_ref, ctx2_ref
        )
        h3_ref[...] = h
        hat, _ = norm_parts(h)
        n_ref[image] = (hat * vec(9) + vec(10)).astype(BF)

    for i in range(images):

        @pl.when(step == 2 * images + i)
        def _(i=i):
            to_send = rows_copy(i)
            to_send[0].start()
            to_send[1].start()
            to_send[4].start()
            if i > 0:
                before = rows_copy(i - 1)
                before[0].wait_recv()
                before[1].wait_recv()
                before[2].start()
                before[3].start()

    @pl.when(step == 3 * images - 1)
    def _():
        last = rows_copy(images - 1)
        last[0].wait_recv()
        last[1].wait_recv()
        last[2].start()
        last[3].start()
        pltpu.make_async_copy(b_ref, biases_out, local_sem.at[7]).start()
        for i in range(images):
            moved = rows_copy(i)
            moved[2].wait_recv()
            moved[3].wait_recv()
            for k in range(4):
                moved[k].wait_send()
            moved[4].wait()
        for group in (one, feed, two):
            for copy in group:
                copy.wait_send()
        for copy in small:
            copy.wait_send()
        for copy in saves:
            copy.wait()
        pltpu.make_async_copy(b_ref, biases_out, local_sem.at[7]).wait()


def dense_forward(x, vectors, bias, pack_one, pack_feed, pack_two):
    rows, depth = x.shape
    images = rows // PAD
    shards = 4
    four = pack_one.shape[0]
    width = four // 4
    heads = width // HEAD
    double, hidden = pack_feed.shape
    any_spec = pl.BlockSpec(memory_space=pl.ANY)

    def part(number):
        return lambda s: jnp.clip(s - images * number, 0, images - 1)

    def row_spec(number):
        at = part(number)
        return pl.BlockSpec((PAD, depth), lambda s: (at(s), 0))

    def attend_specs(number):
        at = part(number)
        return [
            pl.BlockSpec((1, shards, 3 * width, PAD), lambda s: (at(s), 0, 0, 0)),
            pl.BlockSpec((1, shards, heads, PAD), lambda s: (at(s), 0, 0, 0)),
            pl.BlockSpec((1, shards, width, PAD), lambda s: (at(s), 0, 0, 0)),
        ]

    tile_at = part(1)
    hid_spec = pl.BlockSpec((shards, PAD, hidden), lambda s: (0, tile_at(s), 0))
    shape = jax.ShapeDtypeStruct
    attend_shapes = [
        shape((images, shards, 3 * width, PAD), BF),
        shape((images, shards, heads, PAD), F32),
        shape((images, shards, width, PAD), BF),
    ]
    out = pl.pallas_call(
        forward_kernel,
        grid=(3 * images,),
        in_specs=[whole(), whole(), whole()] + [any_spec] * 3,
        out_specs=[row_spec(0), row_spec(1), row_spec(2)]
        + attend_specs(0)
        + [hid_spec, hid_spec]
        + attend_specs(2)
        + [any_spec] * 5,
        out_shape=[shape((rows, depth), F32)] * 3
        + attend_shapes
        + [shape((shards, rows, hidden), BF)] * 2
        + attend_shapes
        + [
            shape((shards, four, depth), BF),
            shape((shards, double, hidden), BF),
            shape((shards, four, depth), BF),
            shape((shards, rows, depth), BF),
            shape((shards, 8, depth), F32),
        ],
        scratch_shapes=[
            pltpu.VMEM((images, PAD, depth), F32),
            pltpu.VMEM((shards, four, depth), BF),
            pltpu.VMEM((shards, double, hidden), BF),
            pltpu.VMEM((shards, four, depth), BF),
            pltpu.VMEM((shards, 8, depth), F32),
            pltpu.VMEM((images, PAD, depth), BF),
            pltpu.SemaphoreType.DMA((3, ROUTES)),
            pltpu.SemaphoreType.DMA((3, ROUTES)),
            pltpu.SemaphoreType.DMA((4, 4)),
            pltpu.SemaphoreType.DMA((4, 4)),
            pltpu.SemaphoreType.DMA((3,)),
            pltpu.SemaphoreType.DMA((3,)),
            pltpu.SemaphoreType.DMA((12,)),
        ],
        compiler_params=pltpu.CompilerParams(
            dimension_semantics=("arbitrary",),
            vmem_limit_bytes=VMEM_LIMIT,
            collective_id=0,
            has_side_effects=True,
        ),
        cost_estimate=pl.CostEstimate(
            flops=60_000_000_000, bytes_accessed=60_000_000, transcendentals=10_000_000
        ),
        name="dense_forward",
    )(x, vectors, bias, pack_one, pack_feed, pack_two)
    (h1, h2, h3, q1, l1, c1, hid, slope, q2, l2, c2, w1, wf, w2, normed, biases) = out
    return (h1, h2, h3), (q1, l1, c1), (hid, slope), (q2, l2, c2), (w1, wf, w2), normed, biases


TAIL_ORDER = (0, 3, 0, 1, 1, 0, 2, 3, 0, 1, 0, 2, 1, 3, 0, 2, 0, 1, 2, 4, 0, 1, 2, 3, 1, 2, 4, 1, 2, 0, 3, 1, 2, 4)


def add_rows(dst, src, rows):
    tile = 48

    def body(i, carry):
        at = pl.ds(pl.multiple_of(i * tile, 16), tile)
        dst[at] = (dst[at].astype(F32) + src[at].astype(F32)).astype(BF)
        return carry

    lax.fori_loop(0, rows // tile, body, 0)


def plane_bits(size):
    return [1 << k for k in range(1, size.bit_length() - 1)]


def halvings(rows, bits):
    count = 0
    while count < len(bits) and rows % 32 == 0:
        rows //= 2
        count += 1
    return count


def tail_kernel(size, rows_list, *refs):
    groups = len(rows_list)
    bits = plane_bits(size)
    take = iter(refs)
    sources = [next(take) for _ in range(groups)]
    ig_ref, act_x, act_y, small_ref = [next(take) for _ in range(4)]
    outs = [next(take) for _ in range(groups)]
    ig_out, act_out, total_ref, pair_ref = [next(take) for _ in range(4)]
    keeps = [next(take) for _ in range(groups)]
    cores = [next(take) for _ in range(groups)]
    firsts = [next(take) for _ in range(groups)]
    seconds = [next(take) for _ in range(groups)]
    planes = [next(take) for _ in range(groups)]
    halves = [next(take) for _ in range(groups)]
    landed = next(take)
    send_sem, recv_sem, local_sem, ig_send, ig_recv, small_send, small_recv = take

    mine = lax.axis_index("tp")
    place = lax.axis_index("ep")
    core = lax.rem(place, 2)
    to_x = {"tp": mine ^ 1}
    to_y = {"tp": mine ^ 2}
    to_core = {"ep": place ^ 1}
    to_plane = [{"ep": place ^ bit} for bit in bits]

    barrier = pltpu.get_barrier_semaphore()
    for peer in [to_x, to_y, to_core] + to_plane:
        pl.semaphore_signal(barrier, inc=1, device_id=peer, device_id_type=pl.DeviceIdType.MESH)
    pl.semaphore_wait(barrier, 3 + len(bits))

    def remote(src, dst, sends, recvs, index, peer):
        return pltpu.make_async_remote_copy(
            src_ref=src,
            dst_ref=dst,
            send_sem=sends.at[index],
            recv_sem=recvs.at[index],
            device_id=peer,
            device_id_type=pl.DeviceIdType.MESH,
        )

    def group_steps(g):
        rows = rows_list[g]
        half, quarter = rows // 2, rows // 4
        source, keep, came, first, second = sources[g], keeps[g], cores[g], firsts[g], seconds[g]
        plane, out, whole_half = planes[g], outs[g], halves[g]
        own_half = pl.ds(pl.multiple_of(core * half, half), half)
        other_half = pl.ds(pl.multiple_of((1 - core) * half, half), half)
        number = iter(range(100))
        sent = []

        def send(src, dst, peer):
            copy = remote(src, dst, send_sem, recv_sem, (g, next(number)), peer)
            copy.start()
            sent.append(copy)
            return copy

        every = pl.ds(0, keep.shape[0])
        local = pltpu.make_async_copy(source.at[every, own_half], keep, local_sem.at[g])
        local.start()
        swap = send(source.at[every, other_half], came, to_core)
        yield
        local.wait()
        swap.wait_recv()
        for r in range(keep.shape[0]):
            add_rows(keep.at[r], came.at[r], half)
        low, high = pl.ds(0, quarter), pl.ds(quarter, quarter)
        waits = [
            send(keep.at[1, low], first.at[0], to_x),
            send(keep.at[3, low], first.at[1], to_x),
            send(keep.at[pl.ds(2, 2), high], first.at[pl.ds(2, 2)], to_y),
        ]
        yield
        for copy in waits:
            copy.wait_recv()
        add_rows(keep.at[2, low], first.at[1], quarter)
        add_rows(keep.at[1, high], first.at[3], quarter)
        waits = [
            send(keep.at[2, low], second.at[0], to_y),
            send(keep.at[1, high], second.at[1], to_x),
        ]
        add_rows(keep.at[0, low], first.at[0], quarter)
        add_rows(keep.at[0, high], first.at[2], quarter)
        yield
        for copy in waits:
            copy.wait_recv()
        add_rows(keep.at[0, low], second.at[0], quarter)
        add_rows(keep.at[0, high], second.at[1], quarter)
        start, length, done = 0, half, []
        offset = 0
        for k, bit in enumerate(bits):
            if k < halvings(half, bits):
                length //= 2
                side = lax.rem(place // bit, 2)
                mine_at = pl.ds(pl.multiple_of(start + side * length, 16), length)
                give_at = pl.ds(pl.multiple_of(start + (1 - side) * length, 16), length)
                land = plane.at[pl.ds(offset, length)]
                copy = send(keep.at[0, give_at], land, to_plane[k])
                done.append((mine_at, k))
                start = start + side * length
            else:
                mine_at = pl.ds(pl.multiple_of(start + 0 * place, 16), length)
                land = plane.at[pl.ds(offset, length)]
                copy = send(keep.at[0, mine_at], land, to_plane[k])
            yield
            copy.wait_recv()
            if k >= halvings(half, bits):
                copy.wait_send()
                sent.pop()
            add_rows(keep.at[0, mine_at], land, length)
            offset += length
        at = done[-1][0]
        whole_half[at] = keep[0, at, :]
        for at, k in done[::-1]:
            copy = send(whole_half.at[at], whole_half.at[at], to_plane[k])
            yield
            copy.wait_recv()
        copy = send(whole_half, out.at[own_half], to_core)
        local = pltpu.make_async_copy(whole_half, out.at[own_half], local_sem.at[groups + g])
        local.start()
        yield
        copy.wait_recv()
        local.wait()
        for copy in sent:
            copy.wait_send()

    def ig_steps():
        half = ig_ref.shape[0] // 32 * 16
        low, high = pl.ds(0, half), pl.ds(half, ig_ref.shape[0] - half)
        near = [
            remote(ig_ref, ig_out.at[mine], ig_send, ig_recv, 0, to_x),
            remote(ig_ref, ig_out.at[mine], ig_send, ig_recv, 1, to_y),
        ]
        local = pltpu.make_async_copy(ig_ref, ig_out.at[mine], local_sem.at[2 * groups])
        local.start()
        for copy in near:
            copy.start()
        yield
        passed = [
            remote(act_x.at[low], act_out.at[low], ig_send, ig_recv, 4, to_y),
            remote(act_y.at[high], act_out.at[high], ig_send, ig_recv, 5, to_x),
        ]
        for copy in passed:
            copy.start()
        for copy in near:
            copy.wait_recv()
        relay = [
            remote(ig_out.at[mine ^ 1, low], ig_out.at[mine ^ 1, low], ig_send, ig_recv, 2, to_y),
            remote(ig_out.at[mine ^ 2, high], ig_out.at[mine ^ 2, high], ig_send, ig_recv, 3, to_x),
        ]
        for copy in relay:
            copy.start()
        yield
        for copy in relay:
            copy.wait_recv()
        for copy in passed:
            copy.wait_recv()
        for copy in near + relay + passed:
            copy.wait_send()
        local.wait()

    def small_steps():
        total_ref[...] = small_ref[...]
        peers = [to_x, to_y, to_core] + to_plane
        for k, peer in enumerate(peers):
            copy = remote(total_ref, landed.at[k], small_send, small_recv, k, peer)
            copy.start()
            yield
            copy.wait()
            total_ref[...] += landed[k]
            if k == 2:
                pair_ref[...] = total_ref[...]

    running = [group_steps(g) for g in range(groups)] + [small_steps(), ig_steps()]
    ended = set()

    def advance(which):
        if which not in ended:
            try:
                next(running[which])
            except StopIteration:
                ended.add(which)

    for which in TAIL_ORDER:
        advance(which)
    while len(ended) < len(running):
        for which in range(len(running)):
            advance(which)


def tail(grads, ig, act_x, act_y, small, size):
    shards, _, depth = grads[0].shape
    rows_list = [g.shape[1] for g in grads]
    groups = len(grads)
    bits = plane_bits(size)
    any_spec = pl.BlockSpec(memory_space=pl.ANY)
    shape = jax.ShapeDtypeStruct

    def plane_rows(rows):
        half, total = rows // 2, 0
        for k in range(len(bits)):
            if k < halvings(rows // 2, bits):
                half //= 2
            total += half
        return total

    copies = 4 + 2 + 2 * len(bits) + 1
    return pl.pallas_call(
        lambda *refs: tail_kernel(size, rows_list, *refs),
        in_specs=[any_spec] * (groups + 3) + [whole()],
        out_specs=[any_spec] * (groups + 2) + [whole(), whole()],
        out_shape=[shape((rows, depth), BF) for rows in rows_list]
        + [shape((shards,) + ig.shape, BF), shape(ig.shape, BF), shape(small.shape, F32), shape(small.shape, F32)],
        scratch_shapes=[pltpu.VMEM((shards, rows // 2, depth), BF) for rows in rows_list]
        + [pltpu.VMEM((shards, rows // 2, depth), BF) for rows in rows_list]
        + [pltpu.VMEM((4, rows // 4, depth), BF) for rows in rows_list]
        + [pltpu.VMEM((2, rows // 4, depth), BF) for rows in rows_list]
        + [pltpu.VMEM((plane_rows(rows), depth), BF) for rows in rows_list]
        + [pltpu.VMEM((rows // 2, depth), BF) for rows in rows_list]
        + [
            pltpu.VMEM((3 + len(bits),) + small.shape, F32),
            pltpu.SemaphoreType.DMA((groups, copies)),
            pltpu.SemaphoreType.DMA((groups, copies)),
            pltpu.SemaphoreType.DMA((2 * groups + 1,)),
            pltpu.SemaphoreType.DMA((6,)),
            pltpu.SemaphoreType.DMA((6,)),
            pltpu.SemaphoreType.DMA((3 + len(bits),)),
            pltpu.SemaphoreType.DMA((3 + len(bits),)),
        ],
        compiler_params=pltpu.CompilerParams(
            vmem_limit_bytes=VMEM_LIMIT, collective_id=1, has_side_effects=True
        ),
        cost_estimate=pl.CostEstimate(flops=30_000_000, bytes_accessed=60_000_000, transcendentals=0),
        name="tail",
    )(*grads, ig, act_x, act_y, small)


def hop(value, axis, bit):
    size = lax.axis_size(axis)
    return lax.ppermute(value, axis, [(i, i ^ bit) for i in range(size)])


def after(value, *deps):
    return lax.optimization_barrier((value, deps))[0]


def near(value):
    return hop(value, "tp", 1), hop(value, "tp", 2)


def far(from_x, from_y):
    half = from_x.shape[0] // 2
    low = hop(from_x[:half], "tp", 2)
    high = hop(from_y[half:], "tp", 1)
    return jnp.concatenate([low, high])


def gather_tp_small(value):
    return jnp.stack([value, hop(value, "tp", 1), hop(value, "tp", 2), hop(value, "tp", 3)])


def take_half(value, which, axis=0):
    half = value.shape[axis] // 2
    return lax.dynamic_slice_in_dim(value, which * half, half, axis=axis)


def join_halves(value, other, which, axis=0):
    half = value.shape[axis]
    three = jnp.concatenate([value, other, value], axis=axis)
    return lax.dynamic_slice_in_dim(three, which * half, 2 * half, axis=axis)


def plus(a, b):
    return (a.astype(F32) + b.astype(F32)).astype(BF)


def core_sum(value):
    core = lax.axis_index("ep") % 2
    return plus(take_half(value, core, 1), hop(take_half(value, 1 - core, 1), "ep", 1))


def swap_ep(value):
    return lax.all_to_all(value, "ep", split_axis=0, concat_axis=0, tiled=True)


def route_kernel(order_ref, index_ref, hot_ref, out_ref, rank_ref):
    rows = order_ref.shape[1]
    tile = rows // 7
    half = hot_ref.shape[1] // 2
    for i in range(7):
        ids = lax.broadcasted_iota(jnp.int32, (tile, 1), 0) + tile * i
        match = jnp.where(order_ref[...] == ids, 1.0, 0.0).astype(BF)
        rank_ref[tile * i : tile * (i + 1), :] = dot(match, index_ref[...], NN)
    parts = rank_ref[...]
    rank = parts[:, 0:1] * 64.0 + parts[:, 1:2]
    rank_row = jnp.transpose(jnp.broadcast_to(rank, parts.shape))[0:1, :]
    hot = hot_ref[...]
    total = jnp.sum(hot.astype(F32), axis=0, keepdims=True)
    lanes = lax.broadcasted_iota(jnp.int32, (1, 2 * half), 1)
    firsts = jnp.where(lanes < half, total, 0.0)
    firsts = jnp.concatenate([jnp.zeros((1, half), F32), firsts[:, :half]], axis=1)
    for i in range(7):
        at = slice(tile * i, tile * (i + 1))
        earlier = jnp.where(rank_row < rank[at], 1.0, 0.0).astype(BF)
        count = dot(earlier, hot, NN) + firsts
        picked = count * hot[at].astype(F32)
        first = jnp.sum(jnp.where(lanes < half, picked, 0.0), axis=1, keepdims=True)
        second = jnp.sum(jnp.where(lanes < half, 0.0, picked), axis=1, keepdims=True)
        out_ref[at, :] = jnp.where(lanes == 0, first, second)


def route(picks, order):
    rows = picks.shape[0]
    half = 64
    ids = jnp.arange(half, dtype=jnp.int32)[None, :]
    hot = jnp.concatenate([picks[:, 0:1] == ids, picks[:, 1:2] == ids], axis=1).astype(BF)
    line = jnp.arange(rows, dtype=jnp.int32)[:, None]
    column = jnp.arange(2 * half, dtype=jnp.int32)[None, :]
    index = jnp.where(column == 0, line // 64, jnp.where(column == 1, line % 64, 0)).astype(BF)
    out = pl.pallas_call(
        route_kernel,
        in_specs=[whole(), whole(), whole()],
        out_specs=whole(),
        out_shape=jax.ShapeDtypeStruct((rows, 2 * half), F32),
        scratch_shapes=[pltpu.VMEM((rows, 2 * half), F32)],
        compiler_params=pltpu.CompilerParams(vmem_limit_bytes=VMEM_LIMIT),
        cost_estimate=pl.CostEstimate(
            flops=4 * rows * rows * 128, bytes_accessed=4_000_000, transcendentals=0
        ),
        name="route",
    )(order.reshape(1, rows), after(index, hot), hot)
    return out[:, :2].astype(jnp.int32)


def body(
    tokens,
    cotangent,
    picks,
    priority,
    router_noise,
    dense_norm_gain,
    dense_norm_bias,
    dense_attend_in,
    dense_attend_bias,
    dense_attend_out,
    dense_attend_out_bias,
    feed_norm_gain,
    feed_norm_bias,
    feed_in,
    feed_in_bias,
    feed_out,
    feed_out_bias,
    sparse_norm_gain,
    sparse_norm_bias,
    sparse_attend_in,
    sparse_attend_bias,
    sparse_attend_out,
    sparse_attend_out_bias,
    route_norm_gain,
    route_norm_bias,
    router,
    expert_in,
    expert_in_bias,
    expert_out,
    expert_out_bias,
):
    shards = lax.axis_size("tp")
    experts = lax.axis_size("ep")
    mine = lax.axis_index("tp")
    rows_dev, depth = tokens.shape
    own = rows_dev // shards
    images = own // LEN
    own_pad = images * PAD
    capacity = rows_dev // experts
    part = -(-capacity // (8 * shards)) * 8
    width = dense_attend_bias.shape[1]
    hidden = feed_in_bias.shape[0]

    def pad_images(value):
        blocks = value.reshape(-1, LEN, value.shape[-1])
        return jnp.pad(blocks, ((0, 0), (0, PAD - LEN), (0, 0))).reshape(-1, value.shape[-1])

    def drop_pad(value):
        return value.reshape(images, PAD, depth)[:, :LEN].reshape(own, depth)

    def own_rows(value):
        return lax.dynamic_slice_in_dim(value, mine * own, own, axis=0)

    def by_index(value):
        return jnp.stack(
            [
                lax.dynamic_index_in_dim(value, mine ^ r, axis=0, keepdims=False)
                for r in range(shards)
            ]
        )

    def row(value):
        return value.reshape(1, -1)

    def attend_pack(proj_in, proj_out):
        return jnp.concatenate([proj_in.transpose(1, 2, 0).reshape(3 * width, depth), proj_out])

    pair_side = lax.axis_index("ep") % 2
    chip_side = mine % 2
    same = pair_side == chip_side
    keep_exp = jnp.where(pair_side == 0, expert_in[0], expert_out[0])
    give_exp = jnp.where(pair_side == 0, expert_out[0], expert_in[0])
    vectors = jnp.stack(
        [
            dense_norm_gain,
            dense_norm_bias,
            dense_attend_out_bias,
            feed_norm_gain,
            feed_norm_bias,
            feed_out_bias,
            sparse_norm_gain,
            sparse_norm_bias,
            sparse_attend_out_bias,
            route_norm_gain,
            route_norm_bias,
        ]
    )
    vectors = jnp.pad(vectors, ((0, 5), (0, 0)))

    def bias_line(value):
        gap = jnp.zeros((width,), F32)
        return jnp.concatenate([value[0], gap, value[1], jnp.zeros((depth - 3 * width,), F32)])

    own_biases = jnp.stack(
        [
            bias_line(dense_attend_bias),
            bias_line(sparse_attend_bias),
            feed_in_bias,
            expert_in_bias[0],
            expert_out_bias[0],
        ]
    )
    own_biases = jnp.pad(own_biases, ((0, 3), (0, 0)))
    swapped = hop(give_exp, "ep", 1)
    home_exp = jnp.where(same, keep_exp, swapped)
    away_exp = jnp.where(same, swapped, keep_exp)
    level_zero = after(pad_images(own_rows(tokens)), home_exp, away_exp)
    (level_one, level_two, level_three), kept_one, kept_feed, kept_two, gathered, normed, biases = (
        dense_forward(
            level_zero,
            vectors,
            own_biases,
            attend_pack(dense_attend_in, dense_attend_out),
            jnp.concatenate([feed_in, feed_out]),
            attend_pack(sparse_attend_in, sparse_attend_out),
        )
    )
    w_one, w_feed, w_two = gathered
    level_zero = level_zero.astype(F32)
    exp_small = biases[:, 3:5]
    exp_small = jnp.where(same, exp_small, hop(exp_small, "ep", 1))
    b_exp = exp_small[:, 0:1]
    b_exp_out = exp_small[0, 1:2]

    home_exp = after(home_exp, normed)
    away_exp = after(away_exp, normed)
    exp_x = hop(away_exp, "tp", 1)
    exp_far = hop(away_exp, "tp", 3)
    exp_y = hop(home_exp, "tp", 2)
    other_home = hop(home_exp, "ep", 1)

    position = route(after(picks, normed), priority[0])
    targets = jnp.where(position < capacity, picks * (part * shards) + position, -1).T
    slots = jnp.arange(experts * part, dtype=jnp.int32)

    def slots_of(index):
        block, inside = slots // part, slots % part
        expert = 2 * (block // 2) + index % 2
        quarter = 2 * (index // 2) + block % 2
        return expert * (part * shards) + quarter * part + inside

    slot_ids = slots_of(mine)
    pad_targets = jnp.pad(
        targets.reshape(2, -1, LEN), ((0, 0), (0, 0), (0, PAD - LEN)), constant_values=-1
    ).reshape(2, -1)
    near_targets = jnp.concatenate(
        [
            lax.dynamic_slice_in_dim(pad_targets, (mine ^ r) * own_pad, own_pad, axis=1)
            for r in range(shards)
        ],
        axis=1,
    )
    noise_pad = pad_images(router_noise)
    all_slots = jnp.concatenate([slots_of(mine ^ r) for r in range(shards)])
    own_targets = near_targets[:, :own_pad].T
    back_hot = (own_targets[:, 0:1] == all_slots[None, :]) | (
        own_targets[:, 1:2] == all_slots[None, :]
    )
    back_hot_bf = back_hot.astype(BF)

    all_normed = normed.reshape(shards * own_pad, depth)
    route_normed = normed[0]
    noise = jnp.concatenate(
        [
            lax.dynamic_slice_in_dim(noise_pad, (mine ^ r) * own_pad, own_pad, axis=0)
            for r in range(shards)
        ]
    )
    logits = dot(all_normed, router, NN) + noise
    gates = jax.nn.softmax(logits, axis=-1)
    own_hot = (slot_ids[:, None] == near_targets[0][None, :]) | (
        slot_ids[:, None] == near_targets[1][None, :]
    )
    side_gates = lax.dynamic_index_in_dim(
        gates.T.reshape(experts // 2, 2, -1), chip_side, axis=1, keepdims=False
    )
    hot_gates = own_hot.reshape(experts // 2, 2 * part, -1).astype(F32) * side_gates[:, None, :]
    slot_gate = jnp.sum(hot_gates, axis=2).reshape(-1, 1)

    def two_parts(value):
        high = lax.reduce_precision(value, 8, 7)
        rest = jnp.zeros((value.shape[0], 126), BF)
        return jnp.concatenate([high.astype(BF), (value - high).astype(BF), rest], axis=1)

    def swap_rows(value):
        wide = value.shape[-1]
        return swap_ep(value.reshape(experts, part, wide)).reshape(experts * part, wide)

    rows = dot(own_hot.astype(BF), all_normed, NN).astype(BF)
    arrived = swap_rows(jnp.concatenate([rows, two_parts(slot_gate)], axis=1))
    cot_hot = (slot_ids[:, None] == targets[0][None, :]) | (slot_ids[:, None] == targets[1][None, :])
    cot_sent = dot(after(cot_hot.astype(BF), rows), cotangent, NN).astype(BF)
    cot_rows = swap_rows(cot_sent)
    exp_x, exp_y, exp_far = after((exp_x, exp_y, exp_far), cot_sent)
    exp_mine = jnp.stack([home_exp, exp_x, exp_y, exp_far])
    exp_other = jnp.stack(
        [other_home, hop(exp_x, "ep", 1), hop(exp_y, "ep", 1), hop(exp_far, "ep", 1)]
    )
    inputs = arrived[:, :depth]
    gate_in = arrived[:, depth : depth + 2].astype(F32)
    gate_in = gate_in[:, 0:1] + gate_in[:, 1:2]
    outputs, exp_hidden, exp_slope = expert_forward(inputs, exp_mine, exp_other, b_exp, b_exp_out)
    weighted, grad_outputs, grad_inputs, slot_dot, exp_du, small_exp = (
        expert_input(outputs, cot_rows, gate_in, exp_mine, exp_other, exp_slope)
    )
    sent = jnp.concatenate([grad_inputs, two_parts(slot_dot)], axis=1)
    part_exp, grad_slots, weighted = expert_return(
        inputs,
        grad_outputs,
        exp_hidden,
        exp_du,
        sent.reshape(experts, part, sent.shape[1]),
        weighted.reshape(experts, part, depth),
    )
    weighted = weighted.reshape(experts * part, depth)
    grad_slots = grad_slots.reshape(shards * experts * part, sent.shape[1])
    exp_from_y = hop(part_exp[3], "tp", 2)
    dot_slots = grad_slots[:, depth : depth + 2].astype(F32)
    dot_slots = dot_slots[:, 0] + dot_slots[:, 1]
    grad_slots = grad_slots[:, :depth]

    grad_stream = pad_images(own_rows(after(cotangent, cot_sent))).astype(F32)
    own_gates = gates[:own_pad]
    hot_dots = jnp.where(back_hot, dot_slots[None, :], 0.0).reshape(
        own_pad, 2, 2, experts // 2, 2 * part
    )
    by_side = jnp.sum(hot_dots, axis=(1, 4))
    by_side = jnp.where(chip_side == 0, by_side, by_side[:, ::-1])
    grad_gates = by_side.transpose(0, 2, 1).reshape(own_pad, experts)
    grad_logits = own_gates * (grad_gates - jnp.sum(own_gates * grad_gates, axis=1, keepdims=True))
    grad_logits = grad_logits.astype(BF)
    g_router = dot(grad_logits, route_normed, TN)
    grad_normed = dot(grad_logits, router, NT) + dot(back_hot_bf, grad_slots, NN)
    hat, scale = norm_parts(level_three)
    g_route_gain = jnp.sum(grad_normed * hat, axis=0)
    g_route_bias = jnp.sum(grad_normed, axis=0)
    grad_stream = grad_stream + norm_back(hat, scale, route_norm_gain, grad_normed)

    grad_stream, exp_from_y = lax.optimization_barrier((grad_stream, exp_from_y))
    near_weighted = near(after(weighted, grad_stream))
    grad_stream, g_two, small_two = attend_backward(
        grad_stream, level_two, row(sparse_norm_gain), row(sparse_norm_bias), w_two, kept_two
    )
    near_weighted = after(near_weighted, g_two)
    far_weighted = far(*near_weighted)
    exp_from_y2 = hop(after(part_exp[2], g_two), "tp", 2)
    exp_give = plus(part_exp[1], exp_from_y)
    exp_away = hop(after(exp_give, g_two), "tp", 1)
    grad_stream, g_feed, small_feed = feed_backward(
        grad_stream, level_one, row(feed_norm_gain), row(feed_norm_bias), w_feed, kept_feed
    )
    far_weighted, exp_from_y2, exp_away = lax.optimization_barrier(
        ((far_weighted, exp_from_y2, exp_away), g_feed)
    )[0]
    exp_keep = plus(part_exp[0], exp_from_y2)
    keep_sum = jnp.where(same, exp_keep, exp_away)
    other_sum = hop(jnp.where(same, exp_away, exp_keep), "ep", 1)
    weighted_slots = jnp.concatenate([weighted, *near_weighted, far_weighted])
    level_four = level_three + dot(back_hot_bf, weighted_slots, NN)
    own_final = drop_pad(level_four.astype(BF))
    near_final = near(own_final)
    grad_stream = after(grad_stream, own_final)
    grad_stream, g_one, small_one = attend_backward(
        grad_stream, level_zero, row(dense_norm_gain), row(dense_norm_bias), w_one, kept_one
    )
    near_final = after(near_final, g_one)

    blank = jnp.zeros_like(small_exp)
    first = chip_side == 0
    small = jnp.concatenate(
        [
            small_one,
            small_feed,
            small_two,
            jnp.where(first, small_exp, blank),
            jnp.where(first, blank, small_exp),
            g_router,
            jnp.pad(jnp.stack([g_route_gain, g_route_bias]), ((0, 6), (0, 0))),
        ]
    )
    t_two, t_feed, t_one, ig_all, far_final, total, pair_total = tail(
        [g_two, g_feed, g_one], drop_pad(grad_stream.astype(BF)), *near_final, small, experts
    )
    input_grad = ig_all.reshape(rows_dev, depth).astype(F32)
    other_sum = after(other_sum, t_one)

    def absolute(blocks, kind):
        out = jnp.zeros((rows_dev, depth), kind)
        for r in range(shards):
            out = lax.dynamic_update_slice_in_dim(
                out, blocks[r].astype(kind), (mine ^ r) * own, axis=0
            )
        return out

    final = absolute([own_final, *near_final, far_final], BF)

    def attend_split(value):
        value = value.astype(F32)
        return (
            value[: 3 * width].reshape(3, width, depth).transpose(2, 0, 1),
            value[3 * width :],
        )

    t_exp_in = jnp.where(pair_side == 0, keep_sum, other_sum).astype(F32)
    t_exp_out = jnp.where(pair_side == 0, other_sum, keep_sum).astype(F32)
    t_in_two, t_out_two = attend_split(t_two)
    t_in_one, t_out_one = attend_split(t_one)
    t_feed = t_feed.astype(F32)

    def own_line(value, start):
        return lax.dynamic_slice_in_dim(value, start + mine, 1, axis=0)[0]

    def two_biases(start):
        line = own_line(total, start)
        return jnp.stack([line[:width], line[2 * width : 3 * width]])

    s_one, s_feed, s_two = total[0:8], total[8:16], total[16:24]
    s_exp = lax.dynamic_slice_in_dim(pair_total, 24 + 8 * pair_side, 8, axis=0)
    s_router = total[40 : 40 + experts].T
    s_route = total[40 + experts :]
    return (
        final,
        input_grad,
        s_one[0],
        s_one[1],
        t_in_one,
        two_biases(3),
        t_out_one,
        s_one[2],
        s_feed[0],
        s_feed[1],
        t_feed[:depth],
        own_line(total, 11),
        t_feed[depth:],
        s_feed[2],
        s_two[0],
        s_two[1],
        t_in_two,
        two_biases(19),
        t_out_two,
        s_two[2],
        s_route[0],
        s_route[1],
        s_router,
        t_exp_in[None],
        own_line(s_exp, 0)[None],
        t_exp_out[None],
        s_exp[4][None],
    )


def solution(mesh):
    in_specs = (
        P("ep", None),
        P("ep", None),
        P("ep", None),
        P("ep", None),
        P("ep", None),
        P(),
        P(),
        P(None, None, "tp"),
        P(None, "tp"),
        P("tp", None),
        P(),
        P(),
        P(),
        P(None, "tp"),
        P("tp"),
        P("tp", None),
        P(),
        P(),
        P(),
        P(None, None, "tp"),
        P(None, "tp"),
        P("tp", None),
        P(),
        P(),
        P(),
        P(),
        P("ep", None, "tp"),
        P("ep", "tp"),
        P("ep", "tp", None),
        P("ep", None),
    )
    out_specs = (
        P("ep", None),
        P("ep", None),
        P(),
        P(),
        P(None, None, "tp"),
        P(None, "tp"),
        P("tp", None),
        P(),
        P(),
        P(),
        P(None, "tp"),
        P("tp"),
        P("tp", None),
        P(),
        P(),
        P(),
        P(None, None, "tp"),
        P(None, "tp"),
        P("tp", None),
        P(),
        P(),
        P(),
        P(),
        P("ep", None, "tp"),
        P("ep", "tp"),
        P("ep", "tp", None),
        P("ep", None),
    )
    return jax.shard_map(body, mesh=mesh, in_specs=in_specs, out_specs=out_specs, check_vma=False)
```
